32 devices in a mesh: dp: 32 (over z, y, x, core).
Axes of the slice: x: 2, y: 2, z: 4, core: 2. Of those that a mesh axis runs over, the one named last changes fastest.
Arguments:
- patches: bfloat16 [2, 64, 2, 225, 768], P(None, 'dp'), may hold values from -6 to 6
- visible: int32 [2, 64, 128], P(None, 'dp'), may hold values from 0 to 224, as said below
- valid_mask: int32 [2, 64, 128], P(None, 'dp'), may hold values from 0 to 1, as said below
- norm1_gain: float32 [2, 768], replicated, may hold values from 0.25 to 1.75
- norm1_shift: float32 [2, 768], replicated, may hold values from -1.75 to 1.75
- qkv_weight: bfloat16 [2, 768, 2304], replicated, may hold values from -0.21875 to 0.21875
- out_weight: bfloat16 [2, 768, 768], replicated, may hold values from -1.75 to 1.75
- norm2_gain: float32 [2, 768], replicated, may hold values from 0.25 to 1.75
- norm2_shift: float32 [2, 768], replicated, may hold values from -1.75 to 1.75
- up_weight: bfloat16 [2, 768, 3072], replicated, may hold values from -0.21875 to 0.21875
- up_bias: float32 [2, 3072], replicated, may hold values from -1.75 to 1.75
- down_weight: bfloat16 [2, 3072, 768], replicated, may hold values from -0.109375 to 0.109375
Outputs:
- contrast_loss: float32 [], replicated
- patches_grad: float32 [2, 64, 2, 225, 768], P(None, 'dp')
- grad_norm1_gain: float32 [1536], P('dp')
- grad_norm1_shift: float32 [1536], P('dp')
- grad_qkv_weight: float32 [1536, 2304], P('dp')
- grad_out_weight: float32 [1536, 768], P('dp')
- grad_norm2_gain: float32 [1536], P('dp')
- grad_norm2_shift: float32 [1536], P('dp')
- grad_up_weight: float32 [1536, 3072], P('dp')
- grad_up_bias: float32 [6144], P('dp')
- grad_down_weight: float32 [6144, 768], P('dp')
The draws below stay inside these ranges and needn't reach their ends.
Inputs may be any that keep to these rules, and one draw needn't show every extreme that they name: `visible`: the 128 entries of an image are distinct patch numbers of its 15 x 15 grid, row-major. `valid_mask`: in each image the ones come first; each image has 32 to 128 ones, and every micro-batch has an image with exactly 32 and one with exactly 128.
All inputs are finite; a program needn't handle non-finite values.
Results may differ from the reference program's by a relative error of at most 0.0082.
Values sent between devices are 32-bit elements; how exact they have to be, the bound alone decides.
A program may use at most 256 MiB of HBM per device.

```python
import math
import jax
import jax.numpy as jnp
from jax import lax

D = 768
HEADS = 12
HEAD_DIM = 64
FF = 3072
GRID = 15
SLOTS = 128
LEAST = 32
MICRO = 2
PATCHES = 225
BATCH = 64


def draw_visible(key, part):
    key = jax.random.fold_in(key, 11)
    row_keys = jax.random.split(key, MICRO * BATCH)
    orders = jax.vmap(lambda single_key: jax.random.permutation(single_key, PATCHES))(row_keys)
    return orders[:, :SLOTS].reshape(MICRO, BATCH, SLOTS).astype(jnp.int32)


def draw_valid_mask(key, part):
    key = jax.random.fold_in(key, 23)
    key_count, key_full, key_offset = jax.random.split(key, 3)
    counts = jax.random.randint(key_count, (MICRO, BATCH), LEAST, SLOTS + 1)
    fullest = jax.random.randint(key_full, (MICRO,), 0, BATCH)
    offset = jax.random.randint(key_offset, (MICRO,), 1, BATCH)
    emptiest = (fullest + offset) % BATCH
    rows_index = jnp.arange(MICRO)
    counts = counts.at[rows_index, fullest].set(SLOTS)
    counts = counts.at[rows_index, emptiest].set(LEAST)
    slots_index = jnp.arange(SLOTS)
    return (slots_index[None, None, :] < counts[:, :, None]).astype(jnp.int32)


def block_scale(rng, dims, cuts, smallest, high):
    loudness = 1.0
    for axis_at, parts in cuts:
        steps = jax.random.uniform(jax.random.fold_in(jax.random.fold_in(rng, 6), axis_at), (parts,), jnp.float32, smallest / len(cuts), high / len(cuts))
        loudness = loudness * jnp.repeat(jnp.exp(steps), dims[axis_at] // parts).reshape((-1,) + (1,) * (len(dims) - 1 - axis_at))
    return loudness


def scatter_about(stream_key, shape, width, limit, cuts=(), kind=jnp.bfloat16):
    loudness = block_scale(stream_key, shape, cuts, -0.22, 0.18) if cuts else 1.0
    drawn = jax.random.normal(stream_key, shape, jnp.float32) * width * loudness
    return jnp.minimum(jnp.maximum(drawn, -limit), limit).astype(kind)


def setup_inputs(seed: int = 0) -> dict:
    seeds = jax.random.split(jax.random.key(seed), 13)
    return {
        "patches": scatter_about(seeds[0], (MICRO, BATCH, 2, PATCHES, D), 1.0, 6.0, ((1, 32),)),
        "visible": draw_visible(jax.random.fold_in(seeds[12], 71), 0),
        "valid_mask": draw_valid_mask(jax.random.fold_in(seeds[12], 71), 0),
        "norm1_gain": jnp.clip(1.0 + 0.15 * jax.random.normal(seeds[3], (2, D), jnp.float32), 0.25, 1.75),
        "norm1_shift": scatter_about(seeds[4], (2, D), 0.3, 1.75, (), jnp.float32),
        "qkv_weight": scatter_about(seeds[5], (2, D, 3 * D), D ** -0.5, 0.21875),
        "out_weight": scatter_about(seeds[6], (2, D, D), (D // 64) ** -0.5, 1.75),
        "norm2_gain": jnp.clip(1.0 + 0.15 * jax.random.normal(seeds[7], (2, D), jnp.float32), 0.25, 1.75),
        "norm2_shift": scatter_about(seeds[8], (2, D), 0.3, 1.75, (), jnp.float32),
        "up_weight": scatter_about(seeds[9], (2, D, FF), D ** -0.5, 0.21875),
        "up_bias": scatter_about(seeds[10], (2, FF), 0.3, 1.75, (), jnp.float32),
        "down_weight": scatter_about(seeds[11], (2, FF, D), FF ** -0.5, 0.109375),
    }


@jax.custom_vjp
def low(v):
    return lax.optimization_barrier(v.astype(jnp.bfloat16)).astype(jnp.float32)

@jax.custom_vjp
def low_back(v):
    return v

def low_keep(v):
    return (low(v), None)

def low_pass(kept, grad):
    return (grad,)

def back_keep(v):
    return (v, None)

def back_low(kept, grad):
    return (low(grad),)
low.defvjp(low_keep, low_pass)
low_back.defvjp(back_keep, back_low)
norm_epsilon = 1e-06
unit_epsilon = 1e-06
logit_scale = 100.0
masked_score = -1e+30
highest = lax.Precision.HIGHEST

def layer_norm(values_in, gain_vec, shift_vec):
    centre = values_in - lax.optimization_barrier(jnp.mean(values_in, axis=-1, keepdims=True))
    normed = centre * lax.rsqrt(lax.optimization_barrier(jnp.mean(centre * centre, axis=-1, keepdims=True)) + norm_epsilon)
    return normed * gain_vec + shift_vec

def alibi_bias(visible_rows):
    rows_pos = (visible_rows // GRID).astype(jnp.float32)
    cols_pos = (visible_rows % GRID).astype(jnp.float32)
    rows_gap = rows_pos[:, :, None] - rows_pos[:, None, :]
    cols_gap = cols_pos[:, :, None] - cols_pos[:, None, :]
    distance = jnp.sqrt(rows_gap * rows_gap + cols_gap * cols_gap)
    slopes = jnp.exp2(-8.0 * (jnp.arange(HEADS, dtype=jnp.float32) + 1.0) / HEADS)
    return -slopes[None, :, None, None] * distance[:, None, :, :]

def encode_block(tokens_in, visible_rows, mask_rows, params):
    gain_one, shift_one, w_qkv, w_out, gain_two, shift_two, w_up, b_up, w_down = params
    group_count, slot_count, model_width = tokens_in.shape
    head_scale = 1.0 / math.sqrt(HEAD_DIM)
    hidden_one = low(layer_norm(tokens_in, gain_one, shift_one))
    packed = low_back(low(jnp.einsum('gsd,de->gse', hidden_one, w_qkv, precision=highest)))
    shaped = packed.reshape(group_count, slot_count, 3, HEADS, HEAD_DIM)
    queries = shaped[:, :, 0]
    key_rows = shaped[:, :, 1]
    value_rows = shaped[:, :, 2]
    scores = jnp.einsum('gqhd,gkhd->ghqk', queries, key_rows, precision=highest) * head_scale + alibi_bias(visible_rows)
    scores = low_back(scores)
    key_ok = (mask_rows > 0)[:, None, None, :]
    scores = jnp.where(key_ok, scores, masked_score)
    row_max = lax.optimization_barrier(jnp.max(scores, axis=-1, keepdims=True))
    exponent = jnp.exp(scores - row_max)
    attention = exponent / lax.optimization_barrier(jnp.sum(exponent, axis=-1, keepdims=True))
    attended = jnp.einsum('ghqk,gkhd->gqhd', low(attention), value_rows, precision=highest)
    attended = low_back(low(attended.reshape(group_count, slot_count, model_width)))
    mixed_rows = tokens_in + low_back(jnp.einsum('gsd,de->gse', attended, w_out, precision=highest))
    hidden_two = low(layer_norm(mixed_rows, gain_two, shift_two))
    upper_pre = low_back(jnp.einsum('gsd,df->gsf', hidden_two, w_up, precision=highest) + b_up)
    active = low(jax.nn.gelu(upper_pre, approximate=False))
    output_rows = mixed_rows + low_back(jnp.einsum('gsf,fd->gsd', active, w_down, precision=highest))
    weight_mask = mask_rows.astype(jnp.float32)
    pooled = lax.optimization_barrier(jnp.sum(output_rows * weight_mask[:, :, None], axis=1)) / lax.optimization_barrier(jnp.sum(weight_mask, axis=1))[:, None]
    return pooled * lax.rsqrt(lax.optimization_barrier(jnp.sum(pooled * pooled, axis=-1, keepdims=True)) + unit_epsilon)

def contrast(unit_optical, unit_radar):
    logits = logit_scale * jnp.dot(unit_optical, unit_radar.T, precision=highest)
    diagonal = jnp.diagonal(logits)
    rows_part = jnp.sum(jax.nn.logsumexp(logits, axis=1) - diagonal)
    cols_part = jnp.sum(jax.nn.logsumexp(logits, axis=0) - diagonal)
    return rows_part + cols_part

def forward(patch_values, gain_one, shift_one, w_qkv, w_out, gain_two, shift_two, w_up, b_up, w_down, visible, valid_mask):
    group_size = math.gcd(BATCH, 32)
    group_count = BATCH // group_size
    total_loss = jnp.zeros((), jnp.float32)
    for micro_index in range(MICRO):
        unit_list = []
        for modality in range(2):
            params = (gain_one[modality], shift_one[modality], w_qkv[modality], w_out[modality], gain_two[modality], shift_two[modality], w_up[modality], b_up[modality], w_down[modality])
            gathered = jnp.take_along_axis(patch_values[micro_index, :, modality], visible[micro_index][:, :, None], axis=1)

            def encode_group(pieces, params=params):
                return encode_block(pieces[0], pieces[1], pieces[2], params)
            unit_rows = lax.map(jax.checkpoint(encode_group), (gathered.reshape(group_count, group_size, SLOTS, D), visible[micro_index].reshape(group_count, group_size, SLOTS), valid_mask[micro_index].reshape(group_count, group_size, SLOTS)))
            unit_list.append(unit_rows.reshape(BATCH, D))
        total_loss = total_loss + contrast(unit_list[0], unit_list[1])
    return total_loss / (2 * BATCH * MICRO)

def flatten_pair(grad_value):
    return grad_value.reshape((grad_value.shape[0] * grad_value.shape[1],) + grad_value.shape[2:])

def reference(patches, visible, valid_mask, norm1_gain, norm1_shift, qkv_weight, out_weight, norm2_gain, norm2_shift, up_weight, up_bias, down_weight):

    def objective(patch_values, gain_one, shift_one, w_qkv, w_out, gain_two, shift_two, w_up, b_up, w_down):
        return forward(patch_values, gain_one, shift_one, w_qkv, w_out, gain_two, shift_two, w_up, b_up, w_down, visible, valid_mask)
    loss_value, pull_back = jax.vjp(objective, patches.astype(jnp.float32), norm1_gain, norm1_shift, qkv_weight.astype(jnp.float32), out_weight.astype(jnp.float32), norm2_gain, norm2_shift, up_weight.astype(jnp.float32), up_bias, down_weight.astype(jnp.float32))
    grad_list = pull_back(jnp.ones_like(loss_value))
    flat = [flatten_pair(grad_list[number]) for number in range(1, 10)]
    return (loss_value, grad_list[0], flat[0], flat[1], flat[2], flat[3], flat[4], flat[5], flat[6], flat[7], flat[8])
```

```python
import functools
import math

import jax
import jax.numpy as jnp
from jax import lax
from jax.experimental import pallas as pl
from jax.experimental.pallas import tpu as pltpu
from jax.sharding import PartitionSpec as P

HEADS = 12
HEAD_DIM = 64
GRID = 15
MESH = pl.DeviceIdType.MESH

norm_epsilon = 1e-06
unit_epsilon = 1e-06
logit_scale = 100.0
masked_score = -1e30
highest = lax.Precision.HIGHEST
head_scale = 1.0 / math.sqrt(HEAD_DIM)
f32 = jnp.float32
bf16 = jnp.bfloat16


def exact_gelu(values_in):
    return jax.nn.gelu(values_in, approximate=False)


def layer_norm(values_in, gain_vec, shift_vec):
    centre = values_in - jnp.mean(values_in, axis=-1, keepdims=True)
    inverse = lax.rsqrt(jnp.mean(centre * centre, axis=-1, keepdims=True) + norm_epsilon)
    normed = centre * inverse
    return (normed * gain_vec + shift_vec, normed, inverse)


def norm_back(grad_out, normed, inverse, gain_vec):
    grad_normed = grad_out * gain_vec
    mean_plain = jnp.mean(grad_normed, axis=-1, keepdims=True)
    mean_normed = jnp.mean(grad_normed * normed, axis=-1, keepdims=True)
    grad_in = inverse * (grad_normed - mean_plain - normed * mean_normed)
    return (grad_in, jnp.sum(grad_out * normed, axis=0), jnp.sum(grad_out, axis=0))


def alibi_bias(visible_rows):
    rows_pos = (visible_rows // GRID).astype(f32)
    cols_pos = (visible_rows % GRID).astype(f32)
    rows_gap = rows_pos[:, :, None] - rows_pos[:, None, :]
    cols_gap = cols_pos[:, :, None] - cols_pos[:, None, :]
    distance = jnp.sqrt(rows_gap * rows_gap + cols_gap * cols_gap)
    slopes = jnp.exp2(-8.0 * (jnp.arange(HEADS, dtype=f32) + 1.0) / HEADS)
    return -slopes[None, :, None, None] * distance[:, None, :, :]


def split_heads(packed):
    images, slot_count, _ = packed.shape
    shaped = packed.reshape(images, slot_count, 3, HEADS, HEAD_DIM)
    return (shaped[:, :, 0], shaped[:, :, 1], shaped[:, :, 2])


def encode_forward(tokens_in, visible_rows, mask_rows, params):
    gain_one, shift_one, w_qkv, w_out, gain_two, shift_two, w_up, b_up, w_down = params
    images, slots, width = tokens_in.shape
    flat_in = tokens_in.reshape(images * slots, width)
    hidden_one, normed_one, inverse_one = layer_norm(flat_in, gain_one, shift_one)
    hidden_one = hidden_one.astype(bf16)
    packed = jnp.dot(hidden_one, w_qkv, preferred_element_type=f32).astype(bf16)
    packed = packed.reshape(images, slots, 3 * width)
    queries, keys, values = split_heads(packed)
    scores = jnp.einsum("iqhd,ikhd->ihqk", queries, keys, preferred_element_type=f32)
    scores = scores * head_scale + alibi_bias(visible_rows)
    scores = jnp.where((mask_rows > 0)[:, None, None, :], scores, masked_score)
    attention = jax.nn.softmax(scores, axis=-1)
    attended = jnp.einsum("ihqk,ikhd->iqhd", attention.astype(bf16), values, preferred_element_type=f32)
    attended = attended.reshape(images * slots, width).astype(bf16)
    mixed = flat_in + jnp.dot(attended, w_out, preferred_element_type=f32)
    hidden_two, normed_two, inverse_two = layer_norm(mixed, gain_two, shift_two)
    hidden_two = hidden_two.astype(bf16)
    upper = jnp.dot(hidden_two, w_up, preferred_element_type=f32) + b_up
    active, gelu_back = jax.vjp(exact_gelu, upper)
    active = active.astype(bf16).astype(f32)
    weight = mask_rows.astype(f32)
    active_sum = jnp.sum(active.reshape(images, slots, -1) * weight[:, :, None], axis=1)
    mixed_sum = jnp.sum(mixed.reshape(images, slots, width) * weight[:, :, None], axis=1)
    saved = (normed_one, inverse_one, hidden_one, packed, attention, attended, normed_two, inverse_two, hidden_two, gelu_back)
    return active_sum, mixed_sum, saved


def pool(active_sum, mixed_sum, mask_rows, w_down):
    counted = jnp.sum(mask_rows.astype(f32), axis=1)[:, None]
    down = jnp.dot(active_sum, w_down.astype(f32), precision=highest)
    return (mixed_sum + down) / counted


def encode_backward(grad_pooled, saved, mask_rows, params):
    normed_one, inverse_one, hidden_one, packed, attention, attended, normed_two, inverse_two, hidden_two, gelu_back = saved
    gain_one, shift_one, w_qkv, w_out, gain_two, shift_two, w_up, b_up, w_down = params
    images, slots, three_width = packed.shape
    width = three_width // 3
    rows = images * slots
    weight = mask_rows.astype(f32)
    counted = jnp.sum(weight, axis=1)[:, None]
    grad_row = grad_pooled / counted
    grad_output = (weight[:, :, None] * grad_row[:, None, :]).reshape(rows, width)
    grad_active = jnp.dot(grad_row.astype(bf16), w_down.T, preferred_element_type=f32)
    grad_active = (weight[:, :, None] * grad_active[:, None, :]).reshape(rows, -1)
    grad_upper = gelu_back(grad_active)[0].astype(bf16)
    grad_bias = jnp.sum(grad_upper.astype(f32), axis=0)
    grad_up = jnp.dot(hidden_two.T, grad_upper, preferred_element_type=f32)
    grad_hidden_two = jnp.dot(grad_upper, w_up.T, preferred_element_type=f32)
    grad_norm_two, grad_gain_two, grad_shift_two = norm_back(grad_hidden_two, normed_two, inverse_two, gain_two)
    grad_mixed = grad_output + grad_norm_two
    grad_mixed_low = grad_mixed.astype(bf16)
    grad_out = jnp.dot(attended.T, grad_mixed_low, preferred_element_type=f32)
    grad_attended = jnp.dot(grad_mixed_low, w_out.T, preferred_element_type=f32).astype(bf16)
    grad_attended = grad_attended.reshape(images, slots, HEADS, HEAD_DIM)
    queries, keys, values = split_heads(packed)
    grad_value = jnp.einsum("ihqk,iqhd->ikhd", attention.astype(bf16), grad_attended, preferred_element_type=f32)
    grad_attention = jnp.einsum("iqhd,ikhd->ihqk", grad_attended, values, preferred_element_type=f32)
    grad_scores = attention * (grad_attention - jnp.sum(attention * grad_attention, axis=-1, keepdims=True))
    grad_scores = grad_scores.astype(bf16)
    grad_query = jnp.einsum("ihqk,ikhd->iqhd", grad_scores, keys, preferred_element_type=f32) * head_scale
    grad_key = jnp.einsum("ihqk,iqhd->ikhd", grad_scores, queries, preferred_element_type=f32) * head_scale
    grad_packed = jnp.stack([grad_query, grad_key, grad_value], axis=2).astype(bf16).reshape(rows, three_width)
    grad_qkv = jnp.dot(hidden_one.T, grad_packed, preferred_element_type=f32)
    grad_hidden_one = jnp.dot(grad_packed, w_qkv.T, preferred_element_type=f32)
    grad_norm_one, grad_gain_one, grad_shift_one = norm_back(grad_hidden_one, normed_one, inverse_one, gain_one)
    grad_tokens = (grad_mixed + grad_norm_one).reshape(images, slots, width)
    return grad_tokens, (grad_gain_one, grad_shift_one, grad_qkv, grad_out, grad_gain_two, grad_shift_two, grad_up, grad_bias)


def contrast(pooled, own_rows, micro_count):
    count = pooled.shape[0]
    images = own_rows // (2 * micro_count)
    inverse = lax.rsqrt(jnp.sum(pooled * pooled, axis=-1, keepdims=True) + unit_epsilon)
    unit = pooled * inverse
    logits = logit_scale * lax.dot_general(unit, unit, (((1,), (1,)), ((), ())), precision=highest, preferred_element_type=f32)
    row = lax.broadcasted_iota(jnp.int32, (count, count), 0)
    col = lax.broadcasted_iota(jnp.int32, (count, count), 1)
    half = own_rows // 2
    row_mod, col_mod = (row // half) % 2, (col // half) % 2
    row_micro, col_micro = (row // images) % micro_count, (col // images) % micro_count
    allowed = (row_mod != col_mod) & (row_micro == col_micro)
    paired = jnp.where(col == row + half * (1 - 2 * row_mod), 1.0, 0.0)
    logits = jnp.where(allowed, logits, masked_score)
    row_max = jnp.max(logits, axis=1, keepdims=True)
    row_lse = row_max + jnp.log(jnp.sum(jnp.exp(logits - row_max), axis=1, keepdims=True))
    col_max = jnp.max(logits, axis=0, keepdims=True)
    col_lse = col_max + jnp.log(jnp.sum(jnp.exp(logits - col_max), axis=0, keepdims=True))
    scale = 1.0 / count
    diagonal = jnp.sum(jnp.where(paired > 0, logits, 0.0), axis=1, keepdims=True)
    loss = scale * jnp.sum(row_lse - diagonal, axis=0, keepdims=True)
    spread = jnp.exp(logits - row_lse) + jnp.exp(logits - col_lse) - 2.0 * paired
    grad_unit = (logit_scale * scale) * jnp.dot(spread, unit, precision=highest, preferred_element_type=f32)
    grad_pooled = inverse * (grad_unit - unit * jnp.sum(unit * grad_unit, axis=-1, keepdims=True))
    return loss, grad_pooled


def meet(peers):
    barrier = pltpu.get_barrier_semaphore()
    for peer in peers:
        pl.semaphore_signal(barrier, inc=1, device_id=(peer,), device_id_type=MESH)
    pl.semaphore_wait(barrier, len(peers))


def gather_kernel(n, micro_count, pooled_ref, sums_ref, loss_ref, grad_ref, got_ref, every, send_sem, recv_sem, sum_send, sum_recv, local_sem):
    me = lax.axis_index("dp")
    rows = pooled_ref.shape[0]
    barrier = pltpu.get_barrier_semaphore()

    def greet(step, carry):
        pl.semaphore_signal(barrier, inc=1, device_id=(lax.rem(me + step, n),), device_id_type=MESH)
        return carry

    lax.fori_loop(1, n, greet, 0)
    pl.semaphore_wait(barrier, n - 1)
    every[me] = pooled_ref[...]
    slot = 0

    def copies(sources, flip, first):
        made = []
        for number, source in enumerate(sources):
            made.append(
                pltpu.make_async_remote_copy(
                    src_ref=every.at[source],
                    dst_ref=every.at[source],
                    send_sem=send_sem.at[first + number],
                    recv_sem=recv_sem.at[first + number],
                    device_id=(me ^ flip,),
                    device_id_type=MESH,
                )
            )
        for copy in made:
            copy.start()
        return made

    def finish(made):
        for copy in made:
            copy.wait()

    held = [me]
    waves = []
    for number, flip in enumerate((8, 16, 24)):
        waves += copies([me], flip, number)
    def sums_out(step, carry):
        peer = lax.rem(me + step, n)
        pltpu.make_async_remote_copy(
            src_ref=sums_ref.at[peer], dst_ref=got_ref.at[me], send_sem=sum_send.at[step], recv_sem=sum_recv.at[step],
            device_id=(peer,), device_id_type=MESH).start()
        return carry

    own = pltpu.make_async_copy(sums_ref.at[me], got_ref.at[me], local_sem)
    own.start()
    finish(waves)
    held = [me, me ^ 8, me ^ 16, me ^ 24]
    wave = copies(held, 4, 3)
    lax.fori_loop(1, n, sums_out, 0)
    finish(wave)
    held = held + [one ^ 4 for one in held]
    finish(copies(held, 2, 7))
    held = held + [one ^ 2 for one in held]
    finish(copies(held, 1, 15))
    loss, grad = contrast(every[...].reshape(n * rows, every.shape[2]), rows, micro_count)
    loss_ref[...] = jnp.broadcast_to(loss, loss_ref.shape)
    grad_ref[...] = grad
    own.wait()

    def sums_in(step, carry):
        peer = lax.rem(me + n - step, n)
        pltpu.make_async_remote_copy(
            src_ref=sums_ref.at[peer], dst_ref=got_ref.at[peer], send_sem=sum_send.at[step], recv_sem=sum_recv.at[step],
            device_id=(peer,), device_id_type=MESH).wait()
        return carry

    lax.fori_loop(1, n, sums_in, 0)


def gather_and_contrast(n, micro_count, pooled, sums):
    rows, width = pooled.shape
    vmem = pl.BlockSpec(memory_space=pltpu.VMEM)
    return pl.pallas_call(
        functools.partial(gather_kernel, n, micro_count),
        out_shape=(
            jax.ShapeDtypeStruct((8, 128), f32),
            jax.ShapeDtypeStruct((n * rows, width), f32),
            jax.ShapeDtypeStruct(sums.shape, f32),
        ),
        in_specs=[vmem, vmem],
        out_specs=(vmem, vmem, vmem),
        scratch_shapes=[
            pltpu.VMEM((n, rows, width), f32),
            pltpu.SemaphoreType.DMA((31,)),
            pltpu.SemaphoreType.DMA((31,)),
            pltpu.SemaphoreType.DMA((n,)),
            pltpu.SemaphoreType.DMA((n,)),
            pltpu.SemaphoreType.DMA,
        ],
        compiler_params=pltpu.CompilerParams(collective_id=0, has_side_effects=True, vmem_limit_bytes=48 << 20),
    )(pooled, sums)


CHUNK = 384


def scatter_kernel(chunks, terms_ref, out_ref, mine, core_got, first_got, second_got, owner_got, sems):
    me = lax.axis_index("dp")
    core, xx, yy, zz = me % 2, (me // 2) % 2, (me // 4) % 2, me // 8
    low_z = zz // 2
    kind = zz % 2
    meet([me ^ 1, me ^ 2, me ^ 4, me ^ 8, me ^ 16, me ^ 24])

    def columns(chunk):
        return pl.ds(pl.multiple_of(chunk * CHUNK, 128), CHUNK)

    def sem(stage, chunk, way):
        return sems.at[stage, chunk, way]

    def take(chunk):
        return pltpu.make_async_copy(terms_ref.at[:, :, :, core, :, columns(chunk)], mine.at[chunk], sem(0, chunk, 0))

    def to_core(chunk):
        return pltpu.make_async_remote_copy(
            src_ref=terms_ref.at[:, :, :, 1 - core, :, columns(chunk)], dst_ref=core_got.at[chunk],
            send_sem=sem(1, chunk, 0), recv_sem=sem(1, chunk, 1), device_id=(me ^ 1,), device_id_type=MESH)

    def first(chunk, along_x):
        src = mine.at[chunk, :, :, 1 - xx] if along_x else mine.at[chunk, :, 1 - yy]
        return pltpu.make_async_remote_copy(
            src_ref=src, dst_ref=first_got.at[chunk],
            send_sem=sem(2, chunk, 0), recv_sem=sem(2, chunk, 1), device_id=(me ^ (2 if along_x else 4),), device_id_type=MESH)

    def second(chunk, along_x):
        src = mine.at[chunk, :, 1 - yy, xx] if along_x else mine.at[chunk, :, yy, 1 - xx]
        return pltpu.make_async_remote_copy(
            src_ref=src, dst_ref=second_got.at[chunk],
            send_sem=sem(3, chunk, 0), recv_sem=sem(3, chunk, 1), device_id=(me ^ (4 if along_x else 2),), device_id_type=MESH)

    def third(chunk, half):
        target = 2 * kind + half
        return target, pltpu.make_async_remote_copy(
            src_ref=mine.at[chunk, half, yy, xx], dst_ref=owner_got.at[chunk, low_z],
            send_sem=sem(4, chunk, half), recv_sem=sem(5, chunk, low_z),
            device_id=(target * 8 + me % 8,), device_id_type=MESH)

    def start_core(chunk, carry):
        take(chunk).start()
        to_core(chunk).start()
        return carry

    lax.fori_loop(0, chunks, start_core, 0)

    def stage(pair, body):
        @pl.when((pair >= 0) & (pair < chunks // 2))
        def _():
            for odd in (0, 1):
                body(2 * pair + odd, odd == 0)

    def run_first(chunk, along_x):
        take(chunk).wait()
        to_core(chunk).wait()
        mine[chunk] = mine[chunk] + core_got[chunk]
        first(chunk, along_x).start()

    def run_second(chunk, along_x):
        first(chunk, along_x).wait()
        if along_x:
            mine[chunk, :, :, xx] = mine[chunk, :, :, xx] + first_got[chunk]
        else:
            mine[chunk, :, yy] = mine[chunk, :, yy] + first_got[chunk]
        second(chunk, along_x).start()

    def run_third(chunk, along_x):
        second(chunk, along_x).wait()
        mine[chunk, :, yy, xx] = mine[chunk, :, yy, xx] + second_got[chunk]
        for half in (0, 1):
            target, copy = third(chunk, half)

            @pl.when(target != zz)
            def _():
                copy.start()

            @pl.when(target == zz)
            def _():
                owner_got[chunk, low_z] = mine[chunk, half, yy, xx]

    def run_last(chunk, along_x):
        for half in (0, 1):
            target, copy = third(chunk, half)

            @pl.when(target != zz)
            def _():
                copy.wait_send()

        for source in (0, 1):
            @pl.when(2 * source + low_z != zz)
            def _():
                pltpu.make_async_remote_copy(
                    src_ref=mine.at[chunk, 0, yy, xx], dst_ref=owner_got.at[chunk, source],
                    send_sem=sem(4, chunk, 0), recv_sem=sem(5, chunk, source),
                    device_id=(me ^ 8,), device_id_type=MESH).wait_recv()

        out_ref[:, columns(chunk)] = owner_got[chunk, 0] + owner_got[chunk, 1]

    def step(pair, carry):
        stage(pair, run_first)
        stage(pair - 1, run_second)
        stage(pair - 2, run_third)
        stage(pair - 3, run_last)
        return carry

    lax.fori_loop(0, chunks // 2 + 3, step, 0)


def scatter_terms(terms):
    rows, columns = terms.shape
    own = rows // 16
    chunks = columns // CHUNK
    return pl.pallas_call(
        functools.partial(scatter_kernel, chunks),
        out_shape=jax.ShapeDtypeStruct((own, columns), f32),
        in_specs=[pl.BlockSpec(memory_space=pl.ANY)],
        out_specs=pl.BlockSpec(memory_space=pltpu.VMEM),
        scratch_shapes=[
            pltpu.VMEM((chunks, 2, 2, 2, own, CHUNK), f32),
            pltpu.VMEM((chunks, 2, 2, 2, own, CHUNK), f32),
            pltpu.VMEM((chunks, 2, 2, own, CHUNK), f32),
            pltpu.VMEM((chunks, 2, own, CHUNK), f32),
            pltpu.VMEM((chunks, 2, own, CHUNK), f32),
            pltpu.SemaphoreType.DMA((6, chunks, 2)),
        ],
        compiler_params=pltpu.CompilerParams(collective_id=1, has_side_effects=True, vmem_limit_bytes=56 << 20),
    )(terms.reshape(2, 2, 2, 2, own, columns))


def params_of(weights, modality):
    return tuple(lax.dynamic_index_in_dim(one, modality, 0, keepdims=False) for one in weights)


def tokens_of(patches, visible, modality):
    micro_count, images, _, patch_count, width = patches.shape
    cells = lax.dynamic_index_in_dim(patches, modality, 2, keepdims=False).reshape(micro_count * images, patch_count, width)
    picked = (visible[:, :, None] == jnp.arange(patch_count)[None, None, :]).astype(bf16)
    return jnp.einsum("isp,ipd->isd", picked, cells, preferred_element_type=f32)


def cells_of(grad_tokens, visible, patch_count):
    picked = (visible[:, None, :] == jnp.arange(patch_count)[None, :, None]).astype(f32)
    return jnp.einsum("ips,isd->ipd", picked, grad_tokens, precision=highest)


def on_device(patches, visible, valid_mask, *weights):
    n = lax.axis_size("dp")
    me = lax.axis_index("dp")
    micro_count, images, _, patch_count, width = patches.shape
    own = micro_count * images
    slots = visible.shape[-1]
    ff = weights[6].shape[2]
    seen = visible.reshape(own, slots)
    mask = valid_mask.reshape(own, slots)
    tuned = n == 32
    kind = (me // 8) % 2 if tuned else 0
    first = params_of(weights, kind)
    other = params_of(weights, 1 - kind)
    tokens_first = tokens_of(patches, seen, kind)
    tokens_other = tokens_of(patches, seen, 1 - kind)
    seen_first, mask_first = seen, mask
    if tuned:
        swap = [(i, i ^ 8) for i in range(n)]
        foreign, seen_there, mask_there = (lax.ppermute(one, "dp", swap) for one in (tokens_other, seen, mask))
        tokens_first = jnp.concatenate([tokens_first, foreign])
        seen_first = jnp.concatenate([seen, seen_there])
        mask_first = jnp.concatenate([mask, mask_there])
    active_first, mixed_first, saved_first = encode_forward(tokens_first, seen_first, mask_first, first)
    active_other, mixed_other, saved_other = encode_forward(tokens_other, seen, mask, other)
    pooled_first = pool(active_first[:own], mixed_first[:own], mask, first[8])
    pooled_other = pool(active_other, mixed_other, mask, other[8])
    counted = jnp.sum(mask.astype(f32), axis=1)[:, None]
    swapped = jnp.asarray(kind == 1)
    pooled = jnp.where(swapped, jnp.concatenate([pooled_other, pooled_first]), jnp.concatenate([pooled_first, pooled_other]))
    share_first, share_other = active_first[:own] / counted, active_other / counted
    shares = jnp.where(swapped, jnp.stack([share_other, share_first]), jnp.stack([share_first, share_other]))
    down_rows = 2 * ff // n
    shares = shares.reshape(2, own, n // 2, down_rows).transpose(0, 2, 1, 3).reshape(n, own * down_rows)
    if tuned:
        padded = jnp.pad(shares, ((0, 0), (0, 1024 - own * down_rows))).reshape(n, 8, 128)
        loss, grad_all, got = gather_and_contrast(n, micro_count, pooled, padded)
        got = got.reshape(n, 1024)[:, : own * down_rows]
    else:
        loss, grad_all = contrast(lax.all_gather(pooled, "dp", axis=0, tiled=True), 2 * own, micro_count)
        got = lax.all_to_all(shares, "dp", 0, 0, tiled=True)
    grad_all = grad_all.reshape(n, 2, own, width)
    holder = me // (n // 2)
    grad_down = jnp.einsum(
        "iw,id->wd", got.reshape(n * own, down_rows),
        lax.dynamic_index_in_dim(grad_all, holder, 1, keepdims=False).reshape(n * own, width), precision=highest)
    mine = lax.dynamic_index_in_dim(grad_all, me, 0, keepdims=False)
    grad_first = lax.dynamic_index_in_dim(mine, kind, 0, keepdims=False)
    grad_other = lax.dynamic_index_in_dim(mine, 1 - kind, 0, keepdims=False)
    if tuned:
        there = lax.dynamic_index_in_dim(grad_all, me ^ 8, 0, keepdims=False)
        grad_first = jnp.concatenate([grad_first, lax.dynamic_index_in_dim(there, kind, 0, keepdims=False)])
    back_first, terms_first = encode_backward(grad_first, saved_first, mask_first, first)
    back_other, terms_other = encode_backward(grad_other, saved_other, mask, other)
    cells_first = cells_of(back_first[:own], seen, patch_count)
    cells_other = cells_of(back_other, seen, patch_count)
    patches_grad = jnp.where(swapped, jnp.stack([cells_other, cells_first], 1), jnp.stack([cells_first, cells_other], 1))
    patches_grad = patches_grad.reshape(micro_count, images, 2, patch_count, width)
    if tuned:
        gain_one, shift_one, qkv, out, gain_two, shift_two, up, bias = terms_first
        small = [one.reshape(width, 1) for one in (gain_one, shift_one, gain_two, shift_two)] + [bias.reshape(width, -1)]
        extra = jnp.concatenate(small, axis=1)
        extra = jnp.pad(extra, ((0, 0), (0, 2 * CHUNK - extra.shape[1])))
        summed = scatter_terms(jnp.concatenate([up, out, qkv, extra], axis=1))
        cuts = [ff, ff + width, ff + 4 * width]
        up, out, qkv, extra = jnp.split(summed, cuts, axis=1)
        shards = (extra[:, 0], extra[:, 1], qkv, out, extra[:, 2], extra[:, 3], up, extra[:, 4 : 4 + ff // width].reshape(-1))
    else:
        joined = jax.tree.map(lambda a, b: jnp.concatenate([a, b]), terms_first, terms_other)
        shards = tuple(lax.psum_scatter(one, "dp", scatter_dimension=0, tiled=True) for one in joined)
    return (loss[0, 0], patches_grad) + shards + (grad_down,)


def solution(mesh):
    in_specs = (P(None, "dp"), P(None, "dp"), P(None, "dp")) + (P(),) * 9
    out_specs = (P(), P(None, "dp")) + (P("dp"),) * 9
    return jax.shard_map(on_device, mesh=mesh, in_specs=in_specs, out_specs=out_specs, check_vma=False)
```

```python
import functools
import math

import jax
import jax.numpy as jnp
from jax import lax
from jax.experimental import pallas as pl
from jax.experimental.pallas import tpu as pltpu
from jax.sharding import PartitionSpec as P

HEADS = 12
HEAD_DIM = 64
GRID = 15
MESH = pl.DeviceIdType.MESH

norm_epsilon = 1e-06
unit_epsilon = 1e-06
logit_scale = 100.0
masked_score = -1e30
highest = lax.Precision.HIGHEST
head_scale = 1.0 / math.sqrt(HEAD_DIM)
f32 = jnp.float32
bf16 = jnp.bfloat16


def exact_gelu(values_in):
    return jax.nn.gelu(values_in, approximate=False)


def layer_norm(values_in, gain_vec, shift_vec):
    centre = values_in - jnp.mean(values_in, axis=-1, keepdims=True)
    inverse = lax.rsqrt(jnp.mean(centre * centre, axis=-1, keepdims=True) + norm_epsilon)
    normed = centre * inverse
    return (normed * gain_vec + shift_vec, normed, inverse)


def norm_back(grad_out, normed, inverse, gain_vec):
    grad_normed = grad_out * gain_vec
    mean_plain = jnp.mean(grad_normed, axis=-1, keepdims=True)
    mean_normed = jnp.mean(grad_normed * normed, axis=-1, keepdims=True)
    grad_in = inverse * (grad_normed - mean_plain - normed * mean_normed)
    return (grad_in, jnp.sum(grad_out * normed, axis=0), jnp.sum(grad_out, axis=0))


def alibi_bias(visible_rows):
    rows_pos = (visible_rows // GRID).astype(f32)
    cols_pos = (visible_rows % GRID).astype(f32)
    rows_gap = rows_pos[:, :, None] - rows_pos[:, None, :]
    cols_gap = cols_pos[:, :, None] - cols_pos[:, None, :]
    distance = jnp.sqrt(rows_gap * rows_gap + cols_gap * cols_gap)
    slopes = jnp.exp2(-8.0 * (jnp.arange(HEADS, dtype=f32) + 1.0) / HEADS)
    return -slopes[None, :, None, None] * distance[:, None, :, :]


def split_heads(packed):
    images, slot_count, _ = packed.shape
    shaped = packed.reshape(images, slot_count, 3, HEADS, HEAD_DIM)
    return (shaped[:, :, 0], shaped[:, :, 1], shaped[:, :, 2])


def encode_forward(tokens_in, visible_rows, mask_rows, params):
    gain_one, shift_one, w_qkv, w_out, gain_two, shift_two, w_up, b_up, w_down = params
    images, slots, width = tokens_in.shape
    flat_in = tokens_in.reshape(images * slots, width)
    hidden_one, normed_one, inverse_one = layer_norm(flat_in, gain_one, shift_one)
    hidden_one = hidden_one.astype(bf16)
    packed = jnp.dot(hidden_one, w_qkv, preferred_element_type=f32).astype(bf16)
    packed = packed.reshape(images, slots, 3 * width)
    queries, keys, values = split_heads(packed)
    scores = jnp.einsum("iqhd,ikhd->ihqk", queries, keys, preferred_element_type=f32)
    scores = scores * head_scale + alibi_bias(visible_rows)
    scores = jnp.where((mask_rows > 0)[:, None, None, :], scores, masked_score)
    attention = jax.nn.softmax(scores, axis=-1)
    attended = jnp.einsum("ihqk,ikhd->iqhd", attention.astype(bf16), values, preferred_element_type=f32)
    attended = attended.reshape(images * slots, width).astype(bf16)
    mixed = flat_in + jnp.dot(attended, w_out, preferred_element_type=f32)
    hidden_two, normed_two, inverse_two = layer_norm(mixed, gain_two, shift_two)
    hidden_two = hidden_two.astype(bf16)
    upper = jnp.dot(hidden_two, w_up, preferred_element_type=f32) + b_up
    active, gelu_back = jax.vjp(exact_gelu, upper)
    active = active.astype(bf16).astype(f32)
    weight = mask_rows.astype(f32)
    active_sum = jnp.sum(active.reshape(images, slots, -1) * weight[:, :, None], axis=1)
    mixed_sum = jnp.sum(mixed.reshape(images, slots, width) * weight[:, :, None], axis=1)
    saved = (normed_one, inverse_one, hidden_one, packed, attention, attended, normed_two, inverse_two, hidden_two, gelu_back)
    return active_sum, mixed_sum, saved


def pool(active_sum, mixed_sum, mask_rows, w_down):
    counted = jnp.sum(mask_rows.astype(f32), axis=1)[:, None]
    down = jnp.dot(active_sum, w_down.astype(f32), precision=highest)
    return (mixed_sum + down) / counted


def encode_backward(grad_pooled, saved, mask_rows, params):
    normed_one, inverse_one, hidden_one, packed, attention, attended, normed_two, inverse_two, hidden_two, gelu_back = saved
    gain_one, shift_one, w_qkv, w_out, gain_two, shift_two, w_up, b_up, w_down = params
    images, slots, three_width = packed.shape
    width = three_width // 3
    rows = images * slots
    weight = mask_rows.astype(f32)
    counted = jnp.sum(weight, axis=1)[:, None]
    grad_row = grad_pooled / counted
    grad_output = (weight[:, :, None] * grad_row[:, None, :]).reshape(rows, width)
    grad_active = jnp.dot(grad_row.astype(bf16), w_down.T, preferred_element_type=f32)
    grad_active = (weight[:, :, None] * grad_active[:, None, :]).reshape(rows, -1)
    grad_upper = gelu_back(grad_active)[0].astype(bf16)
    grad_bias = jnp.sum(grad_upper.astype(f32), axis=0)
    grad_up = jnp.dot(hidden_two.T, grad_upper, preferred_element_type=f32)
    grad_hidden_two = jnp.dot(grad_upper, w_up.T, preferred_element_type=f32)
    grad_norm_two, grad_gain_two, grad_shift_two = norm_back(grad_hidden_two, normed_two, inverse_two, gain_two)
    grad_mixed = grad_output + grad_norm_two
    grad_mixed_low = grad_mixed.astype(bf16)
    grad_out = jnp.dot(attended.T, grad_mixed_low, preferred_element_type=f32)
    grad_attended = jnp.dot(grad_mixed_low, w_out.T, preferred_element_type=f32).astype(bf16)
    grad_attended = grad_attended.reshape(images, slots, HEADS, HEAD_DIM)
    queries, keys, values = split_heads(packed)
    grad_value = jnp.einsum("ihqk,iqhd->ikhd", attention.astype(bf16), grad_attended, preferred_element_type=f32)
    grad_attention = jnp.einsum("iqhd,ikhd->ihqk", grad_attended, values, preferred_element_type=f32)
    grad_scores = attention * (grad_attention - jnp.sum(attention * grad_attention, axis=-1, keepdims=True))
    grad_scores = grad_scores.astype(bf16)
    grad_query = jnp.einsum("ihqk,ikhd->iqhd", grad_scores, keys, preferred_element_type=f32) * head_scale
    grad_key = jnp.einsum("ihqk,iqhd->ikhd", grad_scores, queries, preferred_element_type=f32) * head_scale
    grad_packed = jnp.stack([grad_query, grad_key, grad_value], axis=2).astype(bf16).reshape(rows, three_width)
    grad_qkv = jnp.dot(hidden_one.T, grad_packed, preferred_element_type=f32)
    grad_hidden_one = jnp.dot(grad_packed, w_qkv.T, preferred_element_type=f32)
    grad_norm_one, grad_gain_one, grad_shift_one = norm_back(grad_hidden_one, normed_one, inverse_one, gain_one)
    grad_tokens = (grad_mixed + grad_norm_one).reshape(images, slots, width)
    return grad_tokens, (grad_gain_one, grad_shift_one, grad_qkv, grad_out, grad_gain_two, grad_shift_two, grad_up, grad_bias)


def contrast(pooled, own_rows, micro_count):
    count = pooled.shape[0]
    images = own_rows // (2 * micro_count)
    inverse = lax.rsqrt(jnp.sum(pooled * pooled, axis=-1, keepdims=True) + unit_epsilon)
    unit = pooled * inverse
    logits = logit_scale * lax.dot_general(unit, unit, (((1,), (1,)), ((), ())), precision=highest, preferred_element_type=f32)
    row = lax.broadcasted_iota(jnp.int32, (count, count), 0)
    col = lax.broadcasted_iota(jnp.int32, (count, count), 1)
    half = own_rows // 2
    row_mod, col_mod = (row // half) % 2, (col // half) % 2
    row_micro, col_micro = (row // images) % micro_count, (col // images) % micro_count
    allowed = (row_mod != col_mod) & (row_micro == col_micro)
    paired = jnp.where(col == row + half * (1 - 2 * row_mod), 1.0, 0.0)
    logits = jnp.where(allowed, logits, masked_score)
    row_max = jnp.max(logits, axis=1, keepdims=True)
    row_lse = row_max + jnp.log(jnp.sum(jnp.exp(logits - row_max), axis=1, keepdims=True))
    col_max = jnp.max(logits, axis=0, keepdims=True)
    col_lse = col_max + jnp.log(jnp.sum(jnp.exp(logits - col_max), axis=0, keepdims=True))
    scale = 1.0 / count
    diagonal = jnp.sum(jnp.where(paired > 0, logits, 0.0), axis=1, keepdims=True)
    loss = scale * jnp.sum(row_lse - diagonal, axis=0, keepdims=True)
    spread = jnp.exp(logits - row_lse) + jnp.exp(logits - col_lse) - 2.0 * paired
    grad_unit = (logit_scale * scale) * jnp.dot(spread, unit, precision=highest, preferred_element_type=f32)
    grad_pooled = inverse * (grad_unit - unit * jnp.sum(unit * grad_unit, axis=-1, keepdims=True))
    return loss, grad_pooled


def meet(peers):
    barrier = pltpu.get_barrier_semaphore()
    for peer in peers:
        pl.semaphore_signal(barrier, inc=1, device_id=(peer,), device_id_type=MESH)
    pl.semaphore_wait(barrier, len(peers))


def gather_kernel(n, micro_count, pooled_ref, sums_ref, loss_ref, grad_ref, got_ref, every, send_sem, recv_sem, sum_send, sum_recv, local_sem):
    me = lax.axis_index("dp")
    rows = pooled_ref.shape[0]
    barrier = pltpu.get_barrier_semaphore()

    def greet(step, carry):
        pl.semaphore_signal(barrier, inc=1, device_id=(lax.rem(me + step, n),), device_id_type=MESH)
        return carry

    lax.fori_loop(1, n, greet, 0)
    pl.semaphore_wait(barrier, n - 1)
    every[me] = pooled_ref[...]
    slot = 0

    def copies(sources, flip, first):
        made = []
        for number, source in enumerate(sources):
            made.append(
                pltpu.make_async_remote_copy(
                    src_ref=every.at[source],
                    dst_ref=every.at[source],
                    send_sem=send_sem.at[first + number],
                    recv_sem=recv_sem.at[first + number],
                    device_id=(me ^ flip,),
                    device_id_type=MESH,
                )
            )
        for copy in made:
            copy.start()
        return made

    def finish(made):
        for copy in made:
            copy.wait()

    held = [me]
    waves = []
    for number, flip in enumerate((8, 16, 24)):
        waves += copies([me], flip, number)
    def sums_out(step, carry):
        peer = lax.rem(me + step, n)
        pltpu.make_async_remote_copy(
            src_ref=sums_ref.at[peer], dst_ref=got_ref.at[me], send_sem=sum_send.at[step], recv_sem=sum_recv.at[step],
            device_id=(peer,), device_id_type=MESH).start()
        return carry

    own = pltpu.make_async_copy(sums_ref.at[me], got_ref.at[me], local_sem)
    own.start()
    finish(waves)
    held = [me, me ^ 8, me ^ 16, me ^ 24]
    wave = copies(held, 4, 3)
    lax.fori_loop(1, n, sums_out, 0)
    finish(wave)
    held = held + [one ^ 4 for one in held]
    finish(copies(held, 2, 7))
    held = held + [one ^ 2 for one in held]
    finish(copies(held, 1, 15))
    loss, grad = contrast(every[...].reshape(n * rows, every.shape[2]), rows, micro_count)
    loss_ref[...] = jnp.broadcast_to(loss, loss_ref.shape)
    grad_ref[...] = grad
    own.wait()

    def sums_in(step, carry):
        peer = lax.rem(me + n - step, n)
        pltpu.make_async_remote_copy(
            src_ref=sums_ref.at[peer], dst_ref=got_ref.at[peer], send_sem=sum_send.at[step], recv_sem=sum_recv.at[step],
            device_id=(peer,), device_id_type=MESH).wait()
        return carry

    lax.fori_loop(1, n, sums_in, 0)


def gather_and_contrast(n, micro_count, pooled, sums):
    rows, width = pooled.shape
    vmem = pl.BlockSpec(memory_space=pltpu.VMEM)
    return pl.pallas_call(
        functools.partial(gather_kernel, n, micro_count),
        out_shape=(
            jax.ShapeDtypeStruct((8, 128), f32),
            jax.ShapeDtypeStruct((n * rows, width), f32),
            jax.ShapeDtypeStruct(sums.shape, f32),
        ),
        in_specs=[vmem, vmem],
        out_specs=(vmem, vmem, vmem),
        scratch_shapes=[
            pltpu.VMEM((n, rows, width), f32),
            pltpu.SemaphoreType.DMA((31,)),
            pltpu.SemaphoreType.DMA((31,)),
            pltpu.SemaphoreType.DMA((n,)),
            pltpu.SemaphoreType.DMA((n,)),
            pltpu.SemaphoreType.DMA,
        ],
        compiler_params=pltpu.CompilerParams(collective_id=0, has_side_effects=True, vmem_limit_bytes=48 << 20),
    )(pooled, sums)


def params_of(weights, modality):
    return tuple(lax.dynamic_index_in_dim(one, modality, 0, keepdims=False) for one in weights)


GROWS = 32
SLOPES = [2.0 ** (-8.0 * (head + 1) / HEADS) for head in range(HEADS)]
ROWS = 32
WIDE = 256


def gelu_pair(upper):
    size = jnp.abs(upper)
    bell = jnp.exp(-0.5 * upper * upper)
    below = 1.0 + (0.3275911 * math.sqrt(0.5)) * size
    t = pltpu.reciprocal(below, approx=True)
    t = t * (2.0 - below * t)
    tail = t * (0.5 * 0.254829592 + t * (0.5 * -0.284496736 + t * (0.5 * 1.421413741 + t * (0.5 * -1.453152027 + t * (0.5 * 1.061405429)))))
    tail = tail * bell
    normal = jnp.where(upper < 0, tail, 1.0 - tail)
    return upper * normal, normal + upper * (bell * (1.0 / math.sqrt(2.0 * math.pi)))


def row_norm(values):
    centre = values - jnp.mean(values, axis=-1, keepdims=True)
    inverse = lax.rsqrt(jnp.mean(centre * centre, axis=-1, keepdims=True) + norm_epsilon)
    return centre * inverse, inverse


def dot(a, b):
    return jnp.dot(a, b, preferred_element_type=f32)


def dot_nt(a, b):
    return lax.dot_general(a, b, (((1,), (1,)), ((), ())), preferred_element_type=f32)


def dot_tn(a, b):
    return lax.dot_general(a, b, (((0,), (0,)), ((), ())), preferred_element_type=f32)


def forward_kernel(kinds, places, tok, row_info, col_info, block_mask, gain_one, shift_one, w_qkv, w_out, gain_two, shift_two, w_up, b_up, w_down,
                   *refs):
    one_t, packed, probs, att_t, mixed, two_t, slope, active_sum, pooled, upper, active, hidden, attended, hidden_t = refs[-14:]
    images, slots, width = tok.shape
    rows = images * slots
    ff = w_up.shape[2]

    def norm_one(image, carry):
        for r in range(0, slots, ROWS):
            normed, _ = row_norm(tok[image, r : r + ROWS, :])
            hidden[image, r : r + ROWS, :] = (normed * gain_one[0] + shift_one[0]).astype(bf16)
        one_t[image] = hidden[image].T.reshape(one_t.shape[1:])
        return carry

    lax.fori_loop(0, images, norm_one, 0)
    flat_one = hidden[...].reshape(rows, width)

    def project(i, carry):
        at = pl.ds(pl.multiple_of(i * 384, 384), 384)
        packed[:, :, at] = dot(flat_one, w_qkv[0, :, at]).astype(bf16).reshape(images, slots, 384)
        return carry

    lax.fori_loop(0, 3 * width // 384, project, 0)
    low_half = lax.broadcasted_iota(jnp.int32, (slots, 128), 1) < HEAD_DIM

    def attend(image, carry):
        info, column = row_info[image], col_info[image]
        gap_r = column[:, 0:1] - info[0:1, :]
        gap_c = column[:, 1:2] - info[1:2, :]
        away = -jnp.sqrt(gap_r * gap_r + gap_c * gap_c)
        away = jnp.where(column[:, 2:3] > 0, away, -1e33)
        for pair in range(HEADS // 2):
            at = slice(pair * 128, pair * 128 + 128)
            queries = packed[image, :, pair * 128 : pair * 128 + 128]
            keys = packed[image, :, width + pair * 128 : width + pair * 128 + 128]
            values = packed[image, :, 2 * width + pair * 128 : 2 * width + pair * 128 + 128]
            blank = jnp.zeros_like(keys)
            two_keys = jnp.concatenate([jnp.where(low_half, keys, blank), jnp.where(low_half, blank, keys)])
            two_values = jnp.concatenate([jnp.where(low_half, values, blank), jnp.where(low_half, blank, values)])
            scores = dot_nt(two_keys, queries)
            shares = []
            for side in (0, 1):
                one = scores[side * slots : side * slots + slots] * head_scale + SLOPES[2 * pair + side] * away
                power = jnp.exp(one - jnp.max(one, axis=0, keepdims=True))
                shares.append((power * (1.0 / jnp.sum(power, axis=0, keepdims=True))).astype(bf16))
            share = jnp.concatenate(shares)
            probs[image, pair] = share
            flipped = dot_tn(two_values, share).astype(bf16)
            hidden_t[at, :] = flipped
            attended[image, :, at] = flipped.T
        att_t[image] = hidden_t[...].reshape(att_t.shape[1:])
        return carry

    lax.fori_loop(0, images, attend, 0)
    flat_att = attended[...].reshape(rows, width)

    def output(i, carry):
        at = pl.ds(pl.multiple_of(i * 256, 256), 256)
        mixed[:, :, at] = tok[:, :, at] + dot(flat_att, w_out[0, :, at]).reshape(images, slots, 256)
        return carry

    lax.fori_loop(0, width // 256, output, 0)

    def norm_two(image, carry):
        for r in range(0, slots, ROWS):
            normed, _ = row_norm(mixed[image, r : r + ROWS, :])
            hidden[image, r : r + ROWS, :] = (normed * gain_two[0] + shift_two[0]).astype(bf16)
        two_t[image] = hidden[image].T.reshape(two_t.shape[1:])
        return carry

    lax.fori_loop(0, images, norm_two, 0)
    flat_two = hidden[...].reshape(rows, width)
    marks = block_mask[0]

    def columns(i):
        return pl.ds(pl.multiple_of(i * WIDE, WIDE), WIDE)

    upper[0] = dot(flat_two, w_up[0, :, columns(0)])

    def bend(i, now):
        bias = b_up[0, :, columns(i)]
        for r in range(0, rows, GROWS):
            value, back = gelu_pair(upper[now, r : r + GROWS, :] + bias)
            active[r : r + GROWS, :] = value.astype(bf16)
            slope[r // slots, r % slots : r % slots + GROWS, columns(i)] = back.astype(bf16)
        active_sum[0, :, columns(i)] = dot(marks, active[...])

    def feed(i, carry):
        upper[1] = dot(flat_two, w_up[0, :, columns(2 * i + 1)])
        bend(2 * i, 0)
        upper[0] = dot(flat_two, w_up[0, :, columns(2 * i + 2)])
        bend(2 * i + 1, 1)
        return carry

    steps = ff // WIDE
    lax.fori_loop(0, steps // 2 - 1, feed, 0)
    upper[1] = dot(flat_two, w_up[0, :, columns(steps - 1)])
    bend(steps - 2, 0)
    bend(steps - 1, 1)
    total = active_sum[0]
    high = total.astype(bf16)
    rest = total - high.astype(f32)
    middle = rest.astype(bf16)
    lowest = (rest - middle.astype(f32)).astype(bf16)
    downs = dot(high, w_down[0]) + dot(middle, w_down[0]) + dot(lowest, w_down[0])
    for image in range(images):
        weight = col_info[image][:, 2:3]
        sums = jnp.sum(mixed[image] * weight, axis=0, keepdims=True)
        pooled[0, image : image + 1, :] = (sums + downs[image : image + 1]) / jnp.sum(weight, axis=0, keepdims=True)
    pooled[0, images:, :] = jnp.zeros((pooled.shape[1] - images, width), f32)


def encode_groups(kinds, places, saved, tokens, row_info, col_info, block_mask, weights, places_total):
    gain_one, shift_one, w_qkv, w_out, gain_two, shift_two, w_up, b_up, w_down = weights
    groups = kinds.shape[0]
    total, slots, width = tokens.shape
    images = total // groups
    ff = w_up.shape[2]

    def grouped(*dims):
        return pl.BlockSpec((images,) + dims, lambda g, kinds, places: (g,) + (0,) * len(dims))

    def placed(*dims):
        return pl.BlockSpec((images,) + dims, lambda g, kinds, places: (places[g],) + (0,) * len(dims))

    def whole(array):
        return pl.BlockSpec((1,) + array.shape[1:], lambda g, kinds, places: (kinds[g],) + (0,) * (array.ndim - 1))

    vectors = [one.reshape(2, 1, -1) for one in (gain_one, shift_one, gain_two, shift_two, b_up)]
    operands = [vectors[0], vectors[1], w_qkv, w_out, vectors[2], vectors[3], w_up, vectors[4], w_down]
    turned = (16, width // 16, slots)
    kept = [(turned, bf16), ((slots, 3 * width), bf16), ((HEADS // 2, 2 * slots, slots), bf16), (turned, bf16), ((slots, width), f32),
            (turned, bf16), ((slots, ff), bf16)]
    before = [] if saved is None else list(saved)
    return pl.pallas_call(
        forward_kernel,
        grid_spec=pltpu.PrefetchScalarGridSpec(
            num_scalar_prefetch=2,
            grid=(groups,),
            in_specs=[grouped(slots, width), grouped(8, slots), grouped(slots, 8),
                      pl.BlockSpec((1, 8, images * slots), lambda g, kinds, places: (g, 0, 0))]
            + [whole(one) for one in operands] + [pl.BlockSpec(memory_space=pl.ANY)] * len(before),
            out_specs=[placed(*dims) for dims, _ in kept]
            + [pl.BlockSpec((1, 8, size), lambda g, kinds, places: (g, 0, 0)) for size in (ff, width)],
            scratch_shapes=[pltpu.VMEM((2, images * slots, WIDE), f32), pltpu.VMEM((images * slots, WIDE), bf16),
                            pltpu.VMEM((images, slots, width), bf16), pltpu.VMEM((images, slots, width), bf16), pltpu.VMEM((width, slots), bf16)],
        ),
        out_shape=[jax.ShapeDtypeStruct((places_total * images,) + dims, dtype) for dims, dtype in kept]
        + [jax.ShapeDtypeStruct((groups, 8, size), f32) for size in (ff, width)],
        input_output_aliases={15 + i: i for i in range(len(before))},
        compiler_params=pltpu.CompilerParams(vmem_limit_bytes=60 << 20),
        cost_estimate=pl.CostEstimate(flops=2 * total * slots * 8 * width * width, bytes_accessed=groups * (25 << 20), transcendentals=0),
    )(kinds, places, tokens, row_info, col_info, block_mask, *operands, *before)


def slot_info(seen, mask):
    rows = jnp.stack([(seen // GRID).astype(f32), (seen % GRID).astype(f32), mask.astype(f32)], axis=1)
    return jnp.pad(rows, ((0, 0), (0, 5), (0, 0)))


def group_marks(mask, images):
    total, slots = mask.shape
    eye = (jnp.arange(8)[:, None] == jnp.arange(images)[None, :]).astype(bf16)
    marks = mask.reshape(total // images, 1, images, slots).astype(bf16) * eye[None, :, :, None]
    return marks.reshape(total // images, 8, images * slots)


CHUNK = 384


def tokens_kernel(kinds, seen, cells, out):
    patch_count = cells.shape[2]
    slots = seen.shape[2]
    picked = jnp.where(lax.broadcasted_iota(jnp.int32, (patch_count, slots), 0) == seen[0], 1.0, 0.0).astype(bf16)
    out[0] = dot_tn(picked, cells[0, 0])


def pick_tokens(kinds, seen, cells):
    images, _, patch_count, width = cells.shape
    slots = seen.shape[1]
    return pl.pallas_call(
        tokens_kernel,
        grid_spec=pltpu.PrefetchScalarGridSpec(
            num_scalar_prefetch=1,
            grid=(2, images),
            in_specs=[pl.BlockSpec((1, 1, slots), lambda g, i, kinds: (i, 0, 0)),
                      pl.BlockSpec((1, 1, patch_count, width), lambda g, i, kinds: (i, kinds[g], 0, 0))],
            out_specs=pl.BlockSpec((1, slots, width), lambda g, i, kinds: (g * images + i, 0, 0)),
        ),
        out_shape=jax.ShapeDtypeStruct((2 * images, slots, width), f32),
        cost_estimate=pl.CostEstimate(flops=4 * images * slots * 256 * width, bytes_accessed=8 << 20, transcendentals=0),
    )(kinds, seen.reshape(images, 1, slots), cells)


def cells_kernel(kinds, seen, grads, out):
    patch_count = out.shape[2]
    slots = seen.shape[2]
    picked = jnp.where(lax.broadcasted_iota(jnp.int32, (patch_count, slots), 0) == seen[0], 1.0, 0.0).astype(bf16)
    value = grads[0]
    high = value.astype(bf16)
    rest = value - high.astype(f32)
    middle = rest.astype(bf16)
    lowest = (rest - middle.astype(f32)).astype(bf16)
    out[0, 0] = dot(picked, high) + dot(picked, middle) + dot(picked, lowest)


def place_cells(kinds, seen, grads, patch_count):
    total, slots, width = grads.shape
    images = total // 2
    return pl.pallas_call(
        cells_kernel,
        grid_spec=pltpu.PrefetchScalarGridSpec(
            num_scalar_prefetch=1,
            grid=(2, images),
            in_specs=[pl.BlockSpec((1, 1, slots), lambda g, i, kinds: (i, 0, 0)),
                      pl.BlockSpec((1, slots, width), lambda g, i, kinds: (g * images + i, 0, 0))],
            out_specs=pl.BlockSpec((1, 1, patch_count, width), lambda g, i, kinds: (i, kinds[g], 0, 0)),
        ),
        out_shape=jax.ShapeDtypeStruct((images, 2, patch_count, width), f32),
        cost_estimate=pl.CostEstimate(flops=12 * images * slots * 256 * width, bytes_accessed=8 << 20, transcendentals=0),
    )(kinds, seen.reshape(images, 1, slots), grads)


def backward_kernel(own, grad_rows, masks, gain_one, gain_two, tokens, foreign, one_t, packed, probs, att_t, mixed, two_t, slope,
                    w_qkv, w_out, w_up, w_down,
                    up_out, out_out, qkv_out, extra_out, tokens_out,
                    mine, ring, core_got, first_got, second_got, owner_got, summed,
                    extra, extra_mine, extra_core, extra_first, extra_second, extra_owner,
                    wide, mixed_grad, mixed_low, turned, weights, active_grad, sums, packs, shares, rows_in, rows_out, hidden_grad,
                    sems, extra_sems, wsem, dsem, tsem, psem, rsem, osem):
    me = lax.axis_index("dp")
    core, xx, yy, zz = me % 2, (me // 2) % 2, (me // 4) % 2, me // 8
    kind, low_z = zz % 2, zz // 2
    slots, width = mixed.shape[1:]
    ff = slope.shape[2]
    both = 2 * own
    pairs = 2 * ff // width
    up_pairs = ff // width

    def load_slope(place, count, j):
        at = pl.ds(pl.multiple_of(j * width, 128), width)
        return pltpu.make_async_copy(slope.at[pl.ds(place, count), :, at], wide.at[pl.ds(0, count), :, at], dsem.at[j])

    def load_down(which, j):
        at = pl.ds(pl.multiple_of(j * width, 128), width)
        return pltpu.make_async_copy(w_down.at[which, at, :], weights.at[1, :, at], wsem.at[j])

    def load_up(which):
        return pltpu.make_async_copy(w_up.at[which], weights.at[0], wsem.at[4])

    def load_rest(which):
        return (pltpu.make_async_copy(w_qkv.at[which], weights.at[1, :, pl.ds(0, 3 * width)], wsem.at[5]),
                pltpu.make_async_copy(w_out.at[which], weights.at[1, :, pl.ds(3 * width, width)], wsem.at[6]))

    def load_turned(source, slot, image, part):
        return pltpu.make_async_copy(
            source.at[image, :, part], turned.at[slot, part, :, :, pl.ds(pl.multiple_of(image * slots, 128), slots)], tsem.at[slot, part, image])

    def all_turned(source, slot, act):
        def one(image, carry):
            for part in (0, 1):
                act(load_turned(source, slot, image, part))
            return carry

        lax.fori_loop(0, both, one, 0)

    def begin(copy):
        copy.start()

    def finish(copy):
        copy.wait()

    for j in range(up_pairs):
        load_down(kind, j).start()
    load_slope(0, both, 0).start()
    all_turned(two_t, 0, begin)
    for j in range(1, up_pairs):
        load_slope(0, both, j).start()
    load_up(kind).start()
    all_turned(att_t, 1, begin)

    meet([me ^ 1, me ^ 2, me ^ 4, me ^ 8, me ^ 16, me ^ 24])

    def sem(stage, chunk, way):
        return sems.at[stage, chunk, way]

    def chunk_sem(chunk, stage, way):
        return sems.at[stage, chunk, way]

    def extra_sem(stage, way):
        return extra_sems.at[stage, way]

    def remote(src, dst, send, recv, flip):
        return pltpu.make_async_remote_copy(src_ref=src, dst_ref=dst, send_sem=send, recv_sem=recv, device_id=(me ^ flip,), device_id_type=MESH)

    def to_core(chunk):
        return remote(ring.at[(chunk // 2) % 2, chunk % 2], core_got.at[chunk], sem(1, chunk, 0), sem(1, chunk, 1), 1)

    def first(chunk, along_x):
        src = mine.at[chunk, :, :, 1 - xx] if along_x else mine.at[chunk, :, 1 - yy]
        return remote(src, first_got.at[chunk], sem(2, chunk, 0), sem(2, chunk, 1), 2 if along_x else 4)

    def second(chunk, along_x):
        src = mine.at[chunk, :, 1 - yy, xx] if along_x else mine.at[chunk, :, yy, 1 - xx]
        return remote(src, second_got.at[chunk], sem(3, chunk, 0), sem(3, chunk, 1), 4 if along_x else 2)

    def third(source, owner, send, recv, half):
        target = 2 * kind + half
        return target, pltpu.make_async_remote_copy(
            src_ref=source.at[half, yy, xx], dst_ref=owner.at[low_z], send_sem=send, recv_sem=recv,
            device_id=(target * 8 + me % 8,), device_id_type=MESH)

    def start_third(source, owner, semaphore):
        for half in (0, 1):
            target, copy = third(source, owner, semaphore(4, half), semaphore(5, low_z), half)

            @pl.when(target != zz)
            def _():
                copy.start()

            @pl.when(target == zz)
            def _():
                owner[low_z] = source[half, yy, xx]

    def wait_third(source, owner, semaphore):
        for half in (0, 1):
            target, copy = third(source, owner, semaphore(4, half), semaphore(5, low_z), half)

            @pl.when(target != zz)
            def _():
                copy.wait_send()

        for origin in (0, 1):
            @pl.when(2 * origin + low_z != zz)
            def _():
                remote(source.at[0, yy, xx], owner.at[origin], semaphore(4, 0), semaphore(5, origin), 8).wait_recv()

    def run_first(pair):
        for odd in (0, 1):
            chunk = 2 * pair + odd
            to_core(chunk).wait()
            mine[chunk] = mine[chunk] + core_got[chunk]
            first(chunk, odd == 0).start()

    def run_second(pair):
        for odd in (0, 1):
            chunk = 2 * pair + odd
            first(chunk, odd == 0).wait()
            if odd == 0:
                mine[chunk, :, :, xx] = mine[chunk, :, :, xx] + first_got[chunk]
            else:
                mine[chunk, :, yy] = mine[chunk, :, yy] + first_got[chunk]
            second(chunk, odd == 0).start()

    def run_third(pair):
        for odd in (0, 1):
            chunk = 2 * pair + odd
            second(chunk, odd == 0).wait()
            mine[chunk, :, yy, xx] = mine[chunk, :, yy, xx] + second_got[chunk]
            start_third(mine.at[chunk], owner_got.at[chunk], functools.partial(chunk_sem, chunk))

    def run_last(pair):
        for odd in (0, 1):
            chunk = 2 * pair + odd
            wait_third(mine.at[chunk], owner_got.at[chunk], functools.partial(chunk_sem, chunk))
            summed[:, pl.ds(pl.multiple_of(chunk * CHUNK, 128), CHUNK)] = owner_got[chunk, 0] + owner_got[chunk, 1]

    def serve(run, low, high):
        def one(pair, carry):
            run(pair)
            return carry

        lax.fori_loop(low, high, one, 0)

    def terms(pair, slot, block):
        for part, row_half in ((0, core), (1, 1 - core)):
            left = turned[slot, row_half].reshape(8 * 48, both * slots)
            if block is None:
                right = mixed_low[...]
            else:
                right = wide[:, :, pl.ds(pl.multiple_of(block * width, 128), width)]
            got = dot(left, right.reshape(both * slots, width))
            for odd in (0, 1):
                piece = got[:, odd * CHUNK : odd * CHUNK + CHUNK].reshape(2, 2, 2, 48, CHUNK)
                if part == 0:
                    mine[2 * pair + odd] = piece
                else:
                    ring[pair % 2, odd] = piece
        for odd in (0, 1):
            to_core(2 * pair + odd).start()

    lanes = lax.broadcasted_iota(jnp.int32, (slots, 128), 1)

    def mask_of(place):
        return jnp.sum(jnp.where(lanes == place, masks[...], 0.0), axis=1, keepdims=True)

    def make_active_grad(first_row, which):
        low = grad_rows[first_row : first_row + 16].astype(bf16)
        for j in range(up_pairs):
            load_down(which, j).wait()
            active_grad[:, j * width : (j + 1) * width] = dot_nt(low, weights[1, :, j * width : (j + 1) * width])
        for copy in load_rest(which):
            copy.start()

    def upper_grad(j, place, count):
        at = pl.ds(pl.multiple_of(j * width, 128), width)
        load_slope(place, count, j).wait()

        def one(image, carry):
            row = active_grad[pl.ds(image, 1), at]
            weight = mask_of(place + image)
            for r in range(0, slots, ROWS):
                value = wide[image, r : r + ROWS, at].astype(f32) * (row * weight[r : r + ROWS])
                wide[image, r : r + ROWS, at] = value.astype(bf16)
            return carry

        lax.fori_loop(0, count, one, 0)

    make_active_grad(0, kind)
    all_turned(two_t, 0, finish)
    ones = jnp.full((128, both * slots), 1.0, bf16)

    def up_pair(j, carry):
        upper_grad(j, 0, both)
        right = wide[:, :, pl.ds(pl.multiple_of(j * width, 128), width)].reshape(both * slots, width)

        terms(j, 0, j)

        @pl.when(j >= 1)
        def _():
            run_first(j - 1)

        bias = dot(ones, right).T.reshape(4, 4, 48, 128)
        lane = lax.broadcasted_iota(jnp.int32, (4, 48, 128), 2)
        spread = jnp.zeros((4, 48, 128), f32)
        for k in range(4):
            spread = spread + jnp.where(lane == 4 + k, bias[:, k], 0.0)
        extra[j // 2, j % 2] = spread.reshape(2, 2, 48, 128)
        return carry

    lax.fori_loop(0, up_pairs, up_pair, 0)
    run_first(up_pairs - 1)
    sums[...] = jnp.zeros_like(sums)

    def hidden_two_back(count):
        def one(k, carry):
            flat = wide[0:count].reshape(count * slots, ff)
            at = pl.ds(pl.multiple_of(k * 256, 256), 256)
            mixed_grad[0:count, :, at] = dot_nt(flat, weights[0, at, :]).reshape(count, slots, 256)
            return carry

        lax.fori_loop(0, width // 256, one, 0)

    def fold(values):
        return jnp.sum(values.reshape(ROWS // 8, 8, width), axis=0)

    def norm_two_back(place, count, keep):
        def load(image):
            return pltpu.make_async_copy(mixed.at[place + image], rows_in.at[image % 2], rsem.at[image % 2])

        load(0).start()

        def one(image, carry):
            @pl.when(image + 1 < count)
            def _():
                load(image + 1).start()

            load(image).wait()
            weight = mask_of(place + image)
            grad_row = grad_rows[pl.ds(place + image, 1), :]
            for r in range(0, slots, ROWS):
                normed, inverse = row_norm(rows_in[image % 2, r : r + ROWS, :])
                grad = mixed_grad[image, r : r + ROWS, :]
                scaled = grad * gain_two[0 if keep else 1]
                back = inverse * (scaled - jnp.mean(scaled, axis=-1, keepdims=True) - normed * jnp.mean(scaled * normed, axis=-1, keepdims=True))
                value = weight[r : r + ROWS] * grad_row + back
                mixed_grad[image, r : r + ROWS, :] = value
                mixed_low[image, r : r + ROWS, :] = value.astype(bf16)
                if keep:
                    sums[2] = sums[2] + fold(grad * normed)
                    sums[3] = sums[3] + fold(grad)
            return carry

        lax.fori_loop(0, count, one, 0)

    def attended_back(count):
        for k in range(0, width, 256):
            flat = mixed_low[0:count].reshape(count * slots, width)
            got = dot_nt(flat, weights[1, k : k + 256, 3 * width : 4 * width])
            wide[0:count, :, 3 * width + k : 3 * width + k + 256] = got.astype(bf16).reshape(count, slots, 256)

    low_half = lax.broadcasted_iota(jnp.int32, (slots, 128), 1) < HEAD_DIM

    def attention_back(place, count):
        def load(image):
            return (pltpu.make_async_copy(packed.at[place + image], packs.at[image % 2], psem.at[0, image % 2]),
                    pltpu.make_async_copy(probs.at[place + image], shares.at[image % 2], psem.at[1, image % 2]))

        for copy in load(0):
            copy.start()

        def one(image, carry):
            @pl.when(image + 1 < count)
            def _():
                for copy in load(image + 1):
                    copy.start()

            for copy in load(image):
                copy.wait()
            now = image % 2
            for pair in range(HEADS // 2):
                at = slice(pair * 128, pair * 128 + 128)
                queries = packs[now, :, pair * 128 : pair * 128 + 128]
                keys = packs[now, :, width + pair * 128 : width + pair * 128 + 128]
                values = packs[now, :, 2 * width + pair * 128 : 2 * width + pair * 128 + 128]
                grad = wide[image, :, 3 * width + pair * 128 : 3 * width + pair * 128 + 128]
                share = shares[now, pair]
                blank = jnp.zeros_like(keys)
                two_keys = jnp.concatenate([jnp.where(low_half, keys, blank), jnp.where(low_half, blank, keys)])
                two_values = jnp.concatenate([jnp.where(low_half, values, blank), jnp.where(low_half, blank, values)])
                grad_share = dot_nt(two_values, grad)
                backs = []
                for side in (0, 1):
                    part = slice(side * slots, side * slots + slots)
                    weight = share[part].astype(f32)
                    product = weight * grad_share[part]
                    backs.append((product - weight * jnp.sum(product, axis=0, keepdims=True)).astype(bf16))
                back = jnp.concatenate(backs)
                grad_values = dot(share, grad)
                grad_keys = dot(back, queries) * head_scale
                grad_queries = dot_tn(back, two_keys) * head_scale
                wide[image, :, pair * 128 : pair * 128 + 128] = grad_queries.astype(bf16)
                wide[image, :, width + pair * 128 : width + pair * 128 + 128] = jnp.where(low_half, grad_keys[:slots], grad_keys[slots:]).astype(bf16)
                wide[image, :, 2 * width + pair * 128 : 2 * width + pair * 128 + 128] = jnp.where(low_half, grad_values[:slots], grad_values[slots:]).astype(bf16)
            return carry

        lax.fori_loop(0, count, one, 0)

    def norm_one_back(place, count, keep, out_place, out_count):
        def load(image):
            return (pltpu.make_async_copy(tokens.at[image], rows_in.at[image % 2], rsem.at[image % 2]),
                    pltpu.make_async_copy(foreign.at[image - own], rows_in.at[image % 2], rsem.at[image % 2]))

        def start_load(image):
            if not keep:
                pltpu.make_async_copy(tokens.at[own + image], rows_in.at[image % 2], rsem.at[image % 2]).start()
                return

            @pl.when(image < own)
            def _():
                pltpu.make_async_copy(tokens.at[image % own], rows_in.at[image % 2], rsem.at[image % 2]).start()

            @pl.when(image >= own)
            def _():
                pltpu.make_async_copy(foreign.at[image % own], rows_in.at[image % 2], rsem.at[image % 2]).start()

        def store(image):
            return pltpu.make_async_copy(rows_out.at[image % 2], tokens_out.at[out_place + image], osem.at[image % 2])

        start_load(0)

        def one(image, carry):
            @pl.when(image + 1 < count)
            def _():
                start_load(image + 1)

            pltpu.make_async_copy(tokens.at[0], rows_in.at[image % 2], rsem.at[image % 2]).wait()

            @pl.when((image >= 2) & (image - 2 < out_count))
            def _():
                store(image - 2).wait()

            hidden_grad[...] = dot_nt(wide[image, :, 0 : 3 * width], weights[1, :, 0 : 3 * width])
            for r in range(0, slots, ROWS):
                normed, inverse = row_norm(rows_in[image % 2, r : r + ROWS, :])
                grad = hidden_grad[r : r + ROWS, :]
                scaled = grad * gain_one[0 if keep else 1]
                back = inverse * (scaled - jnp.mean(scaled, axis=-1, keepdims=True) - normed * jnp.mean(scaled * normed, axis=-1, keepdims=True))
                rows_out[image % 2, r : r + ROWS, :] = mixed_grad[image, r : r + ROWS, :] + back
                if keep:
                    sums[0] = sums[0] + fold(grad * normed)
                    sums[1] = sums[1] + fold(grad)

            @pl.when(image < out_count)
            def _():
                store(image).start()

            return carry

        lax.fori_loop(0, count, one, 0)
        for image in range(max(count - 2, 0), count):
            if image < out_count:
                store(image).wait()

    load_up(kind).wait()
    hidden_two_back(both)
    load_up(1 - kind).start()
    all_turned(one_t, 0, begin)
    norm_two_back(0, both, True)
    all_turned(att_t, 1, finish)
    terms(up_pairs, 1, None)
    for copy in load_rest(kind):
        copy.wait()
    attended_back(both)
    run_first(up_pairs)
    serve(run_second, 0, 1)
    attention_back(0, both)
    all_turned(one_t, 0, finish)

    def qkv_pair(j, carry):
        terms(up_pairs + 1 + j, 0, j)
        run_second(j + 1)
        run_first(up_pairs + 1 + j)
        return carry

    lax.fori_loop(0, 3, qkv_pair, 0)
    serve(run_third, 0, 2)
    norm_one_back(0, both, True, 0, own)

    vectors = jnp.concatenate([jnp.sum(sums[k], axis=0, keepdims=True) for k in range(4)] + [jnp.zeros((124, width), f32)])
    extra[...] = extra[...] + vectors.T.reshape(extra.shape)
    extra_mine[...] = extra[:, :, :, core]
    extra_to_core = remote(extra.at[:, :, :, 1 - core], extra_core, extra_sems.at[1, 0], extra_sems.at[1, 1], 1)
    extra_first_copy = remote(extra_mine.at[:, :, 1 - xx], extra_first, extra_sems.at[2, 0], extra_sems.at[2, 1], 2)
    extra_second_copy = remote(extra_mine.at[:, 1 - yy, xx], extra_second, extra_sems.at[3, 0], extra_sems.at[3, 1], 4)
    extra_to_core.start()

    for j in range(up_pairs):
        load_slope(both, own, j).start()
        load_down(1 - kind, j).start()
    serve(run_third, 2, 3)
    serve(run_second, 4, 5)
    make_active_grad(both, 1 - kind)

    def other_pair(j, carry):
        upper_grad(j, both, own)
        return carry

    lax.fori_loop(0, up_pairs, other_pair, 0)
    extra_to_core.wait()
    extra_mine[...] = extra_mine[...] + extra_core[...]
    extra_first_copy.start()
    load_up(1 - kind).wait()
    hidden_two_back(own)
    norm_two_back(both, own, False)
    serve(run_third, 3, 4)
    serve(run_second, 5, 6)
    for copy in load_rest(1 - kind):
        copy.wait()
    attended_back(own)
    attention_back(both, own)
    serve(run_third, 4, 5)
    serve(run_second, 6, 7)
    extra_first_copy.wait()
    extra_mine[:, :, xx] = extra_mine[:, :, xx] + extra_first[...]
    extra_second_copy.start()
    norm_one_back(both, own, False, own, own)

    serve(run_second, 7, pairs)
    serve(run_third, 5, pairs)
    extra_second_copy.wait()
    extra_mine[:, yy, xx] = extra_mine[:, yy, xx] + extra_second[...]
    start_third(extra_mine, extra_owner, extra_sem)
    serve(run_last, 0, pairs)
    wait_third(extra_mine, extra_owner, extra_sem)
    extra_out[...] = extra_owner[0] + extra_owner[1]
    tail = [pltpu.make_async_copy(summed.at[:, pl.ds(0, ff)], up_out, wsem.at[0]),
            pltpu.make_async_copy(summed.at[:, pl.ds(ff, width)], out_out, wsem.at[1]),
            pltpu.make_async_copy(summed.at[:, pl.ds(ff + width, 3 * width)], qkv_out, wsem.at[2])]
    for copy in tail:
        copy.start()
    for copy in tail:
        copy.wait()


def backward(own, grad_rows, masks, tokens, foreign, saved, kind, weights):
    gain_one, shift_one, w_qkv, w_out, gain_two, shift_two, w_up, b_up, w_down = weights
    slots, width = tokens.shape[1:]
    ff = w_up.shape[2]
    both = 2 * own
    chunks = 2 * ff // CHUNK
    one_t, packed, probs, att_t, mixed, two_t, slope = saved
    split = lambda one: one.reshape(one.shape[0], 8, 2, one.shape[2], one.shape[3])
    anywhere, vmem = pl.BlockSpec(memory_space=pl.ANY), pl.BlockSpec(memory_space=pltpu.VMEM)
    gains = [jnp.where(kind == 1, one[::-1], one).reshape(2, 1, width) for one in (gain_one, gain_two)]
    return pl.pallas_call(
        functools.partial(backward_kernel, own),
        out_shape=(
            jax.ShapeDtypeStruct((48, ff), f32), jax.ShapeDtypeStruct((48, width), f32), jax.ShapeDtypeStruct((48, 3 * width), f32),
            jax.ShapeDtypeStruct((48, 128), f32), jax.ShapeDtypeStruct((both, slots, width), f32),
        ),
        in_specs=[vmem] * 4 + [anywhere] * 13,
        out_specs=(anywhere, anywhere, anywhere, vmem, anywhere),
        scratch_shapes=[
            pltpu.VMEM((chunks, 2, 2, 2, 48, CHUNK), f32),
            pltpu.VMEM((2, 2, 2, 2, 2, 48, CHUNK), f32),
            pltpu.VMEM((chunks, 2, 2, 2, 48, CHUNK), f32),
            pltpu.VMEM((chunks, 2, 2, 48, CHUNK), f32),
            pltpu.VMEM((chunks, 2, 48, CHUNK), f32),
            pltpu.VMEM((chunks, 2, 48, CHUNK), f32),
            pltpu.VMEM((48, 2 * ff), f32),
            pltpu.VMEM((2, 2, 2, 2, 48, 128), f32),
            pltpu.VMEM((2, 2, 2, 48, 128), f32),
            pltpu.VMEM((2, 2, 2, 48, 128), f32),
            pltpu.VMEM((2, 2, 48, 128), f32),
            pltpu.VMEM((2, 48, 128), f32),
            pltpu.VMEM((2, 48, 128), f32),
            pltpu.VMEM((both, slots, ff), bf16),
            pltpu.VMEM((both, slots, width), f32),
            pltpu.VMEM((both, slots, width), bf16),
            pltpu.VMEM((2, 2, 8, 48, both * slots), bf16),
            pltpu.VMEM((2, width, ff), bf16),
            pltpu.VMEM((16, ff), f32),
            pltpu.VMEM((4, 8, width), f32),
            pltpu.VMEM((2, slots, 3 * width), bf16),
            pltpu.VMEM((2, HEADS // 2, 2 * slots, slots), bf16),
            pltpu.VMEM((2, slots, width), f32),
            pltpu.VMEM((2, slots, width), f32),
            pltpu.VMEM((slots, width), f32),
            pltpu.SemaphoreType.DMA((6, chunks, 2)),
            pltpu.SemaphoreType.DMA((6, 2)),
            pltpu.SemaphoreType.DMA((7,)),
            pltpu.SemaphoreType.DMA((4,)),
            pltpu.SemaphoreType.DMA((2, 2, both)),
            pltpu.SemaphoreType.DMA((2, 2)),
            pltpu.SemaphoreType.DMA((2,)),
            pltpu.SemaphoreType.DMA((2,)),
        ],
        compiler_params=pltpu.CompilerParams(collective_id=1, has_side_effects=True, vmem_limit_bytes=63 << 20),
    )(grad_rows, masks, gains[0], gains[1], tokens, foreign, split(one_t), packed, probs, split(att_t), mixed, split(two_t), slope,
      w_qkv, w_out, w_up, w_down)


def tokens_of(patches, visible, modality):
    micro_count, images, _, patch_count, width = patches.shape
    cells = lax.dynamic_index_in_dim(patches, modality, 2, keepdims=False).reshape(micro_count * images, patch_count, width)
    picked = (visible[:, :, None] == jnp.arange(patch_count)[None, None, :]).astype(bf16)
    return jnp.einsum("isp,ipd->isd", picked, cells, preferred_element_type=f32)


def cells_of(grad_tokens, visible, patch_count):
    picked = (visible[:, None, :] == jnp.arange(patch_count)[None, :, None]).astype(f32)
    return jnp.einsum("ips,isd->ipd", picked, grad_tokens, precision=highest)


def on_tuned(patches, visible, valid_mask, weights):
    n = lax.axis_size("dp")
    me = lax.axis_index("dp")
    micro_count, images, _, patch_count, width = patches.shape
    own = micro_count * images
    slots = visible.shape[-1]
    ff = weights[6].shape[2]
    kind = (me // 8) % 2
    kinds = jnp.stack([kind, 1 - kind]).astype(jnp.int32)
    seen, mask = visible.reshape(own, slots), valid_mask.reshape(own, slots)
    tokens = pick_tokens(kinds, seen, patches.reshape(own, 2, patch_count, width))
    rows = slot_info(seen, mask)
    swap = [(i, i ^ 8) for i in range(n)]
    foreign = lax.ppermute(tokens[own:], "dp", swap)
    rows_there = lax.ppermute(rows, "dp", swap)
    marks, marks_there = group_marks(rows[:, 2], own), group_marks(rows_there[:, 2], own)
    twice = jnp.concatenate([rows, rows])
    results = encode_groups(kinds, jnp.asarray([0, 2], jnp.int32), None, tokens, twice, twice.transpose(0, 2, 1), jnp.concatenate([marks, marks]), weights, 3)
    active_sum, pooled = results[7:]
    counted = jnp.sum(rows[:, 2], axis=1)
    swapped = kind == 1
    pooled = jnp.where(swapped, pooled[::-1, :own], pooled[:, :own]).reshape(2 * own, width)
    shares = active_sum[:, :own] / counted[None, :, None]
    shares = jnp.where(swapped, shares[::-1], shares)
    down_rows = 2 * ff // n
    shares = shares.reshape(2, own, n // 2, down_rows).transpose(0, 2, 1, 3).reshape(n, own * down_rows)
    padded = jnp.pad(shares, ((0, 0), (0, 1024 - own * down_rows))).reshape(n, 8, 128)
    loss, grad_all, got = gather_and_contrast(n, micro_count, pooled, padded)
    got = got.reshape(n, 1024)[:, : own * down_rows]
    saved = encode_groups(kinds[:1], jnp.asarray([1], jnp.int32), results[:7], foreign, rows_there, rows_there.transpose(0, 2, 1), marks_there, weights, 3)[:7]
    grad_all = grad_all.reshape(n, 2, own, width)
    holder = me // (n // 2)
    grad_down = jnp.einsum(
        "iw,id->wd", got.reshape(n * own, down_rows),
        lax.dynamic_index_in_dim(grad_all, holder, 1, keepdims=False).reshape(n * own, width), precision=highest)
    mine = lax.dynamic_index_in_dim(grad_all, me, 0, keepdims=False)
    there = lax.dynamic_index_in_dim(grad_all, me ^ 8, 0, keepdims=False)
    counted_there = jnp.sum(rows_there[:, 2], axis=1)
    grad_rows = jnp.concatenate([
        lax.dynamic_index_in_dim(mine, kind, 0, keepdims=False) / counted[:, None],
        lax.dynamic_index_in_dim(there, kind, 0, keepdims=False) / counted_there[:, None],
        lax.dynamic_index_in_dim(mine, 1 - kind, 0, keepdims=False) / counted[:, None],
        jnp.zeros((24 - 3 * own, width), f32)])
    masks = jnp.concatenate([rows[:, 2], rows_there[:, 2], rows[:, 2], jnp.zeros((128 - 3 * own, slots), f32)]).T
    up, out, qkv, extra, grad_tokens = backward(own, grad_rows, masks, tokens, foreign, saved, kind, weights)
    patches_grad = place_cells(kinds, seen, grad_tokens, patch_count).reshape(patches.shape)
    return (loss[0, 0], patches_grad, extra[:, 0], extra[:, 1], qkv, out, extra[:, 2], extra[:, 3], up,
            extra[:, 4 : 4 + ff // width].T.reshape(-1), grad_down)


def on_plain(patches, visible, valid_mask, weights):
    n = lax.axis_size("dp")
    me = lax.axis_index("dp")
    micro_count, images, _, patch_count, width = patches.shape
    own = micro_count * images
    slots = visible.shape[-1]
    ff = weights[6].shape[2]
    seen = visible.reshape(own, slots)
    mask = valid_mask.reshape(own, slots)
    outcomes = []
    for modality in (0, 1):
        params = params_of(weights, modality)
        outcomes.append((params,) + encode_forward(tokens_of(patches, seen, modality), seen, mask, params))
    pooled = jnp.concatenate([pool(active, mixed, mask, params[8]) for params, active, mixed, _ in outcomes])
    counted = jnp.sum(mask.astype(f32), axis=1)[:, None]
    shares = jnp.stack([active / counted for _, active, _, _ in outcomes])
    down_rows = 2 * ff // n
    shares = shares.reshape(2, own, n // 2, down_rows).transpose(0, 2, 1, 3).reshape(n, own * down_rows)
    loss, grad_all = contrast(lax.all_gather(pooled, "dp", axis=0, tiled=True), 2 * own, micro_count)
    got = lax.all_to_all(shares, "dp", 0, 0, tiled=True)
    grad_all = grad_all.reshape(n, 2, own, width)
    grad_down = jnp.einsum(
        "iw,id->wd", got.reshape(n * own, down_rows),
        lax.dynamic_index_in_dim(grad_all, me // (n // 2), 1, keepdims=False).reshape(n * own, width), precision=highest)
    mine = lax.dynamic_index_in_dim(grad_all, me, 0, keepdims=False)
    backs = [encode_backward(mine[m], outcomes[m][3], mask, outcomes[m][0]) for m in (0, 1)]
    patches_grad = jnp.stack([cells_of(back[0], seen, patch_count) for back in backs], 1).reshape(patches.shape)
    joined = jax.tree.map(lambda a, b: jnp.concatenate([a, b]), backs[0][1], backs[1][1])
    shards = tuple(lax.psum_scatter(one, "dp", scatter_dimension=0, tiled=True) for one in joined)
    return (loss[0, 0], patches_grad) + shards + (grad_down,)


def solution(mesh):
    in_specs = (P(None, "dp"), P(None, "dp"), P(None, "dp")) + (P(),) * 9
    out_specs = (P(), P(None, "dp")) + (P("dp"),) * 9

    def on_device(patches, visible, valid_mask, *weights):
        run = on_tuned if lax.axis_size("dp") == 32 else on_plain
        return run(patches, visible, valid_mask, weights)

    return jax.shard_map(on_device, mesh=mesh, in_specs=in_specs, out_specs=out_specs, check_vma=False)
```

```python
import functools
import math

import jax
import jax.numpy as jnp
from jax import lax
from jax.experimental import pallas as pl
from jax.experimental.pallas import tpu as pltpu
from jax.sharding import PartitionSpec as P

HEADS = 12
HEAD_DIM = 64
GRID = 15
MESH = pl.DeviceIdType.MESH

norm_epsilon = 1e-06
unit_epsilon = 1e-06
logit_scale = 100.0
masked_score = -1e30
highest = lax.Precision.HIGHEST
head_scale = 1.0 / math.sqrt(HEAD_DIM)
f32 = jnp.float32
bf16 = jnp.bfloat16


def exact_gelu(values_in):
    return jax.nn.gelu(values_in, approximate=False)


def layer_norm(values_in, gain_vec, shift_vec):
    centre = values_in - jnp.mean(values_in, axis=-1, keepdims=True)
    inverse = lax.rsqrt(jnp.mean(centre * centre, axis=-1, keepdims=True) + norm_epsilon)
    normed = centre * inverse
    return (normed * gain_vec + shift_vec, normed, inverse)


def norm_back(grad_out, normed, inverse, gain_vec):
    grad_normed = grad_out * gain_vec
    mean_plain = jnp.mean(grad_normed, axis=-1, keepdims=True)
    mean_normed = jnp.mean(grad_normed * normed, axis=-1, keepdims=True)
    grad_in = inverse * (grad_normed - mean_plain - normed * mean_normed)
    return (grad_in, jnp.sum(grad_out * normed, axis=0), jnp.sum(grad_out, axis=0))


def alibi_bias(visible_rows):
    rows_pos = (visible_rows // GRID).astype(f32)
    cols_pos = (visible_rows % GRID).astype(f32)
    rows_gap = rows_pos[:, :, None] - rows_pos[:, None, :]
    cols_gap = cols_pos[:, :, None] - cols_pos[:, None, :]
    distance = jnp.sqrt(rows_gap * rows_gap + cols_gap * cols_gap)
    slopes = jnp.exp2(-8.0 * (jnp.arange(HEADS, dtype=f32) + 1.0) / HEADS)
    return -slopes[None, :, None, None] * distance[:, None, :, :]


def split_heads(packed):
    images, slot_count, _ = packed.shape
    shaped = packed.reshape(images, slot_count, 3, HEADS, HEAD_DIM)
    return (shaped[:, :, 0], shaped[:, :, 1], shaped[:, :, 2])


def encode_forward(tokens_in, visible_rows, mask_rows, params):
    gain_one, shift_one, w_qkv, w_out, gain_two, shift_two, w_up, b_up, w_down = params
    images, slots, width = tokens_in.shape
    flat_in = tokens_in.reshape(images * slots, width)
    hidden_one, normed_one, inverse_one = layer_norm(flat_in, gain_one, shift_one)
    hidden_one = hidden_one.astype(bf16)
    packed = jnp.dot(hidden_one, w_qkv, preferred_element_type=f32).astype(bf16)
    packed = packed.reshape(images, slots, 3 * width)
    queries, keys, values = split_heads(packed)
    scores = jnp.einsum("iqhd,ikhd->ihqk", queries, keys, preferred_element_type=f32)
    scores = scores * head_scale + alibi_bias(visible_rows)
    scores = jnp.where((mask_rows > 0)[:, None, None, :], scores, masked_score)
    attention = jax.nn.softmax(scores, axis=-1)
    attended = jnp.einsum("ihqk,ikhd->iqhd", attention.astype(bf16), values, preferred_element_type=f32)
    attended = attended.reshape(images * slots, width).astype(bf16)
    mixed = flat_in + jnp.dot(attended, w_out, preferred_element_type=f32)
    hidden_two, normed_two, inverse_two = layer_norm(mixed, gain_two, shift_two)
    hidden_two = hidden_two.astype(bf16)
    upper = jnp.dot(hidden_two, w_up, preferred_element_type=f32) + b_up
    active, gelu_back = jax.vjp(exact_gelu, upper)
    active = active.astype(bf16).astype(f32)
    weight = mask_rows.astype(f32)
    active_sum = jnp.sum(active.reshape(images, slots, -1) * weight[:, :, None], axis=1)
    mixed_sum = jnp.sum(mixed.reshape(images, slots, width) * weight[:, :, None], axis=1)
    saved = (normed_one, inverse_one, hidden_one, packed, attention, attended, normed_two, inverse_two, hidden_two, gelu_back)
    return active_sum, mixed_sum, saved


def pool(active_sum, mixed_sum, mask_rows, w_down):
    counted = jnp.sum(mask_rows.astype(f32), axis=1)[:, None]
    down = jnp.dot(active_sum, w_down.astype(f32), precision=highest)
    return (mixed_sum + down) / counted


def encode_backward(grad_pooled, saved, mask_rows, params):
    normed_one, inverse_one, hidden_one, packed, attention, attended, normed_two, inverse_two, hidden_two, gelu_back = saved
    gain_one, shift_one, w_qkv, w_out, gain_two, shift_two, w_up, b_up, w_down = params
    images, slots, three_width = packed.shape
    width = three_width // 3
    rows = images * slots
    weight = mask_rows.astype(f32)
    counted = jnp.sum(weight, axis=1)[:, None]
    grad_row = grad_pooled / counted
    grad_output = (weight[:, :, None] * grad_row[:, None, :]).reshape(rows, width)
    grad_active = jnp.dot(grad_row.astype(bf16), w_down.T, preferred_element_type=f32)
    grad_active = (weight[:, :, None] * grad_active[:, None, :]).reshape(rows, -1)
    grad_upper = gelu_back(grad_active)[0].astype(bf16)
    grad_bias = jnp.sum(grad_upper.astype(f32), axis=0)
    grad_up = jnp.dot(hidden_two.T, grad_upper, preferred_element_type=f32)
    grad_hidden_two = jnp.dot(grad_upper, w_up.T, preferred_element_type=f32)
    grad_norm_two, grad_gain_two, grad_shift_two = norm_back(grad_hidden_two, normed_two, inverse_two, gain_two)
    grad_mixed = grad_output + grad_norm_two
    grad_mixed_low = grad_mixed.astype(bf16)
    grad_out = jnp.dot(attended.T, grad_mixed_low, preferred_element_type=f32)
    grad_attended = jnp.dot(grad_mixed_low, w_out.T, preferred_element_type=f32).astype(bf16)
    grad_attended = grad_attended.reshape(images, slots, HEADS, HEAD_DIM)
    queries, keys, values = split_heads(packed)
    grad_value = jnp.einsum("ihqk,iqhd->ikhd", attention.astype(bf16), grad_attended, preferred_element_type=f32)
    grad_attention = jnp.einsum("iqhd,ikhd->ihqk", grad_attended, values, preferred_element_type=f32)
    grad_scores = attention * (grad_attention - jnp.sum(attention * grad_attention, axis=-1, keepdims=True))
    grad_scores = grad_scores.astype(bf16)
    grad_query = jnp.einsum("ihqk,ikhd->iqhd", grad_scores, keys, preferred_element_type=f32) * head_scale
    grad_key = jnp.einsum("ihqk,iqhd->ikhd", grad_scores, queries, preferred_element_type=f32) * head_scale
    grad_packed = jnp.stack([grad_query, grad_key, grad_value], axis=2).astype(bf16).reshape(rows, three_width)
    grad_qkv = jnp.dot(hidden_one.T, grad_packed, preferred_element_type=f32)
    grad_hidden_one = jnp.dot(grad_packed, w_qkv.T, preferred_element_type=f32)
    grad_norm_one, grad_gain_one, grad_shift_one = norm_back(grad_hidden_one, normed_one, inverse_one, gain_one)
    grad_tokens = (grad_mixed + grad_norm_one).reshape(images, slots, width)
    return grad_tokens, (grad_gain_one, grad_shift_one, grad_qkv, grad_out, grad_gain_two, grad_shift_two, grad_up, grad_bias)


def contrast(pooled, own_rows, micro_count):
    count = pooled.shape[0]
    images = own_rows // (2 * micro_count)
    inverse = lax.rsqrt(jnp.sum(pooled * pooled, axis=-1, keepdims=True) + unit_epsilon)
    unit = pooled * inverse
    logits = logit_scale * lax.dot_general(unit, unit, (((1,), (1,)), ((), ())), precision=highest, preferred_element_type=f32)
    row = lax.broadcasted_iota(jnp.int32, (count, count), 0)
    col = lax.broadcasted_iota(jnp.int32, (count, count), 1)
    half = own_rows // 2
    row_mod, col_mod = (row // half) % 2, (col // half) % 2
    row_micro, col_micro = (row // images) % micro_count, (col // images) % micro_count
    allowed = (row_mod != col_mod) & (row_micro == col_micro)
    paired = jnp.where(col == row + half * (1 - 2 * row_mod), 1.0, 0.0)
    logits = jnp.where(allowed, logits, masked_score)
    row_max = jnp.max(logits, axis=1, keepdims=True)
    row_lse = row_max + jnp.log(jnp.sum(jnp.exp(logits - row_max), axis=1, keepdims=True))
    col_max = jnp.max(logits, axis=0, keepdims=True)
    col_lse = col_max + jnp.log(jnp.sum(jnp.exp(logits - col_max), axis=0, keepdims=True))
    scale = 1.0 / count
    diagonal = jnp.sum(jnp.where(paired > 0, logits, 0.0), axis=1, keepdims=True)
    loss = scale * jnp.sum(row_lse - diagonal, axis=0, keepdims=True)
    spread = jnp.exp(logits - row_lse) + jnp.exp(logits - col_lse) - 2.0 * paired
    grad_unit = (logit_scale * scale) * jnp.dot(spread, unit, precision=highest, preferred_element_type=f32)
    grad_pooled = inverse * (grad_unit - unit * jnp.sum(unit * grad_unit, axis=-1, keepdims=True))
    return loss, grad_pooled


def params_of(weights, modality):
    return tuple(lax.dynamic_index_in_dim(one, modality, 0, keepdims=False) for one in weights)


GROWS = 32
SLOPES = [2.0 ** (-8.0 * (head + 1) / HEADS) for head in range(HEADS)]
ROWS = 32
WIDE = 256


def gelu_pair(upper):
    size = jnp.abs(upper)
    bell = jnp.exp(-0.5 * upper * upper)
    below = 1.0 + (0.3275911 * math.sqrt(0.5)) * size
    t = pltpu.reciprocal(below, approx=True)
    t = t * (2.0 - below * t)
    tail = t * (0.5 * 0.254829592 + t * (0.5 * -0.284496736 + t * (0.5 * 1.421413741 + t * (0.5 * -1.453152027 + t * (0.5 * 1.061405429)))))
    tail = tail * bell
    normal = jnp.where(upper < 0, tail, 1.0 - tail)
    return upper * normal, normal + upper * (bell * (1.0 / math.sqrt(2.0 * math.pi)))


def row_norm(values):
    centre = values - jnp.mean(values, axis=-1, keepdims=True)
    inverse = lax.rsqrt(jnp.mean(centre * centre, axis=-1, keepdims=True) + norm_epsilon)
    return centre * inverse, inverse


def dot(a, b):
    return jnp.dot(a, b, preferred_element_type=f32)


def dot_nt(a, b):
    return lax.dot_general(a, b, (((1,), (1,)), ((), ())), preferred_element_type=f32)


def dot_tn(a, b):
    return lax.dot_general(a, b, (((0,), (0,)), ((), ())), preferred_element_type=f32)


def roll_if(flag, value):
    return jnp.where(flag == 1, jnp.concatenate([value[4:], value[:4]]), value)


def forward_kernel(n, micro_count, info_in, gain_one, shift_one, gain_two, shift_two, b_up, patches, w_qkv, w_out, w_up, w_down,
                   loss_out, grad_out, got, grad_rows, active_grad, masks, tokens_out, one_out, packed_out, probs_out, att_out, mixed_out, two_out, slope_out,
                   cells, tok, there, wq, wo, wu, wd, one_t, packed, probs, att_t, mixed, two_t, slope, upper, active, hidden, attended, turned,
                   active_sum, share, every, send_sem, recv_sem, sum_send, sum_recv, isem, wsem, osem, tsem, xsem):
    me = lax.axis_index("dp")
    kind = (me // 8) % 2
    images, slots, width = info_in.shape[0], info_in.shape[2], tok.shape[2]
    rows = images * slots
    ff = wu.shape[2]

    read_cells = pltpu.make_async_copy(patches, cells, isem)
    read_cells.start()
    reads = []
    for slot, which in ((0, kind), (1, 1 - kind)):
        reads.append([pltpu.make_async_copy(source.at[which], target.at[slot], wsem.at[slot, number])
                      for number, (source, target) in enumerate(((w_qkv, wq), (w_out, wo), (w_up, wu), (w_down, wd)))])
    for copy in reads[0] + reads[1]:
        copy.start()
    barrier = pltpu.get_barrier_semaphore()

    def greet(step, carry):
        pl.semaphore_signal(barrier, inc=1, device_id=(lax.rem(me + step, n),), device_id_type=MESH)
        return carry

    lax.fori_loop(1, n, greet, 0)
    read_cells.wait()

    def pick(modality, place):
        def one(image, carry):
            seen = info_in[image, 3:4, :]
            picked = jnp.where(lax.broadcasted_iota(jnp.int32, (cells.shape[2], slots), 0).astype(f32) == seen, 1.0, 0.0).astype(bf16)
            tok[place + image] = dot_tn(picked, cells[image, modality])
            return carry

        lax.fori_loop(0, images, one, 0)

    pick(1 - kind, 2 * images)
    pl.semaphore_wait(barrier, n - 1)
    send_tokens = [
        pltpu.make_async_remote_copy(src_ref=info_in, dst_ref=there, send_sem=xsem.at[0, 0], recv_sem=xsem.at[0, 1], device_id=(me ^ 8,), device_id_type=MESH),
        pltpu.make_async_remote_copy(src_ref=tok.at[pl.ds(2 * images, images)], dst_ref=tok.at[pl.ds(images, images)],
                                     send_sem=xsem.at[1, 0], recv_sem=xsem.at[1, 1], device_id=(me ^ 8,), device_id_type=MESH)]
    for copy in send_tokens:
        copy.start()
    pick(kind, 0)

    def store_tokens(place):
        at = pl.ds(place * images, images)
        return pltpu.make_async_copy(tok.at[at], tokens_out.at[at], tsem.at[place])

    store_tokens(0).start()
    store_tokens(2).start()

    stores = {}

    def ready(number):
        if number in stores:
            stores.pop(number).wait()

    def store(number, place):
        source, target = ((one_t, one_out), (packed, packed_out), (probs, probs_out), (att_t, att_out), (mixed, mixed_out), (two_t, two_out), (slope, slope_out))[number]
        copy = pltpu.make_async_copy(source, target.at[pl.ds(place * images, images)], osem.at[number])
        copy.start()
        stores[number] = copy

    low_half = lax.broadcasted_iota(jnp.int32, (slots, 128), 1) < HEAD_DIM
    row_of = lax.broadcasted_iota(jnp.int32, (8, slots), 0)

    def marks_of(info):
        return jnp.concatenate([jnp.where(row_of == image, info[image, 2:3, :], 0.0) for image in range(images)], axis=1).astype(bf16)

    def group(place, slot, which, info, whole, pauses):
        gain1, shift1 = gain_one[pl.ds(which, 1), :], shift_one[pl.ds(which, 1), :]
        gain2, shift2 = gain_two[pl.ds(which, 1), :], shift_two[pl.ds(which, 1), :]

        def norm(source, first, target, gain, shift):
            def one(image, carry):
                for r in range(0, slots, ROWS):
                    normed, _ = row_norm(source[first + image, r : r + ROWS, :])
                    hidden[image, r : r + ROWS, :] = (normed * gain + shift).astype(bf16)
                target[image] = hidden[image].T.reshape(target.shape[1:])
                return carry

            lax.fori_loop(0, images, one, 0)

        ready(0)
        norm(tok, place * images, one_t, gain1, shift1)
        store(0, place)
        ready(1)
        if pauses is None:
            reads[slot][0].wait()

        def project(i, carry):
            at = pl.ds(pl.multiple_of(i * 768, 768), 768)
            packed[:, :, at] = dot(hidden[...].reshape(rows, width), wq[slot, :, at]).astype(bf16).reshape(images, slots, 768)
            return carry

        lax.fori_loop(0, 3 * width // 768, project, 0)
        store(1, place)
        if pauses:
            pauses[0]()
        ready(2)
        ready(3)

        def attend(image, carry):
            line = info[image]
            column = line.T
            gap_r = column[:, 0:1] - line[0:1, :]
            gap_c = column[:, 1:2] - line[1:2, :]
            away = -jnp.sqrt(gap_r * gap_r + gap_c * gap_c)
            away = jnp.where(column[:, 2:3] > 0, away, -1e33)
            for pair in range(HEADS // 2):
                at = slice(pair * 128, pair * 128 + 128)
                queries = packed[image, :, pair * 128 : pair * 128 + 128]
                keys = packed[image, :, width + pair * 128 : width + pair * 128 + 128]
                values = packed[image, :, 2 * width + pair * 128 : 2 * width + pair * 128 + 128]
                blank = jnp.zeros_like(keys)
                two_keys = jnp.concatenate([jnp.where(low_half, keys, blank), jnp.where(low_half, blank, keys)])
                two_values = jnp.concatenate([jnp.where(low_half, values, blank), jnp.where(low_half, blank, values)])
                scores = dot_nt(two_keys, queries)
                shares = []
                for side in (0, 1):
                    one = scores[side * slots : side * slots + slots] * head_scale + SLOPES[2 * pair + side] * away
                    power = jnp.exp(one - jnp.max(one, axis=0, keepdims=True))
                    shares.append((power * (1.0 / jnp.sum(power, axis=0, keepdims=True))).astype(bf16))
                both_shares = jnp.concatenate(shares)
                probs[image, pair] = both_shares
                flipped = dot_tn(two_values, both_shares).astype(bf16)
                turned[at, :] = flipped
                attended[image, :, at] = flipped.T
            att_t[image] = turned[...].reshape(att_t.shape[1:])
            return carry

        lax.fori_loop(0, images, attend, 0)
        store(2, place)
        store(3, place)
        if pauses:
            pauses[1]()
        ready(4)
        if pauses is None:
            reads[slot][1].wait()

        def output(i, carry):
            at = pl.ds(pl.multiple_of(i * 256, 256), 256)
            mixed[:, :, at] = tok[pl.ds(place * images, images), :, at] + dot(attended[...].reshape(rows, width), wo[slot, :, at]).reshape(images, slots, 256)
            return carry

        lax.fori_loop(0, width // 256, output, 0)
        store(4, place)
        ready(5)
        norm(mixed, 0, two_t, gain2, shift2)
        store(5, place)
        if pauses:
            pauses[2]()
        ready(6)
        if pauses is None:
            reads[slot][2].wait()
        marks = marks_of(info)

        def columns(i):
            return pl.ds(pl.multiple_of(i * WIDE, WIDE), WIDE)

        def rise(i, slot_up):
            upper[slot_up] = dot(hidden[...].reshape(rows, width), wu[slot, :, columns(i)])

        def bend(i, now):
            bias = b_up[pl.ds(which, 1), columns(i)]
            for r in range(0, rows, GROWS):
                value, back = gelu_pair(upper[now, r : r + GROWS, :] + bias)
                if whole:
                    active[r : r + GROWS, :] = value.astype(bf16)
                slope[r // slots, r % slots : r % slots + GROWS, columns(i)] = back.astype(bf16)
            if whole:
                active_sum[slot, :, columns(i)] = dot(marks, active[...])

        rise(0, 0)

        def feed(i, carry):
            rise(2 * i + 1, 1)
            bend(2 * i, 0)
            rise(2 * i + 2, 0)
            bend(2 * i + 1, 1)
            return carry

        steps = ff // WIDE
        lax.fori_loop(0, steps // 2 - 1, feed, 0)
        rise(steps - 1, 1)
        bend(steps - 2, 0)
        bend(steps - 1, 1)
        store(6, place)
        if not whole:
            return None
        reads[slot][3].wait()
        total = active_sum[slot]
        high = total.astype(bf16)
        rest = total - high.astype(f32)
        middle = rest.astype(bf16)
        lowest = (rest - middle.astype(f32)).astype(bf16)
        stacked = jnp.concatenate([high, middle, lowest, jnp.zeros_like(high)])
        parts = dot(stacked, wd[slot])
        downs = parts[0:8] + parts[8:16] + parts[16:24]
        sums, counts = [], []
        for image in range(images):
            weight = info[image].T[:, 2:3]
            sums.append(jnp.sum(mixed[image] * weight, axis=0, keepdims=True))
            counts.append(jnp.sum(weight, axis=0, keepdims=True))
        count = jnp.concatenate(counts + [jnp.ones((8 - images, 1), f32)])
        pooled = (jnp.concatenate(sums + [jnp.zeros((8 - images, width), f32)]) + downs) / count
        share[which] = roll_if(which, total / count)
        return roll_if(which, pooled)

    def copies(sources, flip, first):
        made = []
        for number, source in enumerate(sources):
            made.append(pltpu.make_async_remote_copy(
                src_ref=every.at[source], dst_ref=every.at[source], send_sem=send_sem.at[first + number], recv_sem=recv_sem.at[first + number],
                device_id=(me ^ flip,), device_id_type=MESH))
        for copy in made:
            copy.start()
        return made

    def finish(made):
        for copy in made:
            copy.wait()

    pooled = group(0, 0, kind, info_in, True, None)
    every[me] = pooled + group(2, 1, 1 - kind, info_in, True, None)

    waves = [copies([me], flip, number) [0] for number, flip in enumerate((8, 16, 24))]
    held = [me, me ^ 8, me ^ 16, me ^ 24]
    state = {"wave": waves, "held": held}

    def next_wave(flip, first):
        def run():
            finish(state["wave"])
            state["wave"] = copies(state["held"], flip, first)
            state["held"] = state["held"] + [one ^ flip for one in state["held"]]
        return run

    def sums_out(step, carry):
        peer = lax.rem(me + step, n)
        at = pl.ds(pl.multiple_of(((peer % (n // 2)) // 2) * 384, 384), 384)
        pltpu.make_async_remote_copy(
            src_ref=share.at[peer // (n // 2), :, at], dst_ref=got.at[me], send_sem=sum_send.at[step], recv_sem=sum_recv.at[step],
            device_id=(peer,), device_id_type=MESH).start()
        return carry

    def last_wave():
        next_wave(1, 15)()
        lax.fori_loop(1, n, sums_out, 0)

    send_tokens[0].wait()
    send_tokens[1].wait()
    store_tokens(1).start()
    group(1, 0, kind, there, False, [next_wave(4, 3), next_wave(2, 7), last_wave])
    finish(state["wave"])
    loss, grad = contrast(every[...].reshape(n * 8, width), 8, micro_count)
    loss_out[...] = jnp.broadcast_to(loss, loss_out.shape)
    grad_out[...] = grad
    got[me] = share[me // (n // 2), :, pl.ds(pl.multiple_of(((me % (n // 2)) // 2) * 384, 384), 384)]

    def per_slot(device, which, info):
        count = jnp.concatenate([jnp.sum(info[image, 2:3, :], axis=1, keepdims=True) for image in range(images)])
        return roll_if(which, grad_out[pl.ds(pl.multiple_of(device * 8, 8), 8), :])[0:images] / count

    spread = jnp.concatenate([per_slot(me, kind, info_in), per_slot(me ^ 8, kind, there), per_slot(me, 1 - kind, info_in), jnp.zeros((24 - 3 * images, width), f32)])
    grad_rows[...] = spread
    low = spread[0:16].astype(bf16)
    for j in range(0, ff, width):
        active_grad[:, j : j + width] = dot_nt(low, wd[0, j : j + width, :])
    lines = [info[image, 2:3, :] for info in (info_in, there, info_in) for image in range(images)]
    masks[...] = jnp.concatenate(lines + [jnp.zeros((slots - 3 * images, slots), f32)]).T

    def sums_in(step, carry):
        peer = lax.rem(me + n - step, n)
        pltpu.make_async_remote_copy(
            src_ref=share.at[0, :, pl.ds(0, 384)], dst_ref=got.at[peer], send_sem=sum_send.at[step], recv_sem=sum_recv.at[step],
            device_id=(peer,), device_id_type=MESH).wait()
        return carry

    lax.fori_loop(1, n, sums_in, 0)
    for number in range(7):
        ready(number)
    for place in range(3):
        store_tokens(place).wait()


def forward(n, micro_count, info, patches, weights):
    gain_one, shift_one, w_qkv, w_out, gain_two, shift_two, w_up, b_up, w_down = weights
    images, _, slots = info.shape
    width, ff = w_up.shape[1:]
    anywhere, vmem = pl.BlockSpec(memory_space=pl.ANY), pl.BlockSpec(memory_space=pltpu.VMEM)
    turned = (16, width // 16, slots)
    kept = [(turned, bf16), ((slots, 3 * width), bf16), ((HEADS // 2, 2 * slots, slots), bf16), (turned, bf16), ((slots, width), f32),
            (turned, bf16), ((slots, ff), bf16)]
    return pl.pallas_call(
        functools.partial(forward_kernel, n, micro_count),
        out_shape=[jax.ShapeDtypeStruct(shape, f32) for shape in
                   ((8, 128), (8 * n, width), (n, 8, 384), (24, width), (16, ff), (slots, slots), (3 * images, slots, width))]
        + [jax.ShapeDtypeStruct((3 * images,) + dims, dtype) for dims, dtype in kept],
        in_specs=[vmem] * 6 + [anywhere] * 5,
        out_specs=[vmem] * 6 + [anywhere] * 8,
        scratch_shapes=[
            pltpu.VMEM(patches.shape, bf16),
            pltpu.VMEM((3 * images, slots, width), f32),
            pltpu.VMEM(info.shape, f32),
            pltpu.VMEM(w_qkv.shape, bf16), pltpu.VMEM(w_out.shape, bf16), pltpu.VMEM(w_up.shape, bf16), pltpu.VMEM(w_down.shape, bf16)]
        + [pltpu.VMEM((images,) + dims, dtype) for dims, dtype in kept]
        + [
            pltpu.VMEM((2, images * slots, WIDE), f32),
            pltpu.VMEM((images * slots, WIDE), bf16),
            pltpu.VMEM((images, slots, width), bf16),
            pltpu.VMEM((images, slots, width), bf16),
            pltpu.VMEM((width, slots), bf16),
            pltpu.VMEM((2, 8, ff), f32),
            pltpu.VMEM((2, 8, ff), f32),
            pltpu.VMEM((n, 8, width), f32),
            pltpu.SemaphoreType.DMA((31,)),
            pltpu.SemaphoreType.DMA((31,)),
            pltpu.SemaphoreType.DMA((n,)),
            pltpu.SemaphoreType.DMA((n,)),
            pltpu.SemaphoreType.DMA,
            pltpu.SemaphoreType.DMA((2, 4)),
            pltpu.SemaphoreType.DMA((7,)),
            pltpu.SemaphoreType.DMA((3,)),
            pltpu.SemaphoreType.DMA((2, 2)),
        ],
        compiler_params=pltpu.CompilerParams(collective_id=0, has_side_effects=True, vmem_limit_bytes=63 << 20),
    )(info, gain_one, shift_one, gain_two, shift_two, b_up, patches, w_qkv, w_out, w_up, w_down)


def slot_info(seen, mask):
    rows = jnp.stack([(seen // GRID).astype(f32), (seen % GRID).astype(f32), mask.astype(f32), seen.astype(f32)], axis=1)
    return jnp.pad(rows, ((0, 0), (0, 4), (0, 0)))


CHUNK = 384


def meet(peers):
    barrier = pltpu.get_barrier_semaphore()
    for peer in peers:
        pl.semaphore_signal(barrier, inc=1, device_id=(peer,), device_id_type=MESH)
    pl.semaphore_wait(barrier, len(peers))


def cells_kernel(kinds, seen, grads, out):
    patch_count = out.shape[2]
    slots = seen.shape[2]
    picked = jnp.where(lax.broadcasted_iota(jnp.int32, (patch_count, slots), 0) == seen[0], 1.0, 0.0).astype(bf16)
    value = grads[0]
    high = value.astype(bf16)
    rest = value - high.astype(f32)
    middle = rest.astype(bf16)
    lowest = (rest - middle.astype(f32)).astype(bf16)
    out[0, 0] = dot(picked, high) + dot(picked, middle) + dot(picked, lowest)


def place_cells(kinds, seen, grads, patch_count):
    total, slots, width = grads.shape
    images = total // 2
    return pl.pallas_call(
        cells_kernel,
        grid_spec=pltpu.PrefetchScalarGridSpec(
            num_scalar_prefetch=1,
            grid=(2, images),
            in_specs=[pl.BlockSpec((1, 1, slots), lambda g, i, kinds: (i, 0, 0)),
                      pl.BlockSpec((1, slots, width), lambda g, i, kinds: (g * images + i, 0, 0))],
            out_specs=pl.BlockSpec((1, 1, patch_count, width), lambda g, i, kinds: (i, kinds[g], 0, 0)),
        ),
        out_shape=jax.ShapeDtypeStruct((images, 2, patch_count, width), f32),
        cost_estimate=pl.CostEstimate(flops=12 * images * slots * 256 * width, bytes_accessed=8 << 20, transcendentals=0),
    )(kinds, seen.reshape(images, 1, slots), grads)


def backward_kernel(own, grad_rows, first_active, masks, gain_one, gain_two, got, grad_all, tokens, one_t, packed, probs, att_t, mixed, two_t, slope,
                    w_qkv, w_out, w_up, w_down,
                    up_out, out_out, qkv_out, extra_out, tokens_out, down_out,
                    mine, ring, core_got, first_got, second_got, owner_got,
                    extra, extra_mine, extra_core, extra_first, extra_second, extra_owner,
                    wide, mixed_grad, mixed_low, turned, weights, active_grad, sums, packs, shares, rows_in, rows_out, hidden_grad,
                    sems, extra_sems, wsem, dsem, tsem, psem, rsem, osem):
    me = lax.axis_index("dp")
    core, xx, yy, zz = me % 2, (me // 2) % 2, (me // 4) % 2, me // 8
    kind, low_z = zz % 2, zz // 2
    slots, width = mixed.shape[1:]
    ff = slope.shape[2]
    both = 2 * own
    pairs = 2 * ff // width
    up_pairs = ff // width

    def load_slope(place, count, j):
        at = pl.ds(pl.multiple_of(j * width, 128), width)
        return pltpu.make_async_copy(slope.at[pl.ds(place, count), :, at], wide.at[pl.ds(0, count), :, at], dsem.at[j])

    def load_down(which, j):
        at = pl.ds(pl.multiple_of(j * width, 128), width)
        return pltpu.make_async_copy(w_down.at[which, at, :], weights.at[1, :, at], wsem.at[j])

    def load_up(which):
        return pltpu.make_async_copy(w_up.at[which], weights.at[0], wsem.at[4])

    def load_rest(which):
        return (pltpu.make_async_copy(w_qkv.at[which], weights.at[1, :, pl.ds(0, 3 * width)], wsem.at[5]),
                pltpu.make_async_copy(w_out.at[which], weights.at[1, :, pl.ds(3 * width, width)], wsem.at[6]))

    def load_turned(source, slot, image, part):
        return pltpu.make_async_copy(
            source.at[image, :, part], turned.at[slot, part, :, :, pl.ds(pl.multiple_of(image * slots, 128), slots)], tsem.at[slot, part, image])

    def all_turned(source, slot, act):
        def one(image, carry):
            for part in (0, 1):
                act(load_turned(source, slot, image, part))
            return carry

        lax.fori_loop(0, both, one, 0)

    def begin(copy):
        copy.start()

    def finish(copy):
        copy.wait()

    load_slope(0, both, 0).start()
    all_turned(two_t, 0, begin)
    for j in range(1, up_pairs):
        load_slope(0, both, j).start()
    load_up(kind).start()
    all_turned(att_t, 1, begin)
    for copy in load_rest(kind):
        copy.start()

    meet([me ^ 1, me ^ 2, me ^ 4, me ^ 8, me ^ 16, me ^ 24])

    def sem(stage, chunk, way):
        return sems.at[stage, chunk, way]

    def chunk_sem(chunk, stage, way):
        return sems.at[stage, chunk, way]

    def extra_sem(stage, way):
        return extra_sems.at[stage, way]

    def remote(src, dst, send, recv, flip):
        return pltpu.make_async_remote_copy(src_ref=src, dst_ref=dst, send_sem=send, recv_sem=recv, device_id=(me ^ flip,), device_id_type=MESH)

    def to_core(chunk):
        return remote(ring.at[(chunk // 2) % 2, chunk % 2], core_got.at[chunk], sem(1, chunk, 0), sem(1, chunk, 1), 1)

    def first(chunk, along_x):
        src = mine.at[chunk, :, :, 1 - xx] if along_x else mine.at[chunk, :, 1 - yy]
        return remote(src, first_got.at[chunk], sem(2, chunk, 0), sem(2, chunk, 1), 2 if along_x else 4)

    def second(chunk, along_x):
        src = mine.at[chunk, :, 1 - yy, xx] if along_x else mine.at[chunk, :, yy, 1 - xx]
        return remote(src, second_got.at[chunk], sem(3, chunk, 0), sem(3, chunk, 1), 4 if along_x else 2)

    def third(source, owner, send, recv, half):
        target = 2 * kind + half
        return target, pltpu.make_async_remote_copy(
            src_ref=source.at[half, yy, xx], dst_ref=owner.at[low_z], send_sem=send, recv_sem=recv,
            device_id=(target * 8 + me % 8,), device_id_type=MESH)

    def start_third(source, owner, semaphore):
        for half in (0, 1):
            target, copy = third(source, owner, semaphore(4, half), semaphore(5, low_z), half)

            @pl.when(target != zz)
            def _():
                copy.start()

            @pl.when(target == zz)
            def _():
                owner[low_z] = source[half, yy, xx]

    def wait_third(source, owner, semaphore):
        for half in (0, 1):
            target, copy = third(source, owner, semaphore(4, half), semaphore(5, low_z), half)

            @pl.when(target != zz)
            def _():
                copy.wait_send()

        for origin in (0, 1):
            @pl.when(2 * origin + low_z != zz)
            def _():
                remote(source.at[0, yy, xx], owner.at[origin], semaphore(4, 0), semaphore(5, origin), 8).wait_recv()

    def run_first(pair):
        for odd in (0, 1):
            chunk = 2 * pair + odd
            to_core(chunk).wait_recv()
            mine[chunk] = mine[chunk] + core_got[chunk]
            first(chunk, odd == 0).start()

    def run_second(pair):
        for odd in (0, 1):
            chunk = 2 * pair + odd
            first(chunk, odd == 0).wait()
            if odd == 0:
                mine[chunk, :, :, xx] = mine[chunk, :, :, xx] + first_got[chunk]
            else:
                mine[chunk, :, yy] = mine[chunk, :, yy] + first_got[chunk]
            second(chunk, odd == 0).start()

    def run_third(pair):
        for odd in (0, 1):
            chunk = 2 * pair + odd
            second(chunk, odd == 0).wait()
            mine[chunk, :, yy, xx] = mine[chunk, :, yy, xx] + second_got[chunk]
            start_third(mine.at[chunk], owner_got.at[chunk], functools.partial(chunk_sem, chunk))

    def write(chunk, target, base):
        at = pl.ds(pl.multiple_of((chunk - 2 * base) * CHUNK, 128), CHUNK)
        return pltpu.make_async_copy(owner_got.at[chunk, 0], target.at[:, at], sem(0, chunk, 0))

    outputs = ((up_out, 0, up_pairs), (out_out, up_pairs, up_pairs + 1), (qkv_out, up_pairs + 1, pairs))

    def run_last(target, base, pair):
        for odd in (0, 1):
            chunk = 2 * pair + odd
            wait_third(mine.at[chunk], owner_got.at[chunk], functools.partial(chunk_sem, chunk))
            owner_got[chunk, 0] = owner_got[chunk, 0] + owner_got[chunk, 1]
            write(chunk, target, base).start()

    def serve(run, low, high):
        def one(pair, carry):
            run(pair)
            return carry

        lax.fori_loop(low, high, one, 0)

    def terms(pair, slot, block, reused=True):
        if reused:
            for odd in (0, 1):
                to_core(2 * (pair - 2) + odd).wait_send()
        for part, row_half in ((0, core), (1, 1 - core)):
            left = turned[slot, row_half].reshape(8 * 48, both * slots)
            if block is None:
                right = mixed_low[...]
            else:
                right = wide[:, :, pl.ds(pl.multiple_of(block * width, 128), width)]
            got = dot(left, right.reshape(both * slots, width))
            for odd in (0, 1):
                piece = got[:, odd * CHUNK : odd * CHUNK + CHUNK].reshape(2, 2, 2, 48, CHUNK)
                if part == 0:
                    mine[2 * pair + odd] = piece
                else:
                    ring[pair % 2, odd] = piece
        for odd in (0, 1):
            to_core(2 * pair + odd).start()

    lanes = lax.broadcasted_iota(jnp.int32, (slots, 128), 1)

    def mask_of(place):
        return jnp.sum(jnp.where(lanes == place, masks[...], 0.0), axis=1, keepdims=True)

    def make_active_grad(first_row, which):
        low = grad_rows[first_row : first_row + 16].astype(bf16)
        for j in range(up_pairs):
            load_down(which, j).wait()
            active_grad[:, j * width : (j + 1) * width] = dot_nt(low, weights[1, :, j * width : (j + 1) * width])
        for copy in load_rest(which):
            copy.start()

    def upper_grad(j, place, count):
        at = pl.ds(pl.multiple_of(j * width, 128), width)
        load_slope(place, count, j).wait()

        def one(image, carry):
            row = active_grad[pl.ds(image, 1), at]
            weight = mask_of(place + image)
            for r in range(0, slots, ROWS):
                value = wide[image, r : r + ROWS, at].astype(f32) * (row * weight[r : r + ROWS])
                wide[image, r : r + ROWS, at] = value.astype(bf16)
            return carry

        lax.fori_loop(0, count, one, 0)

    active_grad[...] = first_active[...]
    all_turned(two_t, 0, finish)
    ones = jnp.full((128, both * slots), 1.0, bf16)

    def up_pair(j, carry):
        upper_grad(j, 0, both)

        @pl.when(j >= 2)
        def _():
            for odd in (0, 1):
                to_core(2 * (j - 2) + odd).wait_send()

        right = wide[:, :, pl.ds(pl.multiple_of(j * width, 128), width)].reshape(both * slots, width)
        terms(j, 0, j, False)

        @pl.when((j >= 1) & (j <= 2))
        def _():
            run_first(j - 1)

        bias = dot(ones, right).T.reshape(4, 4, 48, 128)
        lane = lax.broadcasted_iota(jnp.int32, (4, 48, 128), 2)
        spread = jnp.zeros((4, 48, 128), f32)
        for k in range(4):
            spread = spread + jnp.where(lane == 4 + k, bias[:, k], 0.0)
        extra[j // 2, j % 2] = spread.reshape(2, 2, 48, 128)
        return carry

    lax.fori_loop(0, up_pairs, up_pair, 0)
    sums[...] = jnp.zeros_like(sums)

    def hidden_two_back(count):
        def one(k, carry):
            flat = wide[0:count].reshape(count * slots, ff)
            at = pl.ds(pl.multiple_of(k * 256, 256), 256)
            mixed_grad[0:count, :, at] = dot_nt(flat, weights[0, at, :]).reshape(count, slots, 256)
            return carry

        lax.fori_loop(0, width // 256, one, 0)

    def norm_back(rows, grad, gain):
        normed, inverse = row_norm(rows)
        scaled = grad * gain
        back = inverse * (scaled - jnp.mean(scaled, axis=-1, keepdims=True) - normed * jnp.mean(scaled * normed, axis=-1, keepdims=True))
        return normed, back

    def run_hooks(hooks, at):
        for when, act in (hooks or {}).items():
            @pl.when(at == when)
            def _():
                act()

    def fold(values):
        return jnp.sum(values.reshape(ROWS // 8, 8, width), axis=0)

    def norm_two_back(place, count, keep, hooks=None):
        gain = gain_two[pl.ds(kind if keep else 1 - kind, 1), :]

        def load(image):
            return pltpu.make_async_copy(mixed.at[place + image], rows_in.at[image % 2], rsem.at[image % 2])

        load(0).start()

        def one(image, carry):
            @pl.when(image + 1 < count)
            def _():
                load(image + 1).start()

            load(image).wait()
            weight = mask_of(place + image)
            grad_row = grad_rows[pl.ds(place + image, 1), :]
            held, first_sum, second_sum = [], 0.0, 0.0
            for r in range(0, slots, ROWS):
                grad = mixed_grad[image, r : r + ROWS, :]
                normed, back = norm_back(rows_in[image % 2, r : r + ROWS, :], grad, gain)
                value = weight[r : r + ROWS] * grad_row + back
                mixed_low[image, r : r + ROWS, :] = value.astype(bf16)
                held.append(value)
                if keep:
                    first_sum = first_sum + fold(grad * normed)
                    second_sum = second_sum + fold(grad)
            mixed_grad[image] = jnp.concatenate(held)
            if keep:
                sums[2] = sums[2] + first_sum
                sums[3] = sums[3] + second_sum
            run_hooks(hooks, image)
            return carry

        lax.fori_loop(0, count, one, 0)

    def attended_back(count):
        for k in range(0, width, 256):
            flat = mixed_low[0:count].reshape(count * slots, width)
            got = dot_nt(flat, weights[1, k : k + 256, 3 * width : 4 * width])
            wide[0:count, :, 3 * width + k : 3 * width + k + 256] = got.astype(bf16).reshape(count, slots, 256)

    low_half = lax.broadcasted_iota(jnp.int32, (slots, 128), 1) < HEAD_DIM

    def attention_back(place, count, hooks=None):
        def load(image):
            return (pltpu.make_async_copy(packed.at[place + image], packs.at[image % 2], psem.at[0, image % 2]),
                    pltpu.make_async_copy(probs.at[place + image], shares.at[image % 2], psem.at[1, image % 2]))

        for copy in load(0):
            copy.start()

        def one(image, carry):
            @pl.when(image + 1 < count)
            def _():
                for copy in load(image + 1):
                    copy.start()

            for copy in load(image):
                copy.wait()
            now = image % 2
            for pair in range(HEADS // 2):
                at = slice(pair * 128, pair * 128 + 128)
                queries = packs[now, :, pair * 128 : pair * 128 + 128]
                keys = packs[now, :, width + pair * 128 : width + pair * 128 + 128]
                values = packs[now, :, 2 * width + pair * 128 : 2 * width + pair * 128 + 128]
                grad = wide[image, :, 3 * width + pair * 128 : 3 * width + pair * 128 + 128]
                share = shares[now, pair]
                blank = jnp.zeros_like(keys)
                two_keys = jnp.concatenate([jnp.where(low_half, keys, blank), jnp.where(low_half, blank, keys)])
                two_values = jnp.concatenate([jnp.where(low_half, values, blank), jnp.where(low_half, blank, values)])
                grad_share = dot_nt(two_values, grad)
                backs = []
                for side in (0, 1):
                    part = slice(side * slots, side * slots + slots)
                    weight = share[part].astype(f32)
                    product = weight * grad_share[part]
                    backs.append((product - weight * jnp.sum(product, axis=0, keepdims=True)).astype(bf16))
                back = jnp.concatenate(backs)
                grad_values = dot(share, grad)
                grad_keys = dot(back, queries) * head_scale
                grad_queries = dot_tn(back, two_keys) * head_scale
                wide[image, :, pair * 128 : pair * 128 + 128] = grad_queries.astype(bf16)
                wide[image, :, width + pair * 128 : width + pair * 128 + 128] = jnp.where(low_half, grad_keys[:slots], grad_keys[slots:]).astype(bf16)
                wide[image, :, 2 * width + pair * 128 : 2 * width + pair * 128 + 128] = jnp.where(low_half, grad_values[:slots], grad_values[slots:]).astype(bf16)
            run_hooks(hooks, image)
            return carry

        lax.fori_loop(0, count, one, 0)

    def norm_one_back(place, count, keep, out_place, out_count, hooks=None):
        gain = gain_one[pl.ds(kind if keep else 1 - kind, 1), :]

        def load(step):
            return pltpu.make_async_copy(tokens.at[pl.ds(place + 2 * step, 2)], rows_in, rsem.at[0])

        def store(step):
            return pltpu.make_async_copy(rows_out, tokens_out.at[pl.ds(out_place + 2 * step, 2)], osem.at[0])

        load(0).start()

        def one(step, carry):
            flat = wide[pl.ds(2 * step, 2), :, 0 : 3 * width].reshape(2 * slots, 3 * width)
            hidden_grad[...] = dot_nt(flat, weights[1, :, 0 : 3 * width])
            load(step).wait()

            @pl.when((step >= 1) & (step - 1 < out_count // 2))
            def _():
                store(step - 1).wait()

            for side in (0, 1):
                first_sum, second_sum = 0.0, 0.0
                for r in range(0, slots, ROWS):
                    grad = hidden_grad[side * slots + r : side * slots + r + ROWS, :]
                    normed, back = norm_back(rows_in[side, r : r + ROWS, :], grad, gain)
                    rows_out[side, r : r + ROWS, :] = mixed_grad[2 * step + side, r : r + ROWS, :] + back
                    if keep:
                        first_sum = first_sum + fold(grad * normed)
                        second_sum = second_sum + fold(grad)
                if keep:
                    sums[0] = sums[0] + first_sum
                    sums[1] = sums[1] + second_sum

            @pl.when(step + 1 < count // 2)
            def _():
                load(step + 1).start()

            @pl.when(step < out_count // 2)
            def _():
                store(step).start()

            run_hooks(hooks, step)
            return carry

        lax.fori_loop(0, count // 2, one, 0)
        if count == out_count:
            store(count // 2 - 1).wait()

    def serving(*jobs):
        def act():
            for run, pair in jobs:
                run(pair)
        return act

    def step(k):
        run_second(k)
        if k + 2 < pairs:
            run_first(k + 2)
        if k >= 1:
            run_third(k - 1)

    step(0)
    load_up(kind).wait()
    hidden_two_back(both)
    load_up(1 - kind).start()
    all_turned(one_t, 0, begin)
    norm_two_back(0, both, True, {6: lambda: step(1)})
    all_turned(att_t, 1, finish)
    terms(up_pairs, 1, None)
    for copy in load_rest(kind):
        copy.wait()
    attended_back(both)
    attention_back(0, both, {5: lambda: step(2)})
    all_turned(one_t, 0, finish)
    for j in range(2):
        terms(up_pairs + 1 + j, 0, j)
    step(3)
    terms(pairs - 1, 0, 2)
    norm_one_back(0, both, True, 0, own)

    vectors = jnp.concatenate([jnp.sum(sums[k], axis=0, keepdims=True) for k in range(4)] + [jnp.zeros((124, width), f32)])
    extra[...] = extra[...] + vectors.T.reshape(extra.shape)
    extra_mine[...] = extra[:, :, :, core]
    extra_to_core = remote(extra.at[:, :, :, 1 - core], extra_core, extra_sems.at[1, 0], extra_sems.at[1, 1], 1)
    extra_first_copy = remote(extra_mine.at[:, :, 1 - xx], extra_first, extra_sems.at[2, 0], extra_sems.at[2, 1], 2)
    extra_second_copy = remote(extra_mine.at[:, 1 - yy, xx], extra_second, extra_sems.at[3, 0], extra_sems.at[3, 1], 4)
    extra_to_core.start()

    for j in range(up_pairs):
        load_slope(both, own, j).start()
        load_down(1 - kind, j).start()
    make_active_grad(both, 1 - kind)

    def other_pair(j, carry):
        upper_grad(j, both, own)
        return carry

    lax.fori_loop(0, up_pairs, other_pair, 0)
    step(4)
    extra_to_core.wait()
    extra_mine[...] = extra_mine[...] + extra_core[...]
    extra_first_copy.start()
    load_up(1 - kind).wait()
    hidden_two_back(own)
    norm_two_back(both, own, False)
    for copy in load_rest(1 - kind):
        copy.wait()
    attended_back(own)
    attention_back(both, own)
    step(5)
    extra_first_copy.wait()
    extra_mine[:, :, xx] = extra_mine[:, :, xx] + extra_first[...]
    extra_second_copy.start()
    norm_one_back(both, own, False, own, own)

    reads = [pltpu.make_async_copy(grad_all.at[pl.ds(part * slots, slots), :], rows_in.at[part], rsem.at[part]) for part in (0, 1)]
    reads += [pltpu.make_async_copy(got.at[pl.ds(part * slots, slots), :], rows_out.at[part, :, pl.ds(0, CHUNK)], osem.at[part]) for part in (0, 1)]
    for copy in reads:
        copy.start()
    for copy in reads:
        copy.wait()
    sums_all = rows_out[:, :, 0:CHUNK].reshape(2 * slots, CHUNK)
    down = lax.dot_general(sums_all, rows_in[...].reshape(2 * slots, width), (((0,), (0,)), ((), ())), precision=highest, preferred_element_type=f32)
    half = CHUNK // 2
    mixed_grad[0:2, 0 : half // 2, :] = jnp.where(core == 0, down[:half], down[half:]).reshape(2, half // 2, width)
    write_down = pltpu.make_async_copy(mixed_grad.at[pl.ds(0, 2), pl.ds(0, half // 2), :], down_out, wsem.at[3])
    write_down.start()
    step(6)
    step(7)
    run_third(7)
    for chunk in range(2 * pairs - 4, 2 * pairs):
        to_core(chunk).wait_send()
    extra_second_copy.wait()
    extra_mine[:, yy, xx] = extra_mine[:, yy, xx] + extra_second[...]
    start_third(extra_mine, extra_owner, extra_sem)
    for target, low, high in outputs:
        serve(functools.partial(run_last, target, low), low, high)
    wait_third(extra_mine, extra_owner, extra_sem)
    extra_out[...] = extra_owner[0] + extra_owner[1]
    for target, low, high in outputs:
        for chunk in range(2 * low, 2 * high):
            write(chunk, target, low).wait()
    write_down.wait()


def backward(own, grad_rows, first_active, masks, got, grad_all, tokens, saved, weights):
    gain_one, shift_one, w_qkv, w_out, gain_two, shift_two, w_up, b_up, w_down = weights
    slots, width = tokens.shape[1:]
    ff = w_up.shape[2]
    both = 2 * own
    chunks = 2 * ff // CHUNK
    one_t, packed, probs, att_t, mixed, two_t, slope = saved
    split = lambda one: one.reshape(one.shape[0], 8, 2, one.shape[2], one.shape[3])
    anywhere, vmem = pl.BlockSpec(memory_space=pl.ANY), pl.BlockSpec(memory_space=pltpu.VMEM)
    return pl.pallas_call(
        functools.partial(backward_kernel, own),
        out_shape=(
            jax.ShapeDtypeStruct((48, ff), f32), jax.ShapeDtypeStruct((48, width), f32), jax.ShapeDtypeStruct((48, 3 * width), f32),
            jax.ShapeDtypeStruct((48, 128), f32), jax.ShapeDtypeStruct((both, slots, width), f32),
            jax.ShapeDtypeStruct((2, CHUNK // 4, width), f32),
        ),
        in_specs=[vmem] * 5 + [anywhere] * 14,
        out_specs=(anywhere, anywhere, anywhere, vmem, anywhere, anywhere),
        scratch_shapes=[
            pltpu.VMEM((chunks, 2, 2, 2, 48, CHUNK), f32),
            pltpu.VMEM((2, 2, 2, 2, 2, 48, CHUNK), f32),
            pltpu.VMEM((chunks, 2, 2, 2, 48, CHUNK), f32),
            pltpu.VMEM((chunks, 2, 2, 48, CHUNK), f32),
            pltpu.VMEM((chunks, 2, 48, CHUNK), f32),
            pltpu.VMEM((chunks, 2, 48, CHUNK), f32),
            pltpu.VMEM((2, 2, 2, 2, 48, 128), f32),
            pltpu.VMEM((2, 2, 2, 48, 128), f32),
            pltpu.VMEM((2, 2, 2, 48, 128), f32),
            pltpu.VMEM((2, 2, 48, 128), f32),
            pltpu.VMEM((2, 48, 128), f32),
            pltpu.VMEM((2, 48, 128), f32),
            pltpu.VMEM((both, slots, ff), bf16),
            pltpu.VMEM((both, slots, width), f32),
            pltpu.VMEM((both, slots, width), bf16),
            pltpu.VMEM((2, 2, 8, 48, both * slots), bf16),
            pltpu.VMEM((2, width, ff), bf16),
            pltpu.VMEM((16, ff), f32),
            pltpu.VMEM((4, 8, width), f32),
            pltpu.VMEM((2, slots, 3 * width), bf16),
            pltpu.VMEM((2, HEADS // 2, 2 * slots, slots), bf16),
            pltpu.VMEM((2, slots, width), f32),
            pltpu.VMEM((2, slots, width), f32),
            pltpu.VMEM((2 * slots, width), f32),
            pltpu.SemaphoreType.DMA((6, chunks, 2)),
            pltpu.SemaphoreType.DMA((6, 2)),
            pltpu.SemaphoreType.DMA((7,)),
            pltpu.SemaphoreType.DMA((4,)),
            pltpu.SemaphoreType.DMA((2, 2, both)),
            pltpu.SemaphoreType.DMA((2, 2)),
            pltpu.SemaphoreType.DMA((2,)),
            pltpu.SemaphoreType.DMA((2,)),
        ],
        compiler_params=pltpu.CompilerParams(collective_id=1, has_side_effects=True, vmem_limit_bytes=63 << 20),
    )(grad_rows, first_active, masks, gain_one, gain_two, got.reshape(-1, CHUNK), grad_all, tokens, split(one_t), packed, probs, split(att_t), mixed, split(two_t), slope,
      w_qkv, w_out, w_up, w_down)


def tokens_of(patches, visible, modality):
    micro_count, images, _, patch_count, width = patches.shape
    cells = lax.dynamic_index_in_dim(patches, modality, 2, keepdims=False).reshape(micro_count * images, patch_count, width)
    picked = (visible[:, :, None] == jnp.arange(patch_count)[None, None, :]).astype(bf16)
    return jnp.einsum("isp,ipd->isd", picked, cells, preferred_element_type=f32)


def cells_of(grad_tokens, visible, patch_count):
    picked = (visible[:, None, :] == jnp.arange(patch_count)[None, :, None]).astype(f32)
    return jnp.einsum("ips,isd->ipd", picked, grad_tokens, precision=highest)


def on_tuned(patches, visible, valid_mask, weights):
    n = lax.axis_size("dp")
    me = lax.axis_index("dp")
    micro_count, images, _, patch_count, width = patches.shape
    own = micro_count * images
    slots = visible.shape[-1]
    kind = (me // 8) % 2
    kinds = jnp.stack([kind, 1 - kind]).astype(jnp.int32)
    seen, mask = visible.reshape(own, slots), valid_mask.reshape(own, slots)
    loss, grad_all, got, grad_rows, active_grad, masks, tokens, *saved = forward(
        n, micro_count, slot_info(seen, mask), patches.reshape(own, 2, patch_count, width), weights)
    up, out, qkv, extra, grad_tokens, down = backward(own, grad_rows, active_grad, masks, got, grad_all, tokens, saved, weights)
    patches_grad = place_cells(kinds, seen, grad_tokens, patch_count).reshape(patches.shape)
    return (loss[0, 0], patches_grad, extra[:, 0], extra[:, 1], qkv, out, extra[:, 2], extra[:, 3], up,
            extra[:, 4:8].T.reshape(-1), down.reshape(-1, width))


def on_plain(patches, visible, valid_mask, weights):
    n = lax.axis_size("dp")
    me = lax.axis_index("dp")
    micro_count, images, _, patch_count, width = patches.shape
    own = micro_count * images
    slots = visible.shape[-1]
    ff = weights[6].shape[2]
    seen = visible.reshape(own, slots)
    mask = valid_mask.reshape(own, slots)
    outcomes = []
    for modality in (0, 1):
        params = params_of(weights, modality)
        outcomes.append((params,) + encode_forward(tokens_of(patches, seen, modality), seen, mask, params))
    pooled = jnp.concatenate([pool(active, mixed, mask, params[8]) for params, active, mixed, _ in outcomes])
    counted = jnp.sum(mask.astype(f32), axis=1)[:, None]
    shares = jnp.stack([active / counted for _, active, _, _ in outcomes])
    down_rows = 2 * ff // n
    shares = shares.reshape(2, own, n // 2, down_rows).transpose(0, 2, 1, 3).reshape(n, own * down_rows)
    loss, grad_all = contrast(lax.all_gather(pooled, "dp", axis=0, tiled=True), 2 * own, micro_count)
    got = lax.all_to_all(shares, "dp", 0, 0, tiled=True)
    grad_all = grad_all.reshape(n, 2, own, width)
    grad_down = jnp.einsum(
        "iw,id->wd", got.reshape(n * own, down_rows),
        lax.dynamic_index_in_dim(grad_all, me // (n // 2), 1, keepdims=False).reshape(n * own, width), precision=highest)
    mine = lax.dynamic_index_in_dim(grad_all, me, 0, keepdims=False)
    backs = [encode_backward(mine[m], outcomes[m][3], mask, outcomes[m][0]) for m in (0, 1)]
    patches_grad = jnp.stack([cells_of(back[0], seen, patch_count) for back in backs], 1).reshape(patches.shape)
    joined = jax.tree.map(lambda a, b: jnp.concatenate([a, b]), backs[0][1], backs[1][1])
    shards = tuple(lax.psum_scatter(one, "dp", scatter_dimension=0, tiled=True) for one in joined)
    return (loss[0, 0], patches_grad) + shards + (grad_down,)


def solution(mesh):
    in_specs = (P(None, "dp"), P(None, "dp"), P(None, "dp")) + (P(),) * 9
    out_specs = (P(), P(None, "dp")) + (P("dp"),) * 9

    def on_device(patches, visible, valid_mask, *weights):
        run = on_tuned if lax.axis_size("dp") == 32 else on_plain
        return run(patches, visible, valid_mask, weights)

    return jax.shard_map(on_device, mesh=mesh, in_specs=in_specs, out_specs=out_specs, check_vma=False)
```

```python
import functools
import math

import jax
import jax.numpy as jnp
from jax import lax
from jax.experimental import pallas as pl
from jax.experimental.pallas import tpu as pltpu
from jax.sharding import PartitionSpec as P

HEADS = 12
HEAD_DIM = 64
GRID = 15
MESH = pl.DeviceIdType.MESH

norm_epsilon = 1e-06
unit_epsilon = 1e-06
logit_scale = 100.0
masked_score = -1e30
highest = lax.Precision.HIGHEST
head_scale = 1.0 / math.sqrt(HEAD_DIM)
f32 = jnp.float32
bf16 = jnp.bfloat16


def exact_gelu(values_in):
    return jax.nn.gelu(values_in, approximate=False)


def layer_norm(values_in, gain_vec, shift_vec):
    centre = values_in - jnp.mean(values_in, axis=-1, keepdims=True)
    inverse = lax.rsqrt(jnp.mean(centre * centre, axis=-1, keepdims=True) + norm_epsilon)
    normed = centre * inverse
    return (normed * gain_vec + shift_vec, normed, inverse)


def norm_back(grad_out, normed, inverse, gain_vec):
    grad_normed = grad_out * gain_vec
    mean_plain = jnp.mean(grad_normed, axis=-1, keepdims=True)
    mean_normed = jnp.mean(grad_normed * normed, axis=-1, keepdims=True)
    grad_in = inverse * (grad_normed - mean_plain - normed * mean_normed)
    return (grad_in, jnp.sum(grad_out * normed, axis=0), jnp.sum(grad_out, axis=0))


def alibi_bias(visible_rows):
    rows_pos = (visible_rows // GRID).astype(f32)
    cols_pos = (visible_rows % GRID).astype(f32)
    rows_gap = rows_pos[:, :, None] - rows_pos[:, None, :]
    cols_gap = cols_pos[:, :, None] - cols_pos[:, None, :]
    distance = jnp.sqrt(rows_gap * rows_gap + cols_gap * cols_gap)
    slopes = jnp.exp2(-8.0 * (jnp.arange(HEADS, dtype=f32) + 1.0) / HEADS)
    return -slopes[None, :, None, None] * distance[:, None, :, :]


def split_heads(packed):
    images, slot_count, _ = packed.shape
    shaped = packed.reshape(images, slot_count, 3, HEADS, HEAD_DIM)
    return (shaped[:, :, 0], shaped[:, :, 1], shaped[:, :, 2])


def encode_forward(tokens_in, visible_rows, mask_rows, params):
    gain_one, shift_one, w_qkv, w_out, gain_two, shift_two, w_up, b_up, w_down = params
    images, slots, width = tokens_in.shape
    flat_in = tokens_in.reshape(images * slots, width)
    hidden_one, normed_one, inverse_one = layer_norm(flat_in, gain_one, shift_one)
    hidden_one = hidden_one.astype(bf16)
    packed = jnp.dot(hidden_one, w_qkv, preferred_element_type=f32).astype(bf16)
    packed = packed.reshape(images, slots, 3 * width)
    queries, keys, values = split_heads(packed)
    scores = jnp.einsum("iqhd,ikhd->ihqk", queries, keys, preferred_element_type=f32)
    scores = scores * head_scale + alibi_bias(visible_rows)
    scores = jnp.where((mask_rows > 0)[:, None, None, :], scores, masked_score)
    attention = jax.nn.softmax(scores, axis=-1)
    attended = jnp.einsum("ihqk,ikhd->iqhd", attention.astype(bf16), values, preferred_element_type=f32)
    attended = attended.reshape(images * slots, width).astype(bf16)
    mixed = flat_in + jnp.dot(attended, w_out, preferred_element_type=f32)
    hidden_two, normed_two, inverse_two = layer_norm(mixed, gain_two, shift_two)
    hidden_two = hidden_two.astype(bf16)
    upper = jnp.dot(hidden_two, w_up, preferred_element_type=f32) + b_up
    active, gelu_back = jax.vjp(exact_gelu, upper)
    active = active.astype(bf16).astype(f32)
    weight = mask_rows.astype(f32)
    active_sum = jnp.sum(active.reshape(images, slots, -1) * weight[:, :, None], axis=1)
    mixed_sum = jnp.sum(mixed.reshape(images, slots, width) * weight[:, :, None], axis=1)
    saved = (normed_one, inverse_one, hidden_one, packed, attention, attended, normed_two, inverse_two, hidden_two, gelu_back)
    return active_sum, mixed_sum, saved


def pool(active_sum, mixed_sum, mask_rows, w_down):
    counted = jnp.sum(mask_rows.astype(f32), axis=1)[:, None]
    down = jnp.dot(active_sum, w_down.astype(f32), precision=highest)
    return (mixed_sum + down) / counted


def encode_backward(grad_pooled, saved, mask_rows, params):
    normed_one, inverse_one, hidden_one, packed, attention, attended, normed_two, inverse_two, hidden_two, gelu_back = saved
    gain_one, shift_one, w_qkv, w_out, gain_two, shift_two, w_up, b_up, w_down = params
    images, slots, three_width = packed.shape
    width = three_width // 3
    rows = images * slots
    weight = mask_rows.astype(f32)
    counted = jnp.sum(weight, axis=1)[:, None]
    grad_row = grad_pooled / counted
    grad_output = (weight[:, :, None] * grad_row[:, None, :]).reshape(rows, width)
    grad_active = jnp.dot(grad_row.astype(bf16), w_down.T, preferred_element_type=f32)
    grad_active = (weight[:, :, None] * grad_active[:, None, :]).reshape(rows, -1)
    grad_upper = gelu_back(grad_active)[0].astype(bf16)
    grad_bias = jnp.sum(grad_upper.astype(f32), axis=0)
    grad_up = jnp.dot(hidden_two.T, grad_upper, preferred_element_type=f32)
    grad_hidden_two = jnp.dot(grad_upper, w_up.T, preferred_element_type=f32)
    grad_norm_two, grad_gain_two, grad_shift_two = norm_back(grad_hidden_two, normed_two, inverse_two, gain_two)
    grad_mixed = grad_output + grad_norm_two
    grad_mixed_low = grad_mixed.astype(bf16)
    grad_out = jnp.dot(attended.T, grad_mixed_low, preferred_element_type=f32)
    grad_attended = jnp.dot(grad_mixed_low, w_out.T, preferred_element_type=f32).astype(bf16)
    grad_attended = grad_attended.reshape(images, slots, HEADS, HEAD_DIM)
    queries, keys, values = split_heads(packed)
    grad_value = jnp.einsum("ihqk,iqhd->ikhd", attention.astype(bf16), grad_attended, preferred_element_type=f32)
    grad_attention = jnp.einsum("iqhd,ikhd->ihqk", grad_attended, values, preferred_element_type=f32)
    grad_scores = attention * (grad_attention - jnp.sum(attention * grad_attention, axis=-1, keepdims=True))
    grad_scores = grad_scores.astype(bf16)
    grad_query = jnp.einsum("ihqk,ikhd->iqhd", grad_scores, keys, preferred_element_type=f32) * head_scale
    grad_key = jnp.einsum("ihqk,iqhd->ikhd", grad_scores, queries, preferred_element_type=f32) * head_scale
    grad_packed = jnp.stack([grad_query, grad_key, grad_value], axis=2).astype(bf16).reshape(rows, three_width)
    grad_qkv = jnp.dot(hidden_one.T, grad_packed, preferred_element_type=f32)
    grad_hidden_one = jnp.dot(grad_packed, w_qkv.T, preferred_element_type=f32)
    grad_norm_one, grad_gain_one, grad_shift_one = norm_back(grad_hidden_one, normed_one, inverse_one, gain_one)
    grad_tokens = (grad_mixed + grad_norm_one).reshape(images, slots, width)
    return grad_tokens, (grad_gain_one, grad_shift_one, grad_qkv, grad_out, grad_gain_two, grad_shift_two, grad_up, grad_bias)


def contrast(pooled, own_rows, micro_count):
    count = pooled.shape[0]
    images = own_rows // (2 * micro_count)
    inverse = lax.rsqrt(jnp.sum(pooled * pooled, axis=-1, keepdims=True) + unit_epsilon)
    unit = pooled * inverse
    logits = logit_scale * lax.dot_general(unit, unit, (((1,), (1,)), ((), ())), precision=highest, preferred_element_type=f32)
    row = lax.broadcasted_iota(jnp.int32, (count, count), 0)
    col = lax.broadcasted_iota(jnp.int32, (count, count), 1)
    half = own_rows // 2
    row_mod, col_mod = (row // half) % 2, (col // half) % 2
    row_micro, col_micro = (row // images) % micro_count, (col // images) % micro_count
    allowed = (row_mod != col_mod) & (row_micro == col_micro)
    paired = jnp.where(col == row + half * (1 - 2 * row_mod), 1.0, 0.0)
    logits = jnp.where(allowed, logits, masked_score)
    row_max = jnp.max(logits, axis=1, keepdims=True)
    row_lse = row_max + jnp.log(jnp.sum(jnp.exp(logits - row_max), axis=1, keepdims=True))
    col_max = jnp.max(logits, axis=0, keepdims=True)
    col_lse = col_max + jnp.log(jnp.sum(jnp.exp(logits - col_max), axis=0, keepdims=True))
    scale = 1.0 / count
    diagonal = jnp.sum(jnp.where(paired > 0, logits, 0.0), axis=1, keepdims=True)
    loss = scale * jnp.sum(row_lse - diagonal, axis=0, keepdims=True)
    spread = jnp.exp(logits - row_lse) + jnp.exp(logits - col_lse) - 2.0 * paired
    grad_unit = (logit_scale * scale) * jnp.dot(spread, unit, precision=highest, preferred_element_type=f32)
    grad_pooled = inverse * (grad_unit - unit * jnp.sum(unit * grad_unit, axis=-1, keepdims=True))
    return loss, grad_pooled


def params_of(weights, modality):
    return tuple(lax.dynamic_index_in_dim(one, modality, 0, keepdims=False) for one in weights)


GROWS = 32
SLOPES = [2.0 ** (-8.0 * (head + 1) / HEADS) for head in range(HEADS)]
ROWS = 32
WIDE = 512


def gelu_pair(upper):
    size = jnp.abs(upper)
    bell = jnp.exp(-0.5 * upper * upper)
    below = 1.0 + (0.3275911 * math.sqrt(0.5)) * size
    t = pltpu.reciprocal(below, approx=True)
    t = t * (2.0 - below * t)
    tail = t * (0.5 * 0.254829592 + t * (0.5 * -0.284496736 + t * (0.5 * 1.421413741 + t * (0.5 * -1.453152027 + t * (0.5 * 1.061405429)))))
    tail = tail * bell
    normal = jnp.where(upper < 0, tail, 1.0 - tail)
    return upper * normal, normal + upper * (bell * (1.0 / math.sqrt(2.0 * math.pi)))


def row_norm(values):
    centre = values - jnp.mean(values, axis=-1, keepdims=True)
    inverse = lax.rsqrt(jnp.mean(centre * centre, axis=-1, keepdims=True) + norm_epsilon)
    return centre * inverse, inverse


def dot(a, b):
    return jnp.dot(a, b, preferred_element_type=f32)


def dot_nt(a, b):
    return lax.dot_general(a, b, (((1,), (1,)), ((), ())), preferred_element_type=f32)


def dot_tn(a, b):
    return lax.dot_general(a, b, (((0,), (0,)), ((), ())), preferred_element_type=f32)


def roll_if(flag, value):
    return jnp.where(flag == 1, jnp.concatenate([value[4:], value[:4]]), value)


def forward_kernel(n, micro_count, visible, valid_mask, gain_one, shift_one, gain_two, shift_two, b_up, patches, w_qkv, w_out, w_up, w_down,
                   loss_out, grad_out, got, grad_rows, active_grad, masks, tokens_out, one_out, packed_out, probs_out, att_out, mixed_out, two_out, slope_out,
                   cells, tok, info_in, there, wq, wo, wu, wd, one_t, packed, probs, att_t, mixed, two_t, slope, upper, active, hidden, attended, turned,
                   active_sum, share, every, send_sem, recv_sem, sum_send, sum_recv, isem, wsem, osem, tsem, xsem):
    me = lax.axis_index("dp")
    kind = (me // 8) % 2
    images, slots, width = info_in.shape[0], info_in.shape[2], tok.shape[2]
    rows = images * slots
    per_micro = visible.shape[1]
    ff = wu.shape[2]

    read_cells = pltpu.make_async_copy(patches, cells, isem)
    read_cells.start()
    reads = []
    for slot, which in ((0, kind), (1, 1 - kind)):
        reads.append([pltpu.make_async_copy(source.at[which], target.at[slot], wsem.at[slot, number])
                      for number, (source, target) in enumerate(((w_qkv, wq), (w_out, wo), (w_up, wu), (w_down, wd)))])
    for copy in reads[0] + reads[1]:
        copy.start()
    barrier = pltpu.get_barrier_semaphore()

    def greet(step, carry):
        pl.semaphore_signal(barrier, inc=1, device_id=(lax.rem(me + step, n),), device_id_type=MESH)
        return carry

    lax.fori_loop(1, n, greet, 0)

    for image in range(images):
        seen = visible[image // per_micro, image % per_micro : image % per_micro + 1, :].astype(f32)
        grid_row = jnp.floor((seen + 0.5) * (1.0 / GRID))
        valid = valid_mask[image // per_micro, image % per_micro : image % per_micro + 1, :].astype(f32)
        info_in[image] = jnp.concatenate([grid_row, seen - GRID * grid_row, valid, seen, jnp.zeros((4, slots), f32)])
    read_cells.wait()

    def pick(modality, place):
        def one(image, carry):
            seen = info_in[image, 3:4, :]
            picked = jnp.where(lax.broadcasted_iota(jnp.int32, (cells.shape[2], slots), 0).astype(f32) == seen, 1.0, 0.0).astype(bf16)
            tok[place + image] = dot_tn(picked, cells[image, modality])
            return carry

        lax.fori_loop(0, images, one, 0)

    pick(1 - kind, 2 * images)
    pl.semaphore_wait(barrier, n - 1)
    send_tokens = [
        pltpu.make_async_remote_copy(src_ref=info_in, dst_ref=there, send_sem=xsem.at[0, 0], recv_sem=xsem.at[0, 1], device_id=(me ^ 8,), device_id_type=MESH),
        pltpu.make_async_remote_copy(src_ref=tok.at[pl.ds(2 * images, images)], dst_ref=tok.at[pl.ds(images, images)],
                                     send_sem=xsem.at[1, 0], recv_sem=xsem.at[1, 1], device_id=(me ^ 8,), device_id_type=MESH)]
    for copy in send_tokens:
        copy.start()
    pick(kind, 0)

    def store_tokens(place):
        at = pl.ds(place * images, images)
        return pltpu.make_async_copy(tok.at[at], tokens_out.at[at], tsem.at[place])

    store_tokens(0).start()
    store_tokens(2).start()

    stores = {}

    def ready(number):
        if number in stores:
            stores.pop(number).wait()

    def store(number, place):
        source, target = ((one_t, one_out), (packed, packed_out), (probs, probs_out), (att_t, att_out), (mixed, mixed_out), (two_t, two_out), (slope, slope_out))[number]
        copy = pltpu.make_async_copy(source, target.at[pl.ds(place * images, images)], osem.at[number])
        copy.start()
        stores[number] = copy

    low_half = lax.broadcasted_iota(jnp.int32, (slots, 128), 1) < HEAD_DIM
    row_of = lax.broadcasted_iota(jnp.int32, (8, slots), 0)

    def marks_of(info):
        return jnp.concatenate([jnp.where(row_of == image, info[image, 2:3, :], 0.0) for image in range(images)], axis=1).astype(bf16)

    def group(place, slot, which, info, whole, pauses):
        gain1, shift1 = gain_one[pl.ds(which, 1), :], shift_one[pl.ds(which, 1), :]
        gain2, shift2 = gain_two[pl.ds(which, 1), :], shift_two[pl.ds(which, 1), :]

        def norm(source, first, target, gain, shift):
            def one(image, carry):
                for r in range(0, slots, ROWS):
                    normed, _ = row_norm(source[first + image, r : r + ROWS, :])
                    hidden[image, r : r + ROWS, :] = (normed * gain + shift).astype(bf16)
                target[image] = hidden[image].T.reshape(target.shape[1:])
                return carry

            lax.fori_loop(0, images, one, 0)

        ready(0)
        norm(tok, place * images, one_t, gain1, shift1)
        store(0, place)
        ready(1)
        if pauses is None:
            reads[slot][0].wait()

        def project(i, carry):
            at = pl.ds(pl.multiple_of(i * 768, 768), 768)
            packed[:, :, at] = dot(hidden[...].reshape(rows, width), wq[slot, :, at]).astype(bf16).reshape(images, slots, 768)
            return carry

        lax.fori_loop(0, 3 * width // 768, project, 0)
        store(1, place)
        if pauses:
            pauses[0]()
        ready(2)
        ready(3)

        def attend(image, carry):
            line = info[image]
            column = line.T
            gap_r = column[:, 0:1] - line[0:1, :]
            gap_c = column[:, 1:2] - line[1:2, :]
            away = -jnp.sqrt(gap_r * gap_r + gap_c * gap_c)
            away = jnp.where(column[:, 2:3] > 0, away, -1e33)
            for pair in range(HEADS // 2):
                at = slice(pair * 128, pair * 128 + 128)
                queries = packed[image, :, pair * 128 : pair * 128 + 128]
                keys = packed[image, :, width + pair * 128 : width + pair * 128 + 128]
                values = packed[image, :, 2 * width + pair * 128 : 2 * width + pair * 128 + 128]
                blank = jnp.zeros_like(keys)
                two_keys = jnp.concatenate([jnp.where(low_half, keys, blank), jnp.where(low_half, blank, keys)])
                two_values = jnp.concatenate([jnp.where(low_half, values, blank), jnp.where(low_half, blank, values)])
                scores = dot_nt(two_keys, queries)
                shares = []
                for side in (0, 1):
                    one = scores[side * slots : side * slots + slots] * head_scale + SLOPES[2 * pair + side] * away
                    power = jnp.exp(one - jnp.max(one, axis=0, keepdims=True))
                    shares.append((power * (1.0 / jnp.sum(power, axis=0, keepdims=True))).astype(bf16))
                both_shares = jnp.concatenate(shares)
                probs[image, pair] = both_shares
                flipped = dot_tn(two_values, both_shares).astype(bf16)
                turned[at, :] = flipped
                attended[image, :, at] = flipped.T
            att_t[image] = turned[...].reshape(att_t.shape[1:])
            return carry

        lax.fori_loop(0, images, attend, 0)
        store(2, place)
        store(3, place)
        if pauses:
            pauses[1]()
        ready(4)
        if pauses is None:
            reads[slot][1].wait()

        def output(i, carry):
            at = pl.ds(pl.multiple_of(i * 256, 256), 256)
            mixed[:, :, at] = tok[pl.ds(place * images, images), :, at] + dot(attended[...].reshape(rows, width), wo[slot, :, at]).reshape(images, slots, 256)
            return carry

        lax.fori_loop(0, width // 256, output, 0)
        store(4, place)
        ready(5)
        norm(mixed, 0, two_t, gain2, shift2)
        store(5, place)
        if pauses:
            pauses[2]()
        ready(6)
        if pauses is None:
            reads[slot][2].wait()
        marks = marks_of(info)

        def columns(i):
            return pl.ds(pl.multiple_of(i * WIDE, WIDE), WIDE)

        def rise(i, slot_up):
            upper[slot_up] = dot(hidden[...].reshape(rows, width), wu[slot, :, columns(i)])

        def bend(i, now):
            bias = b_up[pl.ds(which, 1), columns(i)]
            for r in range(0, rows, GROWS):
                value, back = gelu_pair(upper[now, r : r + GROWS, :] + bias)
                if whole:
                    active[r : r + GROWS, :] = value.astype(bf16)
                slope[r // slots, r % slots : r % slots + GROWS, columns(i)] = back.astype(bf16)
            if whole:
                active_sum[slot, :, columns(i)] = dot(marks, active[...])

        rise(0, 0)

        def feed(i, carry):
            rise(2 * i + 1, 1)
            bend(2 * i, 0)
            rise(2 * i + 2, 0)
            bend(2 * i + 1, 1)
            return carry

        steps = ff // WIDE
        lax.fori_loop(0, steps // 2 - 1, feed, 0)
        rise(steps - 1, 1)
        bend(steps - 2, 0)
        bend(steps - 1, 1)
        store(6, place)
        if not whole:
            return None
        reads[slot][3].wait()
        total = active_sum[slot]
        high = total.astype(bf16)
        rest = total - high.astype(f32)
        middle = rest.astype(bf16)
        lowest = (rest - middle.astype(f32)).astype(bf16)
        stacked = jnp.concatenate([high, middle, lowest, jnp.zeros_like(high)])
        parts = dot(stacked, wd[slot])
        downs = parts[0:8] + parts[8:16] + parts[16:24]
        sums, counts = [], []
        for image in range(images):
            weight = info[image].T[:, 2:3]
            sums.append(jnp.sum(mixed[image] * weight, axis=0, keepdims=True))
            counts.append(jnp.sum(weight, axis=0, keepdims=True))
        count = jnp.concatenate(counts + [jnp.ones((8 - images, 1), f32)])
        pooled = (jnp.concatenate(sums + [jnp.zeros((8 - images, width), f32)]) + downs) / count
        share[which] = roll_if(which, total / count)
        return roll_if(which, pooled)

    def copies(sources, flip, first):
        made = []
        for number, source in enumerate(sources):
            made.append(pltpu.make_async_remote_copy(
                src_ref=every.at[source], dst_ref=every.at[source], send_sem=send_sem.at[first + number], recv_sem=recv_sem.at[first + number],
                device_id=(me ^ flip,), device_id_type=MESH))
        for copy in made:
            copy.start()
        return made

    def finish(made):
        for copy in made:
            copy.wait()

    pooled = group(0, 0, kind, info_in, True, None)
    every[me] = pooled + group(2, 1, 1 - kind, info_in, True, None)

    waves = [copies([me], flip, number) [0] for number, flip in enumerate((8, 16, 24))]
    held = [me, me ^ 8, me ^ 16, me ^ 24]
    state = {"wave": waves, "held": held}

    def next_wave(flip, first):
        def run():
            finish(state["wave"])
            state["wave"] = copies(state["held"], flip, first)
            state["held"] = state["held"] + [one ^ flip for one in state["held"]]
        return run

    def sums_out(step, carry):
        peer = lax.rem(me + step, n)
        at = pl.ds(pl.multiple_of(((peer % (n // 2)) // 2) * 384, 384), 384)
        pltpu.make_async_remote_copy(
            src_ref=share.at[peer // (n // 2), :, at], dst_ref=got.at[me], send_sem=sum_send.at[step], recv_sem=sum_recv.at[step],
            device_id=(peer,), device_id_type=MESH).start()
        return carry

    def last_wave():
        next_wave(1, 15)()
        lax.fori_loop(1, n, sums_out, 0)

    send_tokens[0].wait()
    send_tokens[1].wait()
    store_tokens(1).start()
    group(1, 0, kind, there, False, [next_wave(4, 3), next_wave(2, 7), last_wave])
    finish(state["wave"])
    loss, grad = contrast(every[...].reshape(n * 8, width), 8, micro_count)
    loss_out[...] = loss
    grad_out[...] = grad
    got[me] = share[me // (n // 2), :, pl.ds(pl.multiple_of(((me % (n // 2)) // 2) * 384, 384), 384)]

    def per_slot(device, which, info):
        count = jnp.concatenate([jnp.sum(info[image, 2:3, :], axis=1, keepdims=True) for image in range(images)])
        return roll_if(which, grad_out[pl.ds(pl.multiple_of(device * 8, 8), 8), :])[0:images] / count

    spread = jnp.concatenate([per_slot(me, kind, info_in), per_slot(me ^ 8, kind, there), per_slot(me, 1 - kind, info_in), jnp.zeros((24 - 3 * images, width), f32)])
    grad_rows[...] = spread
    low = spread[0:16].astype(bf16)
    for j in range(0, ff, width):
        active_grad[:, j : j + width] = dot_nt(low, wd[0, j : j + width, :])
    lines = [info[image, 2:3, :] for info in (info_in, there, info_in) for image in range(images)]
    masks[...] = jnp.concatenate(lines + [jnp.zeros((slots - 3 * images, slots), f32)]).T

    def sums_in(step, carry):
        peer = lax.rem(me + n - step, n)
        pltpu.make_async_remote_copy(
            src_ref=share.at[0, :, pl.ds(0, 384)], dst_ref=got.at[peer], send_sem=sum_send.at[step], recv_sem=sum_recv.at[step],
            device_id=(peer,), device_id_type=MESH).wait()
        return carry

    lax.fori_loop(1, n, sums_in, 0)
    for number in range(7):
        ready(number)
    for place in range(3):
        store_tokens(place).wait()


def forward(n, visible, valid_mask, patches, weights):
    gain_one, shift_one, w_qkv, w_out, gain_two, shift_two, w_up, b_up, w_down = weights
    micro_count, per_micro, slots = visible.shape
    images = micro_count * per_micro
    width, ff = w_up.shape[1:]
    anywhere, vmem = pl.BlockSpec(memory_space=pl.ANY), pl.BlockSpec(memory_space=pltpu.VMEM)
    turned = (16, width // 16, slots)
    kept = [(turned, bf16), ((slots, 3 * width), bf16), ((HEADS // 2, 2 * slots, slots), bf16), (turned, bf16), ((slots, width), f32),
            (turned, bf16), ((slots, ff), bf16)]
    return pl.pallas_call(
        functools.partial(forward_kernel, n, micro_count),
        out_shape=[jax.ShapeDtypeStruct(shape, f32) for shape in
                   ((1, 1), (8 * n, width), (n, 8, 384), (24, width), (16, ff), (slots, slots), (3 * images, slots, width))]
        + [jax.ShapeDtypeStruct((3 * images,) + dims, dtype) for dims, dtype in kept],
        in_specs=[vmem] * 7 + [anywhere] * 5,
        out_specs=[vmem] * 6 + [anywhere] * 8,
        scratch_shapes=[
            pltpu.VMEM(patches.shape, bf16),
            pltpu.VMEM((3 * images, slots, width), f32),
            pltpu.VMEM((images, 8, slots), f32),
            pltpu.VMEM((images, 8, slots), f32),
            pltpu.VMEM(w_qkv.shape, bf16), pltpu.VMEM(w_out.shape, bf16), pltpu.VMEM(w_up.shape, bf16), pltpu.VMEM(w_down.shape, bf16)]
        + [pltpu.VMEM((images,) + dims, dtype) for dims, dtype in kept]
        + [
            pltpu.VMEM((2, images * slots, WIDE), f32),
            pltpu.VMEM((images * slots, WIDE), bf16),
            pltpu.VMEM((images, slots, width), bf16),
            pltpu.VMEM((images, slots, width), bf16),
            pltpu.VMEM((width, slots), bf16),
            pltpu.VMEM((2, 8, ff), f32),
            pltpu.VMEM((2, 8, ff), f32),
            pltpu.VMEM((n, 8, width), f32),
            pltpu.SemaphoreType.DMA((31,)),
            pltpu.SemaphoreType.DMA((31,)),
            pltpu.SemaphoreType.DMA((n,)),
            pltpu.SemaphoreType.DMA((n,)),
            pltpu.SemaphoreType.DMA,
            pltpu.SemaphoreType.DMA((2, 4)),
            pltpu.SemaphoreType.DMA((7,)),
            pltpu.SemaphoreType.DMA((3,)),
            pltpu.SemaphoreType.DMA((2, 2)),
        ],
        compiler_params=pltpu.CompilerParams(collective_id=0, has_side_effects=True, vmem_limit_bytes=63 << 20),
    )(visible, valid_mask, gain_one, shift_one, gain_two, shift_two, b_up, patches, w_qkv, w_out, w_up, w_down)


CHUNK = 384


def meet(peers):
    barrier = pltpu.get_barrier_semaphore()
    for peer in peers:
        pl.semaphore_signal(barrier, inc=1, device_id=(peer,), device_id_type=MESH)
    pl.semaphore_wait(barrier, len(peers))


def finish_kernel(visible, first, second, extra, loss, up, out, qkv, down,
                  cells, gain_one, shift_one, gain_two, shift_two, bias, loss_out, up_out, out_out, qkv_out, down_out):
    step = pl.program_id(0)
    images = visible.shape[1]
    for source, target in ((up, up_out), (out, out_out), (qkv, qkv_out), (down, down_out)):
        target[...] = source[...]

    @pl.when(step == 0)
    def _():
        rows = extra.shape[0]
        lines = jnp.concatenate([extra[...], jnp.zeros((128 - rows, 128), f32)]).T
        for number, target in enumerate((gain_one, shift_one, gain_two, shift_two)):
            target[...] = lines[number : number + 1, 0:rows]
        bias[...] = jnp.concatenate([lines[4 + k : 5 + k, 0:rows] for k in range(4)], axis=1)
        loss_out[...] = loss[...]

    patch_count, slots = cells.shape[1], visible.shape[2]
    seen = visible[step // images, pl.ds(step % images, 1), :]
    picked = jnp.where(lax.broadcasted_iota(jnp.int32, (patch_count, slots), 0) == seen, 1.0, 0.0).astype(bf16)
    for modality, grads in enumerate((first, second)):
        value = grads[0]
        high = value.astype(bf16)
        rest = value - high.astype(f32)
        middle = rest.astype(bf16)
        lowest = (rest - middle.astype(f32)).astype(bf16)
        cells[0, :, modality, :] = dot(picked, high) + dot(picked, middle) + dot(picked, lowest)


def finish(visible, grads, patch_count, extra, loss, passed):
    total, slots, width = grads.shape
    images = total // 2
    rows = extra.shape[0]
    whole = pl.BlockSpec(memory_space=pltpu.VMEM)
    pieces = [pl.BlockSpec((rows, width), lambda i: (0, i)), pl.BlockSpec((rows, width), lambda i: (0, 0)),
              pl.BlockSpec((rows, width), lambda i: (0, jnp.minimum(i, 2))), pl.BlockSpec((1, rows, width), lambda i: (i // 2, i % 2, 0))]
    return pl.pallas_call(
        finish_kernel,
        grid=(images,),
        in_specs=[whole, pl.BlockSpec((1, slots, width), lambda i: (i, 0, 0)), pl.BlockSpec((1, slots, width), lambda i: (images + i, 0, 0)), whole, whole]
        + pieces,
        out_specs=[pl.BlockSpec((1, patch_count, 2, width), lambda i: (i, 0, 0, 0))] + [whole] * 6 + pieces,
        out_shape=[jax.ShapeDtypeStruct((images, patch_count, 2, width), f32)] + [jax.ShapeDtypeStruct((1, rows), f32)] * 4
        + [jax.ShapeDtypeStruct((1, 4 * rows), f32), jax.ShapeDtypeStruct((1, 1), f32)] + [jax.ShapeDtypeStruct(one.shape, f32) for one in passed],
        compiler_params=pltpu.CompilerParams(vmem_limit_bytes=62 << 20),
    )(visible, grads, grads, extra, loss, *passed)


def backward_kernel(own, grad_rows, first_active, masks, gain_one, gain_two, got, grad_all, tokens, one_t, packed, probs, att_t, mixed, two_t, slope,
                    w_qkv, w_out, w_up, w_down,
                    up_out, out_out, qkv_out, extra_out, tokens_out, down_out,
                    mine, ring, core_got, first_got, second_got, owner_got,
                    extra, extra_mine, extra_core, extra_first, extra_second, extra_owner,
                    wide, mixed_grad, mixed_low, turned, weights, active_grad, sums, packs, shares, rows_in, rows_out, hidden_grad,
                    sems, extra_sems, wsem, dsem, tsem, psem, rsem, osem):
    me = lax.axis_index("dp")
    core, xx, yy, zz = me % 2, (me // 2) % 2, (me // 4) % 2, me // 8
    kind, low_z = zz % 2, zz // 2
    slots, width = mixed.shape[1:]
    ff = slope.shape[2]
    both = 2 * own
    pairs = 2 * ff // width
    up_pairs = ff // width

    def load_slope(place, count, j):
        at = pl.ds(pl.multiple_of(j * width, 128), width)
        return pltpu.make_async_copy(slope.at[pl.ds(place, count), :, at], wide.at[pl.ds(0, count), :, at], dsem.at[j])

    def load_down(which, j):
        at = pl.ds(pl.multiple_of(j * width, 128), width)
        return pltpu.make_async_copy(w_down.at[which, at, :], weights.at[1, :, at], wsem.at[j])

    def load_up(which):
        return pltpu.make_async_copy(w_up.at[which], weights.at[0], wsem.at[4])

    def load_rest(which):
        return (pltpu.make_async_copy(w_qkv.at[which], weights.at[1, :, pl.ds(0, 3 * width)], wsem.at[5]),
                pltpu.make_async_copy(w_out.at[which], weights.at[1, :, pl.ds(3 * width, width)], wsem.at[6]))

    def load_turned(source, slot, image, part):
        return pltpu.make_async_copy(
            source.at[image, :, part], turned.at[slot, part, :, :, pl.ds(pl.multiple_of(image * slots, 128), slots)], tsem.at[slot, part, image])

    def all_turned(source, slot, act):
        def one(image, carry):
            for part in (0, 1):
                act(load_turned(source, slot, image, part))
            return carry

        lax.fori_loop(0, both, one, 0)

    def begin(copy):
        copy.start()

    def finish(copy):
        copy.wait()

    load_slope(0, both, 0).start()
    all_turned(two_t, 0, begin)
    for j in range(1, up_pairs):
        load_slope(0, both, j).start()
    load_up(kind).start()
    all_turned(att_t, 1, begin)
    for copy in load_rest(kind):
        copy.start()

    meet([me ^ 1, me ^ 2, me ^ 4, me ^ 8, me ^ 16, me ^ 24])

    def sem(stage, chunk, way):
        return sems.at[stage, chunk, way]

    def chunk_sem(chunk, stage, way):
        return sems.at[stage, chunk, way]

    def extra_sem(stage, way):
        return extra_sems.at[stage, way]

    def remote(src, dst, send, recv, flip):
        return pltpu.make_async_remote_copy(src_ref=src, dst_ref=dst, send_sem=send, recv_sem=recv, device_id=(me ^ flip,), device_id_type=MESH)

    def to_core(chunk):
        return remote(ring.at[(chunk // 2) % 2, chunk % 2], core_got.at[chunk], sem(1, chunk, 0), sem(1, chunk, 1), 1)

    def first(chunk, along_x):
        src = mine.at[chunk, :, :, 1 - xx] if along_x else mine.at[chunk, :, 1 - yy]
        return remote(src, first_got.at[chunk], sem(2, chunk, 0), sem(2, chunk, 1), 2 if along_x else 4)

    def second(chunk, along_x):
        src = mine.at[chunk, :, 1 - yy, xx] if along_x else mine.at[chunk, :, yy, 1 - xx]
        return remote(src, second_got.at[chunk], sem(3, chunk, 0), sem(3, chunk, 1), 4 if along_x else 2)

    def third(source, owner, send, recv, half):
        target = 2 * kind + half
        return target, pltpu.make_async_remote_copy(
            src_ref=source.at[half, yy, xx], dst_ref=owner.at[low_z], send_sem=send, recv_sem=recv,
            device_id=(target * 8 + me % 8,), device_id_type=MESH)

    def start_third(source, owner, semaphore):
        for half in (0, 1):
            target, copy = third(source, owner, semaphore(4, half), semaphore(5, low_z), half)

            @pl.when(target != zz)
            def _():
                copy.start()

            @pl.when(target == zz)
            def _():
                owner[low_z] = source[half, yy, xx]

    def wait_third(source, owner, semaphore):
        for half in (0, 1):
            target, copy = third(source, owner, semaphore(4, half), semaphore(5, low_z), half)

            @pl.when(target != zz)
            def _():
                copy.wait_send()

        for origin in (0, 1):
            @pl.when(2 * origin + low_z != zz)
            def _():
                remote(source.at[0, yy, xx], owner.at[origin], semaphore(4, 0), semaphore(5, origin), 8).wait_recv()

    def run_first(pair):
        for odd in (0, 1):
            chunk = 2 * pair + odd
            to_core(chunk).wait_recv()
            mine[chunk] = mine[chunk] + core_got[chunk]
            first(chunk, odd == 0).start()

    def run_second(pair):
        for odd in (0, 1):
            chunk = 2 * pair + odd
            first(chunk, odd == 0).wait()
            if odd == 0:
                mine[chunk, :, :, xx] = mine[chunk, :, :, xx] + first_got[chunk]
            else:
                mine[chunk, :, yy] = mine[chunk, :, yy] + first_got[chunk]
            second(chunk, odd == 0).start()

    def run_third(pair):
        for odd in (0, 1):
            chunk = 2 * pair + odd
            second(chunk, odd == 0).wait()
            mine[chunk, :, yy, xx] = mine[chunk, :, yy, xx] + second_got[chunk]
            start_third(mine.at[chunk], owner_got.at[chunk], functools.partial(chunk_sem, chunk))

    def write(chunk, target, base):
        at = pl.ds(pl.multiple_of((chunk - 2 * base) * CHUNK, 128), CHUNK)
        return pltpu.make_async_copy(owner_got.at[chunk, 0], target.at[:, at], sem(0, chunk, 0))

    outputs = ((up_out, 0, up_pairs), (out_out, up_pairs, up_pairs + 1), (qkv_out, up_pairs + 1, pairs))

    def run_last(target, base, pair):
        for odd in (0, 1):
            chunk = 2 * pair + odd
            wait_third(mine.at[chunk], owner_got.at[chunk], functools.partial(chunk_sem, chunk))
            owner_got[chunk, 0] = owner_got[chunk, 0] + owner_got[chunk, 1]
            write(chunk, target, base).start()

    def serve(run, low, high):
        def one(pair, carry):
            run(pair)
            return carry

        lax.fori_loop(low, high, one, 0)

    def terms(pair, slot, block, reused=True):
        if reused:
            for odd in (0, 1):
                to_core(2 * (pair - 2) + odd).wait_send()
        for part, row_half in ((0, core), (1, 1 - core)):
            left = turned[slot, row_half].reshape(8 * 48, both * slots)
            if block is None:
                right = mixed_low[...]
            else:
                right = wide[:, :, pl.ds(pl.multiple_of(block * width, 128), width)]
            got = dot(left, right.reshape(both * slots, width))
            for odd in (0, 1):
                piece = got[:, odd * CHUNK : odd * CHUNK + CHUNK].reshape(2, 2, 2, 48, CHUNK)
                if part == 0:
                    mine[2 * pair + odd] = piece
                else:
                    ring[pair % 2, odd] = piece
        for odd in (0, 1):
            to_core(2 * pair + odd).start()

    lanes = lax.broadcasted_iota(jnp.int32, (slots, 128), 1)

    def mask_of(place):
        return jnp.sum(jnp.where(lanes == place, masks[...], 0.0), axis=1, keepdims=True)

    def make_active_grad(first_row, which):
        low = grad_rows[first_row : first_row + 16].astype(bf16)
        for j in range(up_pairs):
            load_down(which, j).wait()
            active_grad[:, j * width : (j + 1) * width] = dot_nt(low, weights[1, :, j * width : (j + 1) * width])
        for copy in load_rest(which):
            copy.start()

    def upper_grad(j, place, count):
        at = pl.ds(pl.multiple_of(j * width, 128), width)
        load_slope(place, count, j).wait()

        def one(image, carry):
            row = active_grad[pl.ds(image, 1), at]
            weight = mask_of(place + image)
            for r in range(0, slots, ROWS):
                value = wide[image, r : r + ROWS, at].astype(f32) * (row * weight[r : r + ROWS])
                wide[image, r : r + ROWS, at] = value.astype(bf16)
            return carry

        lax.fori_loop(0, count, one, 0)

    active_grad[...] = first_active[...]
    all_turned(two_t, 0, finish)
    ones = jnp.full((128, both * slots), 1.0, bf16)

    def up_pair(j, carry):
        upper_grad(j, 0, both)

        @pl.when(j >= 2)
        def _():
            for odd in (0, 1):
                to_core(2 * (j - 2) + odd).wait_send()

        right = wide[:, :, pl.ds(pl.multiple_of(j * width, 128), width)].reshape(both * slots, width)
        terms(j, 0, j, False)

        @pl.when((j >= 1) & (j <= 2))
        def _():
            run_first(j - 1)

        bias = dot(ones, right).T.reshape(4, 4, 48, 128)
        lane = lax.broadcasted_iota(jnp.int32, (4, 48, 128), 2)
        spread = jnp.zeros((4, 48, 128), f32)
        for k in range(4):
            spread = spread + jnp.where(lane == 4 + k, bias[:, k], 0.0)
        extra[j // 2, j % 2] = spread.reshape(2, 2, 48, 128)
        return carry

    lax.fori_loop(0, up_pairs, up_pair, 0)
    sums[...] = jnp.zeros_like(sums)

    def hidden_two_back(count):
        def one(k, carry):
            flat = wide[0:count].reshape(count * slots, ff)
            at = pl.ds(pl.multiple_of(k * 256, 256), 256)
            mixed_grad[0:count, :, at] = dot_nt(flat, weights[0, at, :]).reshape(count, slots, 256)
            return carry

        lax.fori_loop(0, width // 256, one, 0)

    def norm_back(rows, grad, gain):
        normed, inverse = row_norm(rows)
        scaled = grad * gain
        back = inverse * (scaled - jnp.mean(scaled, axis=-1, keepdims=True) - normed * jnp.mean(scaled * normed, axis=-1, keepdims=True))
        return normed, back

    def run_hooks(hooks, at):
        for when, act in (hooks or {}).items():
            @pl.when(at == when)
            def _():
                act()

    def fold(values):
        return jnp.sum(values.reshape(ROWS // 8, 8, width), axis=0)

    def norm_two_back(place, count, keep, hooks=None):
        gain = gain_two[pl.ds(kind if keep else 1 - kind, 1), :]

        def load(image):
            return pltpu.make_async_copy(mixed.at[place + image], rows_in.at[image % 2], rsem.at[image % 2])

        load(0).start()

        def one(image, carry):
            @pl.when(image + 1 < count)
            def _():
                load(image + 1).start()

            load(image).wait()
            weight = mask_of(place + image)
            grad_row = grad_rows[pl.ds(place + image, 1), :]
            held, first_sum, second_sum = [], 0.0, 0.0
            for r in range(0, slots, ROWS):
                grad = mixed_grad[image, r : r + ROWS, :]
                normed, back = norm_back(rows_in[image % 2, r : r + ROWS, :], grad, gain)
                value = weight[r : r + ROWS] * grad_row + back
                mixed_low[image, r : r + ROWS, :] = value.astype(bf16)
                held.append(value)
                if keep:
                    first_sum = first_sum + fold(grad * normed)
                    second_sum = second_sum + fold(grad)
            mixed_grad[image] = jnp.concatenate(held)
            if keep:
                sums[2] = sums[2] + first_sum
                sums[3] = sums[3] + second_sum
            run_hooks(hooks, image)
            return carry

        lax.fori_loop(0, count, one, 0)

    def attended_back(count):
        for k in range(0, width, 256):
            flat = mixed_low[0:count].reshape(count * slots, width)
            got = dot_nt(flat, weights[1, k : k + 256, 3 * width : 4 * width])
            wide[0:count, :, 3 * width + k : 3 * width + k + 256] = got.astype(bf16).reshape(count, slots, 256)

    low_half = lax.broadcasted_iota(jnp.int32, (slots, 128), 1) < HEAD_DIM

    def attention_back(place, count, hooks=None):
        def load(image):
            return (pltpu.make_async_copy(packed.at[place + image], packs.at[image % 2], psem.at[0, image % 2]),
                    pltpu.make_async_copy(probs.at[place + image], shares.at[image % 2], psem.at[1, image % 2]))

        for copy in load(0):
            copy.start()

        def one(image, carry):
            @pl.when(image + 1 < count)
            def _():
                for copy in load(image + 1):
                    copy.start()

            for copy in load(image):
                copy.wait()
            now = image % 2
            for pair in range(HEADS // 2):
                at = slice(pair * 128, pair * 128 + 128)
                queries = packs[now, :, pair * 128 : pair * 128 + 128]
                keys = packs[now, :, width + pair * 128 : width + pair * 128 + 128]
                values = packs[now, :, 2 * width + pair * 128 : 2 * width + pair * 128 + 128]
                grad = wide[image, :, 3 * width + pair * 128 : 3 * width + pair * 128 + 128]
                share = shares[now, pair]
                blank = jnp.zeros_like(keys)
                two_keys = jnp.concatenate([jnp.where(low_half, keys, blank), jnp.where(low_half, blank, keys)])
                two_values = jnp.concatenate([jnp.where(low_half, values, blank), jnp.where(low_half, blank, values)])
                grad_share = dot_nt(two_values, grad)
                backs = []
                for side in (0, 1):
                    part = slice(side * slots, side * slots + slots)
                    weight = share[part].astype(f32)
                    product = weight * grad_share[part]
                    backs.append((product - weight * jnp.sum(product, axis=0, keepdims=True)).astype(bf16))
                back = jnp.concatenate(backs)
                grad_values = dot(share, grad)
                grad_keys = dot(back, queries) * head_scale
                grad_queries = dot_tn(back, two_keys) * head_scale
                wide[image, :, pair * 128 : pair * 128 + 128] = grad_queries.astype(bf16)
                wide[image, :, width + pair * 128 : width + pair * 128 + 128] = jnp.where(low_half, grad_keys[:slots], grad_keys[slots:]).astype(bf16)
                wide[image, :, 2 * width + pair * 128 : 2 * width + pair * 128 + 128] = jnp.where(low_half, grad_values[:slots], grad_values[slots:]).astype(bf16)
            run_hooks(hooks, image)
            return carry

        lax.fori_loop(0, count, one, 0)

    def norm_one_back(place, count, keep, out_place, out_count, hooks=None):
        gain = gain_one[pl.ds(kind if keep else 1 - kind, 1), :]

        def load(step):
            return pltpu.make_async_copy(tokens.at[pl.ds(place + 2 * step, 2)], rows_in, rsem.at[0])

        def store(step):
            return pltpu.make_async_copy(rows_out, tokens_out.at[pl.ds(out_place + 2 * step, 2)], osem.at[0])

        load(0).start()

        def one(step, carry):
            flat = wide[pl.ds(2 * step, 2), :, 0 : 3 * width].reshape(2 * slots, 3 * width)
            hidden_grad[...] = dot_nt(flat, weights[1, :, 0 : 3 * width])
            load(step).wait()

            @pl.when((step >= 1) & (step - 1 < out_count // 2))
            def _():
                store(step - 1).wait()

            for side in (0, 1):
                first_sum, second_sum = 0.0, 0.0
                for r in range(0, slots, ROWS):
                    grad = hidden_grad[side * slots + r : side * slots + r + ROWS, :]
                    normed, back = norm_back(rows_in[side, r : r + ROWS, :], grad, gain)
                    rows_out[side, r : r + ROWS, :] = mixed_grad[2 * step + side, r : r + ROWS, :] + back
                    if keep:
                        first_sum = first_sum + fold(grad * normed)
                        second_sum = second_sum + fold(grad)
                if keep:
                    sums[0] = sums[0] + first_sum
                    sums[1] = sums[1] + second_sum

            @pl.when(step + 1 < count // 2)
            def _():
                load(step + 1).start()

            @pl.when(step < out_count // 2)
            def _():
                store(step).start()

            run_hooks(hooks, step)
            return carry

        lax.fori_loop(0, count // 2, one, 0)
        if count == out_count:
            store(count // 2 - 1).wait()

    def serving(*jobs):
        def act():
            for run, pair in jobs:
                run(pair)
        return act

    def step(k):
        run_second(k)
        if k + 2 < pairs:
            run_first(k + 2)
        if k >= 1:
            run_third(k - 1)

    step(0)
    load_up(kind).wait()
    hidden_two_back(both)
    load_up(1 - kind).start()
    all_turned(one_t, 0, begin)
    norm_two_back(0, both, True, {6: lambda: step(1)})
    all_turned(att_t, 1, finish)
    terms(up_pairs, 1, None)
    for copy in load_rest(kind):
        copy.wait()
    attended_back(both)
    attention_back(0, both, {5: lambda: step(2)})
    all_turned(one_t, 0, finish)
    for j in range(2):
        terms(up_pairs + 1 + j, 0, j)
    step(3)
    terms(pairs - 1, 0, 2)
    norm_one_back(0, both, True, kind * own, own)

    vectors = jnp.concatenate([jnp.sum(sums[k], axis=0, keepdims=True) for k in range(4)] + [jnp.zeros((124, width), f32)])
    extra[...] = extra[...] + vectors.T.reshape(extra.shape)
    extra_mine[...] = extra[:, :, :, core]
    extra_to_core = remote(extra.at[:, :, :, 1 - core], extra_core, extra_sems.at[1, 0], extra_sems.at[1, 1], 1)
    extra_first_copy = remote(extra_mine.at[:, :, 1 - xx], extra_first, extra_sems.at[2, 0], extra_sems.at[2, 1], 2)
    extra_second_copy = remote(extra_mine.at[:, 1 - yy, xx], extra_second, extra_sems.at[3, 0], extra_sems.at[3, 1], 4)
    extra_to_core.start()

    for j in range(up_pairs):
        load_slope(both, own, j).start()
        load_down(1 - kind, j).start()
    make_active_grad(both, 1 - kind)

    def other_pair(j, carry):
        upper_grad(j, both, own)
        return carry

    lax.fori_loop(0, up_pairs, other_pair, 0)
    step(4)
    extra_to_core.wait()
    extra_mine[...] = extra_mine[...] + extra_core[...]
    extra_first_copy.start()
    load_up(1 - kind).wait()
    hidden_two_back(own)
    norm_two_back(both, own, False)
    for copy in load_rest(1 - kind):
        copy.wait()
    attended_back(own)
    attention_back(both, own)
    step(5)
    extra_first_copy.wait()
    extra_mine[:, :, xx] = extra_mine[:, :, xx] + extra_first[...]
    extra_second_copy.start()
    norm_one_back(both, own, False, (1 - kind) * own, own)

    reads = [pltpu.make_async_copy(grad_all.at[pl.ds(part * slots, slots), :], rows_in.at[part], rsem.at[part]) for part in (0, 1)]
    reads += [pltpu.make_async_copy(got.at[pl.ds(part * slots, slots), :], rows_out.at[part, :, pl.ds(0, CHUNK)], osem.at[part]) for part in (0, 1)]
    for copy in reads:
        copy.start()
    for copy in reads:
        copy.wait()
    sums_all = rows_out[:, :, 0:CHUNK].reshape(2 * slots, CHUNK)
    down = lax.dot_general(sums_all, rows_in[...].reshape(2 * slots, width), (((0,), (0,)), ((), ())), precision=highest, preferred_element_type=f32)
    half = CHUNK // 2
    mixed_grad[0:2, 0 : half // 2, :] = jnp.where(core == 0, down[:half], down[half:]).reshape(2, half // 2, width)
    write_down = pltpu.make_async_copy(mixed_grad.at[pl.ds(0, 2), pl.ds(0, half // 2), :], down_out, wsem.at[3])
    write_down.start()
    step(6)
    step(7)
    run_third(7)
    for chunk in range(2 * pairs - 4, 2 * pairs):
        to_core(chunk).wait_send()
    extra_second_copy.wait()
    extra_mine[:, yy, xx] = extra_mine[:, yy, xx] + extra_second[...]
    start_third(extra_mine, extra_owner, extra_sem)
    for target, low, high in outputs:
        serve(functools.partial(run_last, target, low), low, high)
    wait_third(extra_mine, extra_owner, extra_sem)
    extra_out[...] = extra_owner[0] + extra_owner[1]
    for target, low, high in outputs:
        for chunk in range(2 * low, 2 * high):
            write(chunk, target, low).wait()
    write_down.wait()


def backward(own, grad_rows, first_active, masks, got, grad_all, tokens, saved, weights):
    gain_one, shift_one, w_qkv, w_out, gain_two, shift_two, w_up, b_up, w_down = weights
    slots, width = tokens.shape[1:]
    ff = w_up.shape[2]
    both = 2 * own
    chunks = 2 * ff // CHUNK
    one_t, packed, probs, att_t, mixed, two_t, slope = saved
    split = lambda one: one.reshape(one.shape[0], 8, 2, one.shape[2], one.shape[3])
    anywhere, vmem = pl.BlockSpec(memory_space=pl.ANY), pl.BlockSpec(memory_space=pltpu.VMEM)
    return pl.pallas_call(
        functools.partial(backward_kernel, own),
        out_shape=(
            jax.ShapeDtypeStruct((48, ff), f32), jax.ShapeDtypeStruct((48, width), f32), jax.ShapeDtypeStruct((48, 3 * width), f32),
            jax.ShapeDtypeStruct((48, 128), f32), jax.ShapeDtypeStruct((both, slots, width), f32),
            jax.ShapeDtypeStruct((2, CHUNK // 4, width), f32),
        ),
        in_specs=[vmem] * 5 + [anywhere] * 14,
        out_specs=(anywhere, anywhere, anywhere, vmem, anywhere, anywhere),
        scratch_shapes=[
            pltpu.VMEM((chunks, 2, 2, 2, 48, CHUNK), f32),
            pltpu.VMEM((2, 2, 2, 2, 2, 48, CHUNK), f32),
            pltpu.VMEM((chunks, 2, 2, 2, 48, CHUNK), f32),
            pltpu.VMEM((chunks, 2, 2, 48, CHUNK), f32),
            pltpu.VMEM((chunks, 2, 48, CHUNK), f32),
            pltpu.VMEM((chunks, 2, 48, CHUNK), f32),
            pltpu.VMEM((2, 2, 2, 2, 48, 128), f32),
            pltpu.VMEM((2, 2, 2, 48, 128), f32),
            pltpu.VMEM((2, 2, 2, 48, 128), f32),
            pltpu.VMEM((2, 2, 48, 128), f32),
            pltpu.VMEM((2, 48, 128), f32),
            pltpu.VMEM((2, 48, 128), f32),
            pltpu.VMEM((both, slots, ff), bf16),
            pltpu.VMEM((both, slots, width), f32),
            pltpu.VMEM((both, slots, width), bf16),
            pltpu.VMEM((2, 2, 8, 48, both * slots), bf16),
            pltpu.VMEM((2, width, ff), bf16),
            pltpu.VMEM((16, ff), f32),
            pltpu.VMEM((4, 8, width), f32),
            pltpu.VMEM((2, slots, 3 * width), bf16),
            pltpu.VMEM((2, HEADS // 2, 2 * slots, slots), bf16),
            pltpu.VMEM((2, slots, width), f32),
            pltpu.VMEM((2, slots, width), f32),
            pltpu.VMEM((2 * slots, width), f32),
            pltpu.SemaphoreType.DMA((6, chunks, 2)),
            pltpu.SemaphoreType.DMA((6, 2)),
            pltpu.SemaphoreType.DMA((7,)),
            pltpu.SemaphoreType.DMA((4,)),
            pltpu.SemaphoreType.DMA((2, 2, both)),
            pltpu.SemaphoreType.DMA((2, 2)),
            pltpu.SemaphoreType.DMA((2,)),
            pltpu.SemaphoreType.DMA((2,)),
        ],
        compiler_params=pltpu.CompilerParams(collective_id=1, has_side_effects=True, vmem_limit_bytes=63 << 20),
    )(grad_rows, first_active, masks, gain_one, gain_two, got.reshape(-1, CHUNK), grad_all, tokens, split(one_t), packed, probs, split(att_t), mixed, split(two_t), slope,
      w_qkv, w_out, w_up, w_down)


def tokens_of(patches, visible, modality):
    micro_count, images, _, patch_count, width = patches.shape
    cells = lax.dynamic_index_in_dim(patches, modality, 2, keepdims=False).reshape(micro_count * images, patch_count, width)
    picked = (visible[:, :, None] == jnp.arange(patch_count)[None, None, :]).astype(bf16)
    return jnp.einsum("isp,ipd->isd", picked, cells, preferred_element_type=f32)


def cells_of(grad_tokens, visible, patch_count):
    picked = (visible[:, None, :] == jnp.arange(patch_count)[None, :, None]).astype(f32)
    return jnp.einsum("ips,isd->ipd", picked, grad_tokens, precision=highest)


def on_tuned(patches, visible, valid_mask, weights):
    n = lax.axis_size("dp")
    micro_count, images, _, patch_count, width = patches.shape
    own = micro_count * images
    loss, grad_all, got, grad_rows, active_grad, masks, tokens, *saved = forward(
        n, visible, valid_mask, patches.reshape(own, 2, patch_count, width), weights)
    up, out, qkv, extra, grad_tokens, down = backward(own, grad_rows, active_grad, masks, got, grad_all, tokens, saved, weights)
    cells, gain_one, shift_one, gain_two, shift_two, bias, loss, up, out, qkv, down = finish(
        visible, grad_tokens, patch_count, extra, loss, (up, out, qkv, down))
    patches_grad = cells.reshape(micro_count, images, patch_count, 2, width).transpose(0, 1, 3, 2, 4)
    vector = lambda one: one.reshape(-1)
    return (loss.reshape(()), patches_grad, vector(gain_one), vector(shift_one), qkv, out, vector(gain_two), vector(shift_two), up,
            vector(bias), down.reshape(-1, width))


def on_plain(patches, visible, valid_mask, weights):
    n = lax.axis_size("dp")
    me = lax.axis_index("dp")
    micro_count, images, _, patch_count, width = patches.shape
    own = micro_count * images
    slots = visible.shape[-1]
    ff = weights[6].shape[2]
    seen = visible.reshape(own, slots)
    mask = valid_mask.reshape(own, slots)
    outcomes = []
    for modality in (0, 1):
        params = params_of(weights, modality)
        outcomes.append((params,) + encode_forward(tokens_of(patches, seen, modality), seen, mask, params))
    pooled = jnp.concatenate([pool(active, mixed, mask, params[8]) for params, active, mixed, _ in outcomes])
    counted = jnp.sum(mask.astype(f32), axis=1)[:, None]
    shares = jnp.stack([active / counted for _, active, _, _ in outcomes])
    down_rows = 2 * ff // n
    shares = shares.reshape(2, own, n // 2, down_rows).transpose(0, 2, 1, 3).reshape(n, own * down_rows)
    loss, grad_all = contrast(lax.all_gather(pooled, "dp", axis=0, tiled=True), 2 * own, micro_count)
    got = lax.all_to_all(shares, "dp", 0, 0, tiled=True)
    grad_all = grad_all.reshape(n, 2, own, width)
    grad_down = jnp.einsum(
        "iw,id->wd", got.reshape(n * own, down_rows),
        lax.dynamic_index_in_dim(grad_all, me // (n // 2), 1, keepdims=False).reshape(n * own, width), precision=highest)
    mine = lax.dynamic_index_in_dim(grad_all, me, 0, keepdims=False)
    backs = [encode_backward(mine[m], outcomes[m][3], mask, outcomes[m][0]) for m in (0, 1)]
    patches_grad = jnp.stack([cells_of(back[0], seen, patch_count) for back in backs], 1).reshape(patches.shape)
    joined = jax.tree.map(lambda a, b: jnp.concatenate([a, b]), backs[0][1], backs[1][1])
    shards = tuple(lax.psum_scatter(one, "dp", scatter_dimension=0, tiled=True) for one in joined)
    return (loss[0, 0], patches_grad) + shards + (grad_down,)


def solution(mesh):
    in_specs = (P(None, "dp"), P(None, "dp"), P(None, "dp")) + (P(),) * 9
    out_specs = (P(), P(None, "dp")) + (P("dp"),) * 9

    def on_device(patches, visible, valid_mask, *weights):
        run = on_tuned if lax.axis_size("dp") == 32 else on_plain
        return run(patches, visible, valid_mask, weights)

    return jax.shard_map(on_device, mesh=mesh, in_specs=in_specs, out_specs=out_specs, check_vma=False)
```

```python
import functools
import math

import jax
import jax.numpy as jnp
from jax import lax
from jax.experimental import pallas as pl
from jax.experimental.pallas import tpu as pltpu
from jax.sharding import PartitionSpec as P

HEADS = 12
HEAD_DIM = 64
GRID = 15
MESH = pl.DeviceIdType.MESH

norm_epsilon = 1e-06
unit_epsilon = 1e-06
logit_scale = 100.0
masked_score = -1e30
highest = lax.Precision.HIGHEST
head_scale = 1.0 / math.sqrt(HEAD_DIM)
f32 = jnp.float32
bf16 = jnp.bfloat16


def exact_gelu(values_in):
    return jax.nn.gelu(values_in, approximate=False)


def layer_norm(values_in, gain_vec, shift_vec):
    centre = values_in - jnp.mean(values_in, axis=-1, keepdims=True)
    inverse = lax.rsqrt(jnp.mean(centre * centre, axis=-1, keepdims=True) + norm_epsilon)
    normed = centre * inverse
    return (normed * gain_vec + shift_vec, normed, inverse)


def norm_back(grad_out, normed, inverse, gain_vec):
    grad_normed = grad_out * gain_vec
    mean_plain = jnp.mean(grad_normed, axis=-1, keepdims=True)
    mean_normed = jnp.mean(grad_normed * normed, axis=-1, keepdims=True)
    grad_in = inverse * (grad_normed - mean_plain - normed * mean_normed)
    return (grad_in, jnp.sum(grad_out * normed, axis=0), jnp.sum(grad_out, axis=0))


def alibi_bias(visible_rows):
    rows_pos = (visible_rows // GRID).astype(f32)
    cols_pos = (visible_rows % GRID).astype(f32)
    rows_gap = rows_pos[:, :, None] - rows_pos[:, None, :]
    cols_gap = cols_pos[:, :, None] - cols_pos[:, None, :]
    distance = jnp.sqrt(rows_gap * rows_gap + cols_gap * cols_gap)
    slopes = jnp.exp2(-8.0 * (jnp.arange(HEADS, dtype=f32) + 1.0) / HEADS)
    return -slopes[None, :, None, None] * distance[:, None, :, :]


def split_heads(packed):
    images, slot_count, _ = packed.shape
    shaped = packed.reshape(images, slot_count, 3, HEADS, HEAD_DIM)
    return (shaped[:, :, 0], shaped[:, :, 1], shaped[:, :, 2])


def encode_forward(tokens_in, visible_rows, mask_rows, params):
    gain_one, shift_one, w_qkv, w_out, gain_two, shift_two, w_up, b_up, w_down = params
    images, slots, width = tokens_in.shape
    flat_in = tokens_in.reshape(images * slots, width)
    hidden_one, normed_one, inverse_one = layer_norm(flat_in, gain_one, shift_one)
    hidden_one = hidden_one.astype(bf16)
    packed = jnp.dot(hidden_one, w_qkv, preferred_element_type=f32).astype(bf16)
    packed = packed.reshape(images, slots, 3 * width)
    queries, keys, values = split_heads(packed)
    scores = jnp.einsum("iqhd,ikhd->ihqk", queries, keys, preferred_element_type=f32)
    scores = scores * head_scale + alibi_bias(visible_rows)
    scores = jnp.where((mask_rows > 0)[:, None, None, :], scores, masked_score)
    attention = jax.nn.softmax(scores, axis=-1)
    attended = jnp.einsum("ihqk,ikhd->iqhd", attention.astype(bf16), values, preferred_element_type=f32)
    attended = attended.reshape(images * slots, width).astype(bf16)
    mixed = flat_in + jnp.dot(attended, w_out, preferred_element_type=f32)
    hidden_two, normed_two, inverse_two = layer_norm(mixed, gain_two, shift_two)
    hidden_two = hidden_two.astype(bf16)
    upper = jnp.dot(hidden_two, w_up, preferred_element_type=f32) + b_up
    active, gelu_back = jax.vjp(exact_gelu, upper)
    active = active.astype(bf16).astype(f32)
    weight = mask_rows.astype(f32)
    active_sum = jnp.sum(active.reshape(images, slots, -1) * weight[:, :, None], axis=1)
    mixed_sum = jnp.sum(mixed.reshape(images, slots, width) * weight[:, :, None], axis=1)
    saved = (normed_one, inverse_one, hidden_one, packed, attention, attended, normed_two, inverse_two, hidden_two, gelu_back)
    return active_sum, mixed_sum, saved


def pool(active_sum, mixed_sum, mask_rows, w_down):
    counted = jnp.sum(mask_rows.astype(f32), axis=1)[:, None]
    down = jnp.dot(active_sum, w_down.astype(f32), precision=highest)
    return (mixed_sum + down) / counted


def encode_backward(grad_pooled, saved, mask_rows, params):
    normed_one, inverse_one, hidden_one, packed, attention, attended, normed_two, inverse_two, hidden_two, gelu_back = saved
    gain_one, shift_one, w_qkv, w_out, gain_two, shift_two, w_up, b_up, w_down = params
    images, slots, three_width = packed.shape
    width = three_width // 3
    rows = images * slots
    weight = mask_rows.astype(f32)
    counted = jnp.sum(weight, axis=1)[:, None]
    grad_row = grad_pooled / counted
    grad_output = (weight[:, :, None] * grad_row[:, None, :]).reshape(rows, width)
    grad_active = jnp.dot(grad_row.astype(bf16), w_down.T, preferred_element_type=f32)
    grad_active = (weight[:, :, None] * grad_active[:, None, :]).reshape(rows, -1)
    grad_upper = gelu_back(grad_active)[0].astype(bf16)
    grad_bias = jnp.sum(grad_upper.astype(f32), axis=0)
    grad_up = jnp.dot(hidden_two.T, grad_upper, preferred_element_type=f32)
    grad_hidden_two = jnp.dot(grad_upper, w_up.T, preferred_element_type=f32)
    grad_norm_two, grad_gain_two, grad_shift_two = norm_back(grad_hidden_two, normed_two, inverse_two, gain_two)
    grad_mixed = grad_output + grad_norm_two
    grad_mixed_low = grad_mixed.astype(bf16)
    grad_out = jnp.dot(attended.T, grad_mixed_low, preferred_element_type=f32)
    grad_attended = jnp.dot(grad_mixed_low, w_out.T, preferred_element_type=f32).astype(bf16)
    grad_attended = grad_attended.reshape(images, slots, HEADS, HEAD_DIM)
    queries, keys, values = split_heads(packed)
    grad_value = jnp.einsum("ihqk,iqhd->ikhd", attention.astype(bf16), grad_attended, preferred_element_type=f32)
    grad_attention = jnp.einsum("iqhd,ikhd->ihqk", grad_attended, values, preferred_element_type=f32)
    grad_scores = attention * (grad_attention - jnp.sum(attention * grad_attention, axis=-1, keepdims=True))
    grad_scores = grad_scores.astype(bf16)
    grad_query = jnp.einsum("ihqk,ikhd->iqhd", grad_scores, keys, preferred_element_type=f32) * head_scale
    grad_key = jnp.einsum("ihqk,iqhd->ikhd", grad_scores, queries, preferred_element_type=f32) * head_scale
    grad_packed = jnp.stack([grad_query, grad_key, grad_value], axis=2).astype(bf16).reshape(rows, three_width)
    grad_qkv = jnp.dot(hidden_one.T, grad_packed, preferred_element_type=f32)
    grad_hidden_one = jnp.dot(grad_packed, w_qkv.T, preferred_element_type=f32)
    grad_norm_one, grad_gain_one, grad_shift_one = norm_back(grad_hidden_one, normed_one, inverse_one, gain_one)
    grad_tokens = (grad_mixed + grad_norm_one).reshape(images, slots, width)
    return grad_tokens, (grad_gain_one, grad_shift_one, grad_qkv, grad_out, grad_gain_two, grad_shift_two, grad_up, grad_bias)


def contrast(pooled, own_rows, micro_count):
    count = pooled.shape[0]
    images = own_rows // (2 * micro_count)
    inverse = lax.rsqrt(jnp.sum(pooled * pooled, axis=-1, keepdims=True) + unit_epsilon)
    unit = pooled * inverse
    logits = logit_scale * lax.dot_general(unit, unit, (((1,), (1,)), ((), ())), precision=highest, preferred_element_type=f32)
    row = lax.broadcasted_iota(jnp.int32, (count, count), 0)
    col = lax.broadcasted_iota(jnp.int32, (count, count), 1)
    half = own_rows // 2
    row_mod, col_mod = (row // half) % 2, (col // half) % 2
    row_micro, col_micro = (row // images) % micro_count, (col // images) % micro_count
    allowed = (row_mod != col_mod) & (row_micro == col_micro)
    paired = jnp.where(col == row + half * (1 - 2 * row_mod), 1.0, 0.0)
    logits = jnp.where(allowed, logits, masked_score)
    row_max = jnp.max(logits, axis=1, keepdims=True)
    row_lse = row_max + jnp.log(jnp.sum(jnp.exp(logits - row_max), axis=1, keepdims=True))
    col_max = jnp.max(logits, axis=0, keepdims=True)
    col_lse = col_max + jnp.log(jnp.sum(jnp.exp(logits - col_max), axis=0, keepdims=True))
    scale = 1.0 / count
    diagonal = jnp.sum(jnp.where(paired > 0, logits, 0.0), axis=1, keepdims=True)
    loss = scale * jnp.sum(row_lse - diagonal, axis=0, keepdims=True)
    spread = jnp.exp(logits - row_lse) + jnp.exp(logits - col_lse) - 2.0 * paired
    grad_unit = (logit_scale * scale) * jnp.dot(spread, unit, precision=highest, preferred_element_type=f32)
    grad_pooled = inverse * (grad_unit - unit * jnp.sum(unit * grad_unit, axis=-1, keepdims=True))
    return loss, grad_pooled


def params_of(weights, modality):
    return tuple(lax.dynamic_index_in_dim(one, modality, 0, keepdims=False) for one in weights)


GROWS = 32
SLOPES = [2.0 ** (-8.0 * (head + 1) / HEADS) for head in range(HEADS)]
ROWS = 32
WIDE = 512


def gelu_pair(upper):
    size = jnp.abs(upper)
    bell = jnp.exp(-0.5 * upper * upper)
    below = 1.0 + (0.3275911 * math.sqrt(0.5)) * size
    t = pltpu.reciprocal(below, approx=True)
    t = t * (2.0 - below * t)
    tail = t * (0.5 * 0.254829592 + t * (0.5 * -0.284496736 + t * (0.5 * 1.421413741 + t * (0.5 * -1.453152027 + t * (0.5 * 1.061405429)))))
    tail = tail * bell
    normal = jnp.where(upper < 0, tail, 1.0 - tail)
    return upper * normal, normal + upper * (bell * (1.0 / math.sqrt(2.0 * math.pi)))


def row_norm(values):
    centre = values - jnp.mean(values, axis=-1, keepdims=True)
    inverse = lax.rsqrt(jnp.mean(centre * centre, axis=-1, keepdims=True) + norm_epsilon)
    return centre * inverse, inverse


def dot(a, b):
    return jnp.dot(a, b, preferred_element_type=f32)


def dot_nt(a, b):
    return lax.dot_general(a, b, (((1,), (1,)), ((), ())), preferred_element_type=f32)


def dot_tn(a, b):
    return lax.dot_general(a, b, (((0,), (0,)), ((), ())), preferred_element_type=f32)


def roll_if(flag, value):
    return jnp.where(flag == 1, jnp.concatenate([value[4:], value[:4]]), value)


def forward_kernel(n, micro_count, visible, valid_mask, gain_one, shift_one, gain_two, shift_two, b_up, patches, w_qkv, w_out, w_up, w_down,
                   loss_out, grad_out, got, grad_rows, active_grad, masks, tokens_out, one_out, packed_out, probs_out, att_out, mixed_out, two_out, slope_out,
                   cells, tok, info_in, there, wq, wo, wu, wd, one_t, packed, probs, att_t, mixed, two_t, slope, upper, active, hidden, attended, turned,
                   active_sum, share, every, send_sem, recv_sem, sum_send, sum_recv, isem, wsem, osem, tsem, xsem):
    me = lax.axis_index("dp")
    kind = (me // 8) % 2
    images, slots, width = info_in.shape[0], info_in.shape[2], tok.shape[2]
    rows = images * slots
    per_micro = visible.shape[1]
    ff = wu.shape[2]

    read_cells = pltpu.make_async_copy(patches, cells, isem)
    read_cells.start()
    reads = []
    for slot, which in ((0, kind), (1, 1 - kind)):
        reads.append([pltpu.make_async_copy(source.at[which], target.at[slot], wsem.at[slot, number])
                      for number, (source, target) in enumerate(((w_qkv, wq), (w_out, wo), (w_up, wu), (w_down, wd)))])
    for copy in reads[0] + reads[1]:
        copy.start()
    barrier = pltpu.get_barrier_semaphore()

    def greet(step, carry):
        pl.semaphore_signal(barrier, inc=1, device_id=(lax.rem(me + step, n),), device_id_type=MESH)
        return carry

    lax.fori_loop(1, n, greet, 0)

    for image in range(images):
        seen = visible[image // per_micro, image % per_micro : image % per_micro + 1, :].astype(f32)
        grid_row = jnp.floor((seen + 0.5) * (1.0 / GRID))
        valid = valid_mask[image // per_micro, image % per_micro : image % per_micro + 1, :].astype(f32)
        info_in[image] = jnp.concatenate([grid_row, seen - GRID * grid_row, valid, seen, jnp.zeros((4, slots), f32)])
    read_cells.wait()

    def pick(modality, place):
        def one(image, carry):
            seen = info_in[image, 3:4, :]
            picked = jnp.where(lax.broadcasted_iota(jnp.int32, (cells.shape[2], slots), 0).astype(f32) == seen, 1.0, 0.0).astype(bf16)
            tok[place + image] = dot_tn(picked, cells[image, modality])
            return carry

        lax.fori_loop(0, images, one, 0)

    pick(1 - kind, 2 * images)
    pl.semaphore_wait(barrier, n - 1)
    send_tokens = [
        pltpu.make_async_remote_copy(src_ref=info_in, dst_ref=there, send_sem=xsem.at[0, 0], recv_sem=xsem.at[0, 1], device_id=(me ^ 8,), device_id_type=MESH),
        pltpu.make_async_remote_copy(src_ref=tok.at[pl.ds(2 * images, images)], dst_ref=tok.at[pl.ds(images, images)],
                                     send_sem=xsem.at[1, 0], recv_sem=xsem.at[1, 1], device_id=(me ^ 8,), device_id_type=MESH)]
    for copy in send_tokens:
        copy.start()
    pick(kind, 0)

    def store_tokens(place):
        at = pl.ds(place * images, images)
        return pltpu.make_async_copy(tok.at[at], tokens_out.at[at], tsem.at[place])

    store_tokens(0).start()
    store_tokens(2).start()

    stores = {}

    def ready(number):
        if number in stores:
            stores.pop(number).wait()

    def store(number, place):
        source, target = ((one_t, one_out), (packed, packed_out), (probs, probs_out), (att_t, att_out), (mixed, mixed_out), (two_t, two_out), (slope, slope_out))[number]
        copy = pltpu.make_async_copy(source, target.at[pl.ds(place * images, images)], osem.at[number])
        copy.start()
        stores[number] = copy

    low_half = lax.broadcasted_iota(jnp.int32, (slots, 128), 1) < HEAD_DIM
    row_of = lax.broadcasted_iota(jnp.int32, (8, slots), 0)

    def marks_of(info):
        return jnp.concatenate([jnp.where(row_of == image, info[image, 2:3, :], 0.0) for image in range(images)], axis=1).astype(bf16)

    def group(place, slot, which, info, whole, pauses):
        gain1, shift1 = gain_one[pl.ds(which, 1), :], shift_one[pl.ds(which, 1), :]
        gain2, shift2 = gain_two[pl.ds(which, 1), :], shift_two[pl.ds(which, 1), :]

        def norm(source, first, target, gain, shift):
            def one(image, carry):
                for r in range(0, slots, ROWS):
                    normed, _ = row_norm(source[first + image, r : r + ROWS, :])
                    hidden[image, r : r + ROWS, :] = (normed * gain + shift).astype(bf16)
                target[image] = hidden[image].T.reshape(target.shape[1:])
                return carry

            lax.fori_loop(0, images, one, 0)

        ready(0)
        norm(tok, place * images, one_t, gain1, shift1)
        store(0, place)
        ready(1)
        if pauses is None:
            reads[slot][0].wait()

        def project(i, carry):
            at = pl.ds(pl.multiple_of(i * 768, 768), 768)
            packed[:, :, at] = dot(hidden[...].reshape(rows, width), wq[slot, :, at]).astype(bf16).reshape(images, slots, 768)
            return carry

        lax.fori_loop(0, 3 * width // 768, project, 0)
        store(1, place)
        if pauses:
            pauses[0]()
        ready(2)
        ready(3)

        def attend(image, carry):
            line = info[image]
            column = line.T
            gap_r = column[:, 0:1] - line[0:1, :]
            gap_c = column[:, 1:2] - line[1:2, :]
            away = -jnp.sqrt(gap_r * gap_r + gap_c * gap_c)
            away = jnp.where(column[:, 2:3] > 0, away, -1e33)
            for pair in range(HEADS // 2):
                at = slice(pair * 128, pair * 128 + 128)
                queries = packed[image, :, pair * 128 : pair * 128 + 128]
                keys = packed[image, :, width + pair * 128 : width + pair * 128 + 128]
                values = packed[image, :, 2 * width + pair * 128 : 2 * width + pair * 128 + 128]
                blank = jnp.zeros_like(keys)
                two_keys = jnp.concatenate([jnp.where(low_half, keys, blank), jnp.where(low_half, blank, keys)])
                two_values = jnp.concatenate([jnp.where(low_half, values, blank), jnp.where(low_half, blank, values)])
                scores = dot_nt(two_keys, queries)
                shares = []
                for side in (0, 1):
                    one = scores[side * slots : side * slots + slots] * head_scale + SLOPES[2 * pair + side] * away
                    power = jnp.exp(one - jnp.max(one, axis=0, keepdims=True))
                    shares.append((power * (1.0 / jnp.sum(power, axis=0, keepdims=True))).astype(bf16))
                both_shares = jnp.concatenate(shares)
                probs[image, pair] = both_shares
                flipped = dot_tn(two_values, both_shares).astype(bf16)
                turned[at, :] = flipped
                attended[image, :, at] = flipped.T
            att_t[image] = turned[...].reshape(att_t.shape[1:])
            return carry

        lax.fori_loop(0, images, attend, 0)
        store(2, place)
        store(3, place)
        if pauses:
            pauses[1]()
        ready(4)
        if pauses is None:
            reads[slot][1].wait()

        def output(i, carry):
            at = pl.ds(pl.multiple_of(i * 256, 256), 256)
            mixed[:, :, at] = tok[pl.ds(place * images, images), :, at] + dot(attended[...].reshape(rows, width), wo[slot, :, at]).reshape(images, slots, 256)
            return carry

        lax.fori_loop(0, width // 256, output, 0)
        store(4, place)
        ready(5)
        norm(mixed, 0, two_t, gain2, shift2)
        store(5, place)
        if pauses:
            pauses[2]()
        ready(6)
        if pauses is None:
            reads[slot][2].wait()
        marks = marks_of(info)

        def columns(i):
            return pl.ds(pl.multiple_of(i * WIDE, WIDE), WIDE)

        def rise(i, slot_up):
            upper[slot_up] = dot(hidden[...].reshape(rows, width), wu[slot, :, columns(i)])

        def bend(i, now):
            bias = b_up[pl.ds(which, 1), columns(i)]
            for r in range(0, rows, GROWS):
                value, back = gelu_pair(upper[now, r : r + GROWS, :] + bias)
                if whole:
                    active[r : r + GROWS, :] = value.astype(bf16)
                slope[r // slots, r % slots : r % slots + GROWS, columns(i)] = back.astype(bf16)
            if whole:
                active_sum[slot, :, columns(i)] = dot(marks, active[...])

        rise(0, 0)

        def feed(i, carry):
            rise(2 * i + 1, 1)
            bend(2 * i, 0)
            rise(2 * i + 2, 0)
            bend(2 * i + 1, 1)
            return carry

        steps = ff // WIDE
        lax.fori_loop(0, steps // 2 - 1, feed, 0)
        rise(steps - 1, 1)
        bend(steps - 2, 0)
        bend(steps - 1, 1)
        store(6, place)
        if not whole:
            return None
        reads[slot][3].wait()
        total = active_sum[slot]
        high = total.astype(bf16)
        rest = total - high.astype(f32)
        middle = rest.astype(bf16)
        lowest = (rest - middle.astype(f32)).astype(bf16)
        stacked = jnp.concatenate([high, middle, lowest, jnp.zeros_like(high)])
        parts = dot(stacked, wd[slot])
        downs = parts[0:8] + parts[8:16] + parts[16:24]
        sums, counts = [], []
        for image in range(images):
            weight = info[image].T[:, 2:3]
            sums.append(jnp.sum(mixed[image] * weight, axis=0, keepdims=True))
            counts.append(jnp.sum(weight, axis=0, keepdims=True))
        count = jnp.concatenate(counts + [jnp.ones((8 - images, 1), f32)])
        pooled = (jnp.concatenate(sums + [jnp.zeros((8 - images, width), f32)]) + downs) / count
        share[which] = roll_if(which, total / count)
        return roll_if(which, pooled)

    def copies(sources, flip, first):
        made = []
        for number, source in enumerate(sources):
            made.append(pltpu.make_async_remote_copy(
                src_ref=every.at[source], dst_ref=every.at[source], send_sem=send_sem.at[first + number], recv_sem=recv_sem.at[first + number],
                device_id=(me ^ flip,), device_id_type=MESH))
        for copy in made:
            copy.start()
        return made

    def finish(made):
        for copy in made:
            copy.wait()

    pooled = group(0, 0, kind, info_in, True, None)
    every[me] = pooled + group(2, 1, 1 - kind, info_in, True, None)

    waves = [copies([me], flip, number) [0] for number, flip in enumerate((8, 16, 24))]
    held = [me, me ^ 8, me ^ 16, me ^ 24]
    state = {"wave": waves, "held": held}

    def next_wave(flip, first):
        def run():
            finish(state["wave"])
            state["wave"] = copies(state["held"], flip, first)
            state["held"] = state["held"] + [one ^ flip for one in state["held"]]
        return run

    def sums_out(step, carry):
        peer = lax.rem(me + step, n)
        at = pl.ds(pl.multiple_of(((peer % (n // 2)) // 2) * 384, 384), 384)
        pltpu.make_async_remote_copy(
            src_ref=share.at[peer // (n // 2), :, at], dst_ref=got.at[me], send_sem=sum_send.at[step], recv_sem=sum_recv.at[step],
            device_id=(peer,), device_id_type=MESH).start()
        return carry

    def last_wave():
        next_wave(1, 15)()
        lax.fori_loop(1, n, sums_out, 0)

    send_tokens[0].wait()
    send_tokens[1].wait()
    store_tokens(1).start()
    group(1, 0, kind, there, False, [next_wave(4, 3), next_wave(2, 7), last_wave])
    finish(state["wave"])
    loss, grad = contrast(every[...].reshape(n * 8, width), 8, micro_count)
    loss_out[...] = loss
    grad_out[...] = grad
    got[me] = share[me // (n // 2), :, pl.ds(pl.multiple_of(((me % (n // 2)) // 2) * 384, 384), 384)]

    def per_slot(device, which, info):
        count = jnp.concatenate([jnp.sum(info[image, 2:3, :], axis=1, keepdims=True) for image in range(images)])
        return roll_if(which, grad_out[pl.ds(pl.multiple_of(device * 8, 8), 8), :])[0:images] / count

    spread = jnp.concatenate([per_slot(me, kind, info_in), per_slot(me ^ 8, kind, there), per_slot(me, 1 - kind, info_in), jnp.zeros((24 - 3 * images, width), f32)])
    grad_rows[...] = spread
    low = spread[0:16].astype(bf16)
    for j in range(0, ff, width):
        active_grad[:, j : j + width] = dot_nt(low, wd[0, j : j + width, :])
    lines = [info[image, 2:3, :] for info in (info_in, there, info_in) for image in range(images)]
    masks[...] = jnp.concatenate(lines + [jnp.zeros((slots - 3 * images, slots), f32)]).T

    def sums_in(step, carry):
        peer = lax.rem(me + n - step, n)
        pltpu.make_async_remote_copy(
            src_ref=share.at[0, :, pl.ds(0, 384)], dst_ref=got.at[peer], send_sem=sum_send.at[step], recv_sem=sum_recv.at[step],
            device_id=(peer,), device_id_type=MESH).wait()
        return carry

    lax.fori_loop(1, n, sums_in, 0)
    for number in range(7):
        ready(number)
    for place in range(3):
        store_tokens(place).wait()


def forward(n, visible, valid_mask, patches, weights):
    gain_one, shift_one, w_qkv, w_out, gain_two, shift_two, w_up, b_up, w_down = weights
    micro_count, per_micro, slots = visible.shape
    images = micro_count * per_micro
    width, ff = w_up.shape[1:]
    anywhere, vmem = pl.BlockSpec(memory_space=pl.ANY), pl.BlockSpec(memory_space=pltpu.VMEM)
    turned = (16, width // 16, slots)
    kept = [(turned, bf16), ((slots, 3 * width), bf16), ((HEADS // 2, 2 * slots, slots), bf16), (turned, bf16), ((slots, width), f32),
            (turned, bf16), ((slots, ff), bf16)]
    return pl.pallas_call(
        functools.partial(forward_kernel, n, micro_count),
        out_shape=[jax.ShapeDtypeStruct(shape, f32) for shape in
                   ((1, 1), (8 * n, width), (n, 8, 384), (24, width), (16, ff), (slots, slots), (3 * images, slots, width))]
        + [jax.ShapeDtypeStruct((3 * images,) + dims, dtype) for dims, dtype in kept],
        in_specs=[vmem] * 7 + [anywhere] * 5,
        out_specs=[vmem] * 6 + [anywhere] * 8,
        scratch_shapes=[
            pltpu.VMEM(patches.shape, bf16),
            pltpu.VMEM((3 * images, slots, width), f32),
            pltpu.VMEM((images, 8, slots), f32),
            pltpu.VMEM((images, 8, slots), f32),
            pltpu.VMEM(w_qkv.shape, bf16), pltpu.VMEM(w_out.shape, bf16), pltpu.VMEM(w_up.shape, bf16), pltpu.VMEM(w_down.shape, bf16)]
        + [pltpu.VMEM((images,) + dims, dtype) for dims, dtype in kept]
        + [
            pltpu.VMEM((2, images * slots, WIDE), f32),
            pltpu.VMEM((images * slots, WIDE), bf16),
            pltpu.VMEM((images, slots, width), bf16),
            pltpu.VMEM((images, slots, width), bf16),
            pltpu.VMEM((width, slots), bf16),
            pltpu.VMEM((2, 8, ff), f32),
            pltpu.VMEM((2, 8, ff), f32),
            pltpu.VMEM((n, 8, width), f32),
            pltpu.SemaphoreType.DMA((31,)),
            pltpu.SemaphoreType.DMA((31,)),
            pltpu.SemaphoreType.DMA((n,)),
            pltpu.SemaphoreType.DMA((n,)),
            pltpu.SemaphoreType.DMA,
            pltpu.SemaphoreType.DMA((2, 4)),
            pltpu.SemaphoreType.DMA((7,)),
            pltpu.SemaphoreType.DMA((3,)),
            pltpu.SemaphoreType.DMA((2, 2)),
        ],
        compiler_params=pltpu.CompilerParams(collective_id=0, has_side_effects=True, vmem_limit_bytes=63 << 20),
    )(visible, valid_mask, gain_one, shift_one, gain_two, shift_two, b_up, patches, w_qkv, w_out, w_up, w_down)


CHUNK = 384


def meet(peers):
    barrier = pltpu.get_barrier_semaphore()
    for peer in peers:
        pl.semaphore_signal(barrier, inc=1, device_id=(peer,), device_id_type=MESH)
    pl.semaphore_wait(barrier, len(peers))


def finish_kernel(visible, first, second, extra, loss, up, out, qkv, down,
                  cells, gain_one, shift_one, gain_two, shift_two, bias, loss_out, up_out, out_out, qkv_out, down_out):
    step = pl.program_id(0)
    images = visible.shape[1]
    for source, target in ((up, up_out), (out, out_out), (qkv, qkv_out), (down, down_out)):
        target[...] = source[...]

    @pl.when(step == 0)
    def _():
        rows = extra.shape[0]
        lines = jnp.concatenate([extra[...], jnp.zeros((128 - rows, 128), f32)]).T
        for number, target in enumerate((gain_one, shift_one, gain_two, shift_two)):
            target[...] = lines[number : number + 1, 0:rows]
        bias[...] = jnp.concatenate([lines[4 + k : 5 + k, 0:rows] for k in range(4)], axis=1)
        loss_out[...] = loss[...]

    patch_count, slots = cells.shape[1], visible.shape[2]
    seen = visible[step // images, pl.ds(step % images, 1), :]
    picked = jnp.where(lax.broadcasted_iota(jnp.int32, (patch_count, slots), 0) == seen, 1.0, 0.0).astype(bf16)
    for modality, grads in enumerate((first, second)):
        value = grads[0]
        high = value.astype(bf16)
        rest = (value - high.astype(f32)).astype(bf16)
        cells[0, :, modality, :] = dot(picked, high) + dot(picked, rest)


def finish(visible, grads, patch_count, extra, loss, passed):
    total, slots, width = grads.shape
    images = total // 2
    rows = extra.shape[0]
    whole = pl.BlockSpec(memory_space=pltpu.VMEM)
    pieces = [pl.BlockSpec((rows, width), lambda i: (0, i)), pl.BlockSpec((rows, width), lambda i: (0, 0)),
              pl.BlockSpec((rows, width), lambda i: (0, jnp.minimum(i, 2))), pl.BlockSpec((1, rows, width), lambda i: (i // 2, i % 2, 0))]
    return pl.pallas_call(
        finish_kernel,
        grid=(images,),
        in_specs=[whole, pl.BlockSpec((1, slots, width), lambda i: (i, 0, 0)), pl.BlockSpec((1, slots, width), lambda i: (images + i, 0, 0)), whole, whole]
        + pieces,
        out_specs=[pl.BlockSpec((1, patch_count, 2, width), lambda i: (i, 0, 0, 0))] + [whole] * 6 + pieces,
        out_shape=[jax.ShapeDtypeStruct((images, patch_count, 2, width), f32)] + [jax.ShapeDtypeStruct((1, rows), f32)] * 4
        + [jax.ShapeDtypeStruct((1, 4 * rows), f32), jax.ShapeDtypeStruct((1, 1), f32)] + [jax.ShapeDtypeStruct(one.shape, f32) for one in passed],
        compiler_params=pltpu.CompilerParams(vmem_limit_bytes=62 << 20),
    )(visible, grads, grads, extra, loss, *passed)


def backward_kernel(own, grad_rows, first_active, masks, gain_one, gain_two, got, grad_all, tokens, one_t, packed, probs, att_t, mixed, two_t, slope,
                    w_qkv, w_out, w_up, w_down,
                    up_out, out_out, qkv_out, extra_out, tokens_out, down_out,
                    mine, ring, core_got, first_got, second_got, owner_got,
                    extra, extra_mine, extra_core, extra_first, extra_second, extra_owner,
                    wide, mixed_grad, mixed_low, turned, weights, active_grad, sums, packs, shares, rows_in, rows_out, hidden_grad,
                    sems, extra_sems, wsem, dsem, tsem, psem, rsem, osem):
    me = lax.axis_index("dp")
    core, xx, yy, zz = me % 2, (me // 2) % 2, (me // 4) % 2, me // 8
    kind, low_z = zz % 2, zz // 2
    slots, width = mixed.shape[1:]
    ff = slope.shape[2]
    both = 2 * own
    pairs = 2 * ff // width
    up_pairs = ff // width

    def load_slope(place, count, j):
        at = pl.ds(pl.multiple_of(j * width, 128), width)
        return pltpu.make_async_copy(slope.at[pl.ds(place, count), :, at], wide.at[pl.ds(0, count), :, at], dsem.at[j])

    def load_down(which, j):
        at = pl.ds(pl.multiple_of(j * width, 128), width)
        return pltpu.make_async_copy(w_down.at[which, at, :], weights.at[1, :, at], wsem.at[j])

    def load_up(which):
        return pltpu.make_async_copy(w_up.at[which], weights.at[0], wsem.at[4])

    def load_rest(which):
        return (pltpu.make_async_copy(w_qkv.at[which], weights.at[1, :, pl.ds(0, 3 * width)], wsem.at[5]),
                pltpu.make_async_copy(w_out.at[which], weights.at[1, :, pl.ds(3 * width, width)], wsem.at[6]))

    def load_turned(source, slot, image, part):
        return pltpu.make_async_copy(
            source.at[image, :, part], turned.at[slot, part, :, :, pl.ds(pl.multiple_of(image * slots, 128), slots)], tsem.at[slot, part, image])

    def all_turned(source, slot, act):
        def one(image, carry):
            for part in (0, 1):
                act(load_turned(source, slot, image, part))
            return carry

        lax.fori_loop(0, both, one, 0)

    def begin(copy):
        copy.start()

    def finish(copy):
        copy.wait()

    load_slope(0, both, 0).start()
    all_turned(two_t, 0, begin)
    for j in range(1, up_pairs):
        load_slope(0, both, j).start()
    load_up(kind).start()
    all_turned(att_t, 1, begin)
    for copy in load_rest(kind):
        copy.start()

    meet([me ^ 1, me ^ 2, me ^ 4, me ^ 8, me ^ 16, me ^ 24])

    def sem(stage, chunk, way):
        return sems.at[stage, chunk, way]

    def chunk_sem(chunk, stage, way):
        return sems.at[stage, chunk, way]

    def extra_sem(stage, way):
        return extra_sems.at[stage, way]

    def remote(src, dst, send, recv, flip):
        return pltpu.make_async_remote_copy(src_ref=src, dst_ref=dst, send_sem=send, recv_sem=recv, device_id=(me ^ flip,), device_id_type=MESH)

    def to_core(chunk):
        return remote(ring.at[(chunk // 2) % 2, chunk % 2], core_got.at[chunk], sem(1, chunk, 0), sem(1, chunk, 1), 1)

    def first(chunk, along_x):
        src = mine.at[chunk, :, :, 1 - xx] if along_x else mine.at[chunk, :, 1 - yy]
        return remote(src, first_got.at[chunk], sem(2, chunk, 0), sem(2, chunk, 1), 2 if along_x else 4)

    def second(chunk, along_x):
        src = mine.at[chunk, :, 1 - yy, xx] if along_x else mine.at[chunk, :, yy, 1 - xx]
        return remote(src, second_got.at[chunk], sem(3, chunk, 0), sem(3, chunk, 1), 4 if along_x else 2)

    def third(source, owner, send, recv, half):
        target = 2 * kind + half
        return target, pltpu.make_async_remote_copy(
            src_ref=source.at[half, yy, xx], dst_ref=owner.at[low_z], send_sem=send, recv_sem=recv,
            device_id=(target * 8 + me % 8,), device_id_type=MESH)

    def start_third(source, owner, semaphore):
        for half in (0, 1):
            target, copy = third(source, owner, semaphore(4, half), semaphore(5, low_z), half)

            @pl.when(target != zz)
            def _():
                copy.start()

            @pl.when(target == zz)
            def _():
                owner[low_z] = source[half, yy, xx]

    def wait_third(source, owner, semaphore):
        for half in (0, 1):
            target, copy = third(source, owner, semaphore(4, half), semaphore(5, low_z), half)

            @pl.when(target != zz)
            def _():
                copy.wait_send()

        for origin in (0, 1):
            @pl.when(2 * origin + low_z != zz)
            def _():
                remote(source.at[0, yy, xx], owner.at[origin], semaphore(4, 0), semaphore(5, origin), 8).wait_recv()

    def run_first(pair):
        for odd in (0, 1):
            chunk = 2 * pair + odd
            to_core(chunk).wait_recv()
            mine[chunk] = mine[chunk] + core_got[chunk]
            first(chunk, odd == 0).start()

    def run_second(pair):
        for odd in (0, 1):
            chunk = 2 * pair + odd
            first(chunk, odd == 0).wait()
            if odd == 0:
                mine[chunk, :, :, xx] = mine[chunk, :, :, xx] + first_got[chunk]
            else:
                mine[chunk, :, yy] = mine[chunk, :, yy] + first_got[chunk]
            second(chunk, odd == 0).start()

    def run_third(pair):
        for odd in (0, 1):
            chunk = 2 * pair + odd
            second(chunk, odd == 0).wait()
            mine[chunk, :, yy, xx] = mine[chunk, :, yy, xx] + second_got[chunk]
            start_third(mine.at[chunk], owner_got.at[chunk], functools.partial(chunk_sem, chunk))

    def write(chunk, target, base):
        at = pl.ds(pl.multiple_of((chunk - 2 * base) * CHUNK, 128), CHUNK)
        return pltpu.make_async_copy(owner_got.at[chunk, 0], target.at[:, at], sem(0, chunk, 0))

    outputs = ((up_out, 0, up_pairs), (out_out, up_pairs, up_pairs + 1), (qkv_out, up_pairs + 1, pairs))

    def run_last(target, base, pair):
        for odd in (0, 1):
            chunk = 2 * pair + odd
            wait_third(mine.at[chunk], owner_got.at[chunk], functools.partial(chunk_sem, chunk))
            owner_got[chunk, 0] = owner_got[chunk, 0] + owner_got[chunk, 1]
            write(chunk, target, base).start()

    def serve(run, low, high):
        def one(pair, carry):
            run(pair)
            return carry

        lax.fori_loop(low, high, one, 0)

    def terms(pair, slot, block, reused=True):
        if reused:
            for odd in (0, 1):
                to_core(2 * (pair - 2) + odd).wait_send()
        for part, row_half in ((0, core), (1, 1 - core)):
            left = turned[slot, row_half].reshape(8 * 48, both * slots)
            if block is None:
                right = mixed_low[...]
            else:
                right = wide[:, :, pl.ds(pl.multiple_of(block * width, 128), width)]
            got = dot(left, right.reshape(both * slots, width))
            for odd in (0, 1):
                piece = got[:, odd * CHUNK : odd * CHUNK + CHUNK].reshape(2, 2, 2, 48, CHUNK)
                if part == 0:
                    mine[2 * pair + odd] = piece
                else:
                    ring[pair % 2, odd] = piece
        for odd in (0, 1):
            to_core(2 * pair + odd).start()

    lanes = lax.broadcasted_iota(jnp.int32, (slots, 128), 1)

    def mask_of(place):
        return jnp.sum(jnp.where(lanes == place, masks[...], 0.0), axis=1, keepdims=True)

    def make_active_grad(first_row, which):
        low = grad_rows[first_row : first_row + 16].astype(bf16)
        for j in range(up_pairs):
            load_down(which, j).wait()
            active_grad[:, j * width : (j + 1) * width] = dot_nt(low, weights[1, :, j * width : (j + 1) * width])
        for copy in load_rest(which):
            copy.start()

    def upper_grad(j, place, count):
        at = pl.ds(pl.multiple_of(j * width, 128), width)
        load_slope(place, count, j).wait()

        def one(image, carry):
            row = active_grad[pl.ds(image, 1), at]
            weight = mask_of(place + image)
            for r in range(0, slots, ROWS):
                value = wide[image, r : r + ROWS, at].astype(f32) * (row * weight[r : r + ROWS])
                wide[image, r : r + ROWS, at] = value.astype(bf16)
            return carry

        lax.fori_loop(0, count, one, 0)

    active_grad[...] = first_active[...]
    all_turned(two_t, 0, finish)
    ones = jnp.full((128, both * slots), 1.0, bf16)

    def up_pair(j, carry):
        upper_grad(j, 0, both)

        @pl.when(j >= 2)
        def _():
            for odd in (0, 1):
                to_core(2 * (j - 2) + odd).wait_send()

        right = wide[:, :, pl.ds(pl.multiple_of(j * width, 128), width)].reshape(both * slots, width)
        @pl.when((j >= 1) & (j <= 2))
        def _():
            run_first(j - 1)

        terms(j, 0, j, False)

        bias = dot(ones, right).T.reshape(4, 4, 48, 128)
        lane = lax.broadcasted_iota(jnp.int32, (4, 48, 128), 2)
        spread = jnp.zeros((4, 48, 128), f32)
        for k in range(4):
            spread = spread + jnp.where(lane == 4 + k, bias[:, k], 0.0)
        extra[j // 2, j % 2] = spread.reshape(2, 2, 48, 128)
        return carry

    lax.fori_loop(0, up_pairs, up_pair, 0)
    sums[...] = jnp.zeros_like(sums)

    def hidden_two_back(count):
        def one(k, carry):
            flat = wide[0:count].reshape(count * slots, ff)
            at = pl.ds(pl.multiple_of(k * 256, 256), 256)
            mixed_grad[0:count, :, at] = dot_nt(flat, weights[0, at, :]).reshape(count, slots, 256)
            return carry

        lax.fori_loop(0, width // 256, one, 0)

    def norm_back(rows, grad, gain):
        normed, inverse = row_norm(rows)
        scaled = grad * gain
        back = inverse * (scaled - jnp.mean(scaled, axis=-1, keepdims=True) - normed * jnp.mean(scaled * normed, axis=-1, keepdims=True))
        return normed, back

    def run_hooks(hooks, at):
        for when, act in (hooks or {}).items():
            @pl.when(at == when)
            def _():
                act()

    def fold(values):
        return jnp.sum(values.reshape(ROWS // 8, 8, width), axis=0)

    def norm_two_back(place, count, keep, hooks=None):
        gain = gain_two[pl.ds(kind if keep else 1 - kind, 1), :]

        def load(image):
            return pltpu.make_async_copy(mixed.at[place + image], rows_in.at[image % 2], rsem.at[image % 2])

        load(0).start()

        def one(image, carry):
            @pl.when(image + 1 < count)
            def _():
                load(image + 1).start()

            load(image).wait()
            weight = mask_of(place + image)
            grad_row = grad_rows[pl.ds(place + image, 1), :]
            held, first_sum, second_sum = [], 0.0, 0.0
            for r in range(0, slots, ROWS):
                grad = mixed_grad[image, r : r + ROWS, :]
                normed, back = norm_back(rows_in[image % 2, r : r + ROWS, :], grad, gain)
                value = weight[r : r + ROWS] * grad_row + back
                mixed_low[image, r : r + ROWS, :] = value.astype(bf16)
                held.append(value)
                if keep:
                    first_sum = first_sum + fold(grad * normed)
                    second_sum = second_sum + fold(grad)
            mixed_grad[image] = jnp.concatenate(held)
            if keep:
                sums[2] = sums[2] + first_sum
                sums[3] = sums[3] + second_sum
            run_hooks(hooks, image)
            return carry

        lax.fori_loop(0, count, one, 0)

    def attended_back(count):
        for k in range(0, width, 256):
            flat = mixed_low[0:count].reshape(count * slots, width)
            got = dot_nt(flat, weights[1, k : k + 256, 3 * width : 4 * width])
            wide[0:count, :, 3 * width + k : 3 * width + k + 256] = got.astype(bf16).reshape(count, slots, 256)

    low_half = lax.broadcasted_iota(jnp.int32, (slots, 128), 1) < HEAD_DIM

    def attention_back(place, count, hooks=None):
        def load(image):
            return (pltpu.make_async_copy(packed.at[place + image], packs.at[image % 2], psem.at[0, image % 2]),
                    pltpu.make_async_copy(probs.at[place + image], shares.at[image % 2], psem.at[1, image % 2]))

        for copy in load(0):
            copy.start()

        def one(image, carry):
            @pl.when(image + 1 < count)
            def _():
                for copy in load(image + 1):
                    copy.start()

            for copy in load(image):
                copy.wait()
            now = image % 2
            for pair in range(HEADS // 2):
                at = slice(pair * 128, pair * 128 + 128)
                queries = packs[now, :, pair * 128 : pair * 128 + 128]
                keys = packs[now, :, width + pair * 128 : width + pair * 128 + 128]
                values = packs[now, :, 2 * width + pair * 128 : 2 * width + pair * 128 + 128]
                grad = wide[image, :, 3 * width + pair * 128 : 3 * width + pair * 128 + 128]
                share = shares[now, pair]
                blank = jnp.zeros_like(keys)
                two_keys = jnp.concatenate([jnp.where(low_half, keys, blank), jnp.where(low_half, blank, keys)])
                two_values = jnp.concatenate([jnp.where(low_half, values, blank), jnp.where(low_half, blank, values)])
                grad_share = dot_nt(two_values, grad)
                backs = []
                for side in (0, 1):
                    part = slice(side * slots, side * slots + slots)
                    weight = share[part].astype(f32)
                    product = weight * grad_share[part]
                    backs.append((product - weight * jnp.sum(product, axis=0, keepdims=True)).astype(bf16))
                back = jnp.concatenate(backs)
                grad_values = dot(share, grad)
                grad_keys = dot(back, queries) * head_scale
                grad_queries = dot_tn(back, two_keys) * head_scale
                wide[image, :, pair * 128 : pair * 128 + 128] = grad_queries.astype(bf16)
                wide[image, :, width + pair * 128 : width + pair * 128 + 128] = jnp.where(low_half, grad_keys[:slots], grad_keys[slots:]).astype(bf16)
                wide[image, :, 2 * width + pair * 128 : 2 * width + pair * 128 + 128] = jnp.where(low_half, grad_values[:slots], grad_values[slots:]).astype(bf16)
            run_hooks(hooks, image)
            return carry

        lax.fori_loop(0, count, one, 0)

    def norm_one_back(place, count, keep, out_place, out_count, hooks=None):
        gain = gain_one[pl.ds(kind if keep else 1 - kind, 1), :]

        def load(step):
            return pltpu.make_async_copy(tokens.at[pl.ds(place + 2 * step, 2)], rows_in, rsem.at[0])

        def store(step):
            return pltpu.make_async_copy(rows_out, tokens_out.at[pl.ds(out_place + 2 * step, 2)], osem.at[0])

        load(0).start()

        def one(step, carry):
            flat = wide[pl.ds(2 * step, 2), :, 0 : 3 * width].reshape(2 * slots, 3 * width)
            hidden_grad[...] = dot_nt(flat, weights[1, :, 0 : 3 * width])
            load(step).wait()

            @pl.when((step >= 1) & (step - 1 < out_count // 2))
            def _():
                store(step - 1).wait()

            for side in (0, 1):
                first_sum, second_sum = 0.0, 0.0
                for r in range(0, slots, ROWS):
                    grad = hidden_grad[side * slots + r : side * slots + r + ROWS, :]
                    normed, back = norm_back(rows_in[side, r : r + ROWS, :], grad, gain)
                    rows_out[side, r : r + ROWS, :] = mixed_grad[2 * step + side, r : r + ROWS, :] + back
                    if keep:
                        first_sum = first_sum + fold(grad * normed)
                        second_sum = second_sum + fold(grad)
                if keep:
                    sums[0] = sums[0] + first_sum
                    sums[1] = sums[1] + second_sum

            @pl.when(step + 1 < count // 2)
            def _():
                load(step + 1).start()

            @pl.when(step < out_count // 2)
            def _():
                store(step).start()

            run_hooks(hooks, step)
            return carry

        lax.fori_loop(0, count // 2, one, 0)
        if count == out_count:
            store(count // 2 - 1).wait()

    def serving(*jobs):
        def act():
            for run, pair in jobs:
                run(pair)
        return act

    def step(k):
        run_second(k)
        if k + 2 < pairs:
            run_first(k + 2)
        if k >= 1:
            run_third(k - 1)

    step(0)
    load_up(kind).wait()
    hidden_two_back(both)
    load_up(1 - kind).start()
    all_turned(one_t, 0, begin)
    norm_two_back(0, both, True, {3: lambda: step(1)})
    all_turned(att_t, 1, finish)
    terms(up_pairs, 1, None)
    for copy in load_rest(kind):
        copy.wait()
    attended_back(both)
    attention_back(0, both, {3: lambda: step(2)})
    all_turned(one_t, 0, finish)
    terms(up_pairs + 1, 0, 0)
    step(3)
    terms(up_pairs + 2, 0, 1)
    terms(pairs - 1, 0, 2)
    norm_one_back(0, both, True, kind * own, own, {2: lambda: step(4)})

    vectors = jnp.concatenate([jnp.sum(sums[k], axis=0, keepdims=True) for k in range(4)] + [jnp.zeros((124, width), f32)])
    extra[...] = extra[...] + vectors.T.reshape(extra.shape)
    extra_mine[...] = extra[:, :, :, core]
    extra_to_core = remote(extra.at[:, :, :, 1 - core], extra_core, extra_sems.at[1, 0], extra_sems.at[1, 1], 1)
    extra_first_copy = remote(extra_mine.at[:, :, 1 - xx], extra_first, extra_sems.at[2, 0], extra_sems.at[2, 1], 2)
    extra_second_copy = remote(extra_mine.at[:, 1 - yy, xx], extra_second, extra_sems.at[3, 0], extra_sems.at[3, 1], 4)
    extra_to_core.start()

    for j in range(up_pairs):
        load_slope(both, own, j).start()
        load_down(1 - kind, j).start()
    make_active_grad(both, 1 - kind)

    def other_pair(j, carry):
        upper_grad(j, both, own)
        return carry

    lax.fori_loop(0, up_pairs, other_pair, 0)
    step(5)
    extra_to_core.wait()
    extra_mine[...] = extra_mine[...] + extra_core[...]
    extra_first_copy.start()
    load_up(1 - kind).wait()
    hidden_two_back(own)
    norm_two_back(both, own, False)
    for copy in load_rest(1 - kind):
        copy.wait()
    attended_back(own)
    attention_back(both, own)
    step(6)
    extra_first_copy.wait()
    extra_mine[:, :, xx] = extra_mine[:, :, xx] + extra_first[...]
    extra_second_copy.start()
    norm_one_back(both, own, False, (1 - kind) * own, own)

    reads = [pltpu.make_async_copy(grad_all.at[pl.ds(part * slots, slots), :], rows_in.at[part], rsem.at[part]) for part in (0, 1)]
    reads += [pltpu.make_async_copy(got.at[pl.ds(part * slots, slots), :], rows_out.at[part, :, pl.ds(0, CHUNK)], osem.at[part]) for part in (0, 1)]
    for copy in reads:
        copy.start()
    for copy in reads:
        copy.wait()
    sums_all = rows_out[:, :, 0:CHUNK].reshape(2 * slots, CHUNK)
    down = lax.dot_general(sums_all, rows_in[...].reshape(2 * slots, width), (((0,), (0,)), ((), ())), precision=highest, preferred_element_type=f32)
    half = CHUNK // 2
    mixed_grad[0:2, 0 : half // 2, :] = jnp.where(core == 0, down[:half], down[half:]).reshape(2, half // 2, width)
    write_down = pltpu.make_async_copy(mixed_grad.at[pl.ds(0, 2), pl.ds(0, half // 2), :], down_out, wsem.at[3])
    write_down.start()
    step(7)
    run_third(7)
    for chunk in range(2 * pairs - 4, 2 * pairs):
        to_core(chunk).wait_send()
    extra_second_copy.wait()
    extra_mine[:, yy, xx] = extra_mine[:, yy, xx] + extra_second[...]
    start_third(extra_mine, extra_owner, extra_sem)
    for target, low, high in outputs:
        serve(functools.partial(run_last, target, low), low, high)
    wait_third(extra_mine, extra_owner, extra_sem)
    extra_out[...] = extra_owner[0] + extra_owner[1]
    for target, low, high in outputs:
        for chunk in range(2 * low, 2 * high):
            write(chunk, target, low).wait()
    write_down.wait()


def backward(own, grad_rows, first_active, masks, got, grad_all, tokens, saved, weights):
    gain_one, shift_one, w_qkv, w_out, gain_two, shift_two, w_up, b_up, w_down = weights
    slots, width = tokens.shape[1:]
    ff = w_up.shape[2]
    both = 2 * own
    chunks = 2 * ff // CHUNK
    one_t, packed, probs, att_t, mixed, two_t, slope = saved
    split = lambda one: one.reshape(one.shape[0], 8, 2, one.shape[2], one.shape[3])
    anywhere, vmem = pl.BlockSpec(memory_space=pl.ANY), pl.BlockSpec(memory_space=pltpu.VMEM)
    return pl.pallas_call(
        functools.partial(backward_kernel, own),
        out_shape=(
            jax.ShapeDtypeStruct((48, ff), f32), jax.ShapeDtypeStruct((48, width), f32), jax.ShapeDtypeStruct((48, 3 * width), f32),
            jax.ShapeDtypeStruct((48, 128), f32), jax.ShapeDtypeStruct((both, slots, width), f32),
            jax.ShapeDtypeStruct((2, CHUNK // 4, width), f32),
        ),
        in_specs=[vmem] * 5 + [anywhere] * 14,
        out_specs=(anywhere, anywhere, anywhere, vmem, anywhere, anywhere),
        scratch_shapes=[
            pltpu.VMEM((chunks, 2, 2, 2, 48, CHUNK), f32),
            pltpu.VMEM((2, 2, 2, 2, 2, 48, CHUNK), f32),
            pltpu.VMEM((chunks, 2, 2, 2, 48, CHUNK), f32),
            pltpu.VMEM((chunks, 2, 2, 48, CHUNK), f32),
            pltpu.VMEM((chunks, 2, 48, CHUNK), f32),
            pltpu.VMEM((chunks, 2, 48, CHUNK), f32),
            pltpu.VMEM((2, 2, 2, 2, 48, 128), f32),
            pltpu.VMEM((2, 2, 2, 48, 128), f32),
            pltpu.VMEM((2, 2, 2, 48, 128), f32),
            pltpu.VMEM((2, 2, 48, 128), f32),
            pltpu.VMEM((2, 48, 128), f32),
            pltpu.VMEM((2, 48, 128), f32),
            pltpu.VMEM((both, slots, ff), bf16),
            pltpu.VMEM((both, slots, width), f32),
            pltpu.VMEM((both, slots, width), bf16),
            pltpu.VMEM((2, 2, 8, 48, both * slots), bf16),
            pltpu.VMEM((2, width, ff), bf16),
            pltpu.VMEM((16, ff), f32),
            pltpu.VMEM((4, 8, width), f32),
            pltpu.VMEM((2, slots, 3 * width), bf16),
            pltpu.VMEM((2, HEADS // 2, 2 * slots, slots), bf16),
            pltpu.VMEM((2, slots, width), f32),
            pltpu.VMEM((2, slots, width), f32),
            pltpu.VMEM((2 * slots, width), f32),
            pltpu.SemaphoreType.DMA((6, chunks, 2)),
            pltpu.SemaphoreType.DMA((6, 2)),
            pltpu.SemaphoreType.DMA((7,)),
            pltpu.SemaphoreType.DMA((4,)),
            pltpu.SemaphoreType.DMA((2, 2, both)),
            pltpu.SemaphoreType.DMA((2, 2)),
            pltpu.SemaphoreType.DMA((2,)),
            pltpu.SemaphoreType.DMA((2,)),
        ],
        compiler_params=pltpu.CompilerParams(collective_id=1, has_side_effects=True, vmem_limit_bytes=63 << 20),
    )(grad_rows, first_active, masks, gain_one, gain_two, got.reshape(-1, CHUNK), grad_all, tokens, split(one_t), packed, probs, split(att_t), mixed, split(two_t), slope,
      w_qkv, w_out, w_up, w_down)


def tokens_of(patches, visible, modality):
    micro_count, images, _, patch_count, width = patches.shape
    cells = lax.dynamic_index_in_dim(patches, modality, 2, keepdims=False).reshape(micro_count * images, patch_count, width)
    picked = (visible[:, :, None] == jnp.arange(patch_count)[None, None, :]).astype(bf16)
    return jnp.einsum("isp,ipd->isd", picked, cells, preferred_element_type=f32)


def cells_of(grad_tokens, visible, patch_count):
    picked = (visible[:, None, :] == jnp.arange(patch_count)[None, :, None]).astype(f32)
    return jnp.einsum("ips,isd->ipd", picked, grad_tokens, precision=highest)


def on_tuned(patches, visible, valid_mask, weights):
    n = lax.axis_size("dp")
    micro_count, images, _, patch_count, width = patches.shape
    own = micro_count * images
    loss, grad_all, got, grad_rows, active_grad, masks, tokens, *saved = forward(
        n, visible, valid_mask, patches.reshape(own, 2, patch_count, width), weights)
    up, out, qkv, extra, grad_tokens, down = backward(own, grad_rows, active_grad, masks, got, grad_all, tokens, saved, weights)
    cells, gain_one, shift_one, gain_two, shift_two, bias, loss, up, out, qkv, down = finish(
        visible, grad_tokens, patch_count, extra, loss, (up, out, qkv, down))
    patches_grad = cells.reshape(micro_count, images, patch_count, 2, width).transpose(0, 1, 3, 2, 4)
    vector = lambda one: one.reshape(-1)
    return (loss.reshape(()), patches_grad, vector(gain_one), vector(shift_one), qkv, out, vector(gain_two), vector(shift_two), up,
            vector(bias), down.reshape(-1, width))


def on_plain(patches, visible, valid_mask, weights):
    n = lax.axis_size("dp")
    me = lax.axis_index("dp")
    micro_count, images, _, patch_count, width = patches.shape
    own = micro_count * images
    slots = visible.shape[-1]
    ff = weights[6].shape[2]
    seen = visible.reshape(own, slots)
    mask = valid_mask.reshape(own, slots)
    outcomes = []
    for modality in (0, 1):
        params = params_of(weights, modality)
        outcomes.append((params,) + encode_forward(tokens_of(patches, seen, modality), seen, mask, params))
    pooled = jnp.concatenate([pool(active, mixed, mask, params[8]) for params, active, mixed, _ in outcomes])
    counted = jnp.sum(mask.astype(f32), axis=1)[:, None]
    shares = jnp.stack([active / counted for _, active, _, _ in outcomes])
    down_rows = 2 * ff // n
    shares = shares.reshape(2, own, n // 2, down_rows).transpose(0, 2, 1, 3).reshape(n, own * down_rows)
    loss, grad_all = contrast(lax.all_gather(pooled, "dp", axis=0, tiled=True), 2 * own, micro_count)
    got = lax.all_to_all(shares, "dp", 0, 0, tiled=True)
    grad_all = grad_all.reshape(n, 2, own, width)
    grad_down = jnp.einsum(
        "iw,id->wd", got.reshape(n * own, down_rows),
        lax.dynamic_index_in_dim(grad_all, me // (n // 2), 1, keepdims=False).reshape(n * own, width), precision=highest)
    mine = lax.dynamic_index_in_dim(grad_all, me, 0, keepdims=False)
    backs = [encode_backward(mine[m], outcomes[m][3], mask, outcomes[m][0]) for m in (0, 1)]
    patches_grad = jnp.stack([cells_of(back[0], seen, patch_count) for back in backs], 1).reshape(patches.shape)
    joined = jax.tree.map(lambda a, b: jnp.concatenate([a, b]), backs[0][1], backs[1][1])
    shards = tuple(lax.psum_scatter(one, "dp", scatter_dimension=0, tiled=True) for one in joined)
    return (loss[0, 0], patches_grad) + shards + (grad_down,)


def solution(mesh):
    in_specs = (P(None, "dp"), P(None, "dp"), P(None, "dp")) + (P(),) * 9
    out_specs = (P(), P(None, "dp")) + (P("dp"),) * 9

    def on_device(patches, visible, valid_mask, *weights):
        run = on_tuned if lax.axis_size("dp") == 32 else on_plain
        return run(patches, visible, valid_mask, weights)

    return jax.shard_map(on_device, mesh=mesh, in_specs=in_specs, out_specs=out_specs, check_vma=False)
```

```python
import functools
import math

import jax
import jax.numpy as jnp
from jax import lax
from jax.experimental import pallas as pl
from jax.experimental.pallas import tpu as pltpu
from jax.sharding import PartitionSpec as P

HEADS = 12
HEAD_DIM = 64
GRID = 15
MESH = pl.DeviceIdType.MESH

norm_epsilon = 1e-06
unit_epsilon = 1e-06
logit_scale = 100.0
masked_score = -1e30
highest = lax.Precision.HIGHEST
head_scale = 1.0 / math.sqrt(HEAD_DIM)
f32 = jnp.float32
bf16 = jnp.bfloat16


def exact_gelu(values_in):
    return jax.nn.gelu(values_in, approximate=False)


def layer_norm(values_in, gain_vec, shift_vec):
    centre = values_in - jnp.mean(values_in, axis=-1, keepdims=True)
    inverse = lax.rsqrt(jnp.mean(centre * centre, axis=-1, keepdims=True) + norm_epsilon)
    normed = centre * inverse
    return (normed * gain_vec + shift_vec, normed, inverse)


def norm_back(grad_out, normed, inverse, gain_vec):
    grad_normed = grad_out * gain_vec
    mean_plain = jnp.mean(grad_normed, axis=-1, keepdims=True)
    mean_normed = jnp.mean(grad_normed * normed, axis=-1, keepdims=True)
    grad_in = inverse * (grad_normed - mean_plain - normed * mean_normed)
    return (grad_in, jnp.sum(grad_out * normed, axis=0), jnp.sum(grad_out, axis=0))


def alibi_bias(visible_rows):
    rows_pos = (visible_rows // GRID).astype(f32)
    cols_pos = (visible_rows % GRID).astype(f32)
    rows_gap = rows_pos[:, :, None] - rows_pos[:, None, :]
    cols_gap = cols_pos[:, :, None] - cols_pos[:, None, :]
    distance = jnp.sqrt(rows_gap * rows_gap + cols_gap * cols_gap)
    slopes = jnp.exp2(-8.0 * (jnp.arange(HEADS, dtype=f32) + 1.0) / HEADS)
    return -slopes[None, :, None, None] * distance[:, None, :, :]


def split_heads(packed):
    images, slot_count, _ = packed.shape
    shaped = packed.reshape(images, slot_count, 3, HEADS, HEAD_DIM)
    return (shaped[:, :, 0], shaped[:, :, 1], shaped[:, :, 2])


def encode_forward(tokens_in, visible_rows, mask_rows, params):
    gain_one, shift_one, w_qkv, w_out, gain_two, shift_two, w_up, b_up, w_down = params
    images, slots, width = tokens_in.shape
    flat_in = tokens_in.reshape(images * slots, width)
    hidden_one, normed_one, inverse_one = layer_norm(flat_in, gain_one, shift_one)
    hidden_one = hidden_one.astype(bf16)
    packed = jnp.dot(hidden_one, w_qkv, preferred_element_type=f32).astype(bf16)
    packed = packed.reshape(images, slots, 3 * width)
    queries, keys, values = split_heads(packed)
    scores = jnp.einsum("iqhd,ikhd->ihqk", queries, keys, preferred_element_type=f32)
    scores = scores * head_scale + alibi_bias(visible_rows)
    scores = jnp.where((mask_rows > 0)[:, None, None, :], scores, masked_score)
    attention = jax.nn.softmax(scores, axis=-1)
    attended = jnp.einsum("ihqk,ikhd->iqhd", attention.astype(bf16), values, preferred_element_type=f32)
    attended = attended.reshape(images * slots, width).astype(bf16)
    mixed = flat_in + jnp.dot(attended, w_out, preferred_element_type=f32)
    hidden_two, normed_two, inverse_two = layer_norm(mixed, gain_two, shift_two)
    hidden_two = hidden_two.astype(bf16)
    upper = jnp.dot(hidden_two, w_up, preferred_element_type=f32) + b_up
    active, gelu_back = jax.vjp(exact_gelu, upper)
    active = active.astype(bf16).astype(f32)
    weight = mask_rows.astype(f32)
    active_sum = jnp.sum(active.reshape(images, slots, -1) * weight[:, :, None], axis=1)
    mixed_sum = jnp.sum(mixed.reshape(images, slots, width) * weight[:, :, None], axis=1)
    saved = (normed_one, inverse_one, hidden_one, packed, attention, attended, normed_two, inverse_two, hidden_two, gelu_back)
    return active_sum, mixed_sum, saved


def pool(active_sum, mixed_sum, mask_rows, w_down):
    counted = jnp.sum(mask_rows.astype(f32), axis=1)[:, None]
    down = jnp.dot(active_sum, w_down.astype(f32), precision=highest)
    return (mixed_sum + down) / counted


def encode_backward(grad_pooled, saved, mask_rows, params):
    normed_one, inverse_one, hidden_one, packed, attention, attended, normed_two, inverse_two, hidden_two, gelu_back = saved
    gain_one, shift_one, w_qkv, w_out, gain_two, shift_two, w_up, b_up, w_down = params
    images, slots, three_width = packed.shape
    width = three_width // 3
    rows = images * slots
    weight = mask_rows.astype(f32)
    counted = jnp.sum(weight, axis=1)[:, None]
    grad_row = grad_pooled / counted
    grad_output = (weight[:, :, None] * grad_row[:, None, :]).reshape(rows, width)
    grad_active = jnp.dot(grad_row.astype(bf16), w_down.T, preferred_element_type=f32)
    grad_active = (weight[:, :, None] * grad_active[:, None, :]).reshape(rows, -1)
    grad_upper = gelu_back(grad_active)[0].astype(bf16)
    grad_bias = jnp.sum(grad_upper.astype(f32), axis=0)
    grad_up = jnp.dot(hidden_two.T, grad_upper, preferred_element_type=f32)
    grad_hidden_two = jnp.dot(grad_upper, w_up.T, preferred_element_type=f32)
    grad_norm_two, grad_gain_two, grad_shift_two = norm_back(grad_hidden_two, normed_two, inverse_two, gain_two)
    grad_mixed = grad_output + grad_norm_two
    grad_mixed_low = grad_mixed.astype(bf16)
    grad_out = jnp.dot(attended.T, grad_mixed_low, preferred_element_type=f32)
    grad_attended = jnp.dot(grad_mixed_low, w_out.T, preferred_element_type=f32).astype(bf16)
    grad_attended = grad_attended.reshape(images, slots, HEADS, HEAD_DIM)
    queries, keys, values = split_heads(packed)
    grad_value = jnp.einsum("ihqk,iqhd->ikhd", attention.astype(bf16), grad_attended, preferred_element_type=f32)
    grad_attention = jnp.einsum("iqhd,ikhd->ihqk", grad_attended, values, preferred_element_type=f32)
    grad_scores = attention * (grad_attention - jnp.sum(attention * grad_attention, axis=-1, keepdims=True))
    grad_scores = grad_scores.astype(bf16)
    grad_query = jnp.einsum("ihqk,ikhd->iqhd", grad_scores, keys, preferred_element_type=f32) * head_scale
    grad_key = jnp.einsum("ihqk,iqhd->ikhd", grad_scores, queries, preferred_element_type=f32) * head_scale
    grad_packed = jnp.stack([grad_query, grad_key, grad_value], axis=2).astype(bf16).reshape(rows, three_width)
    grad_qkv = jnp.dot(hidden_one.T, grad_packed, preferred_element_type=f32)
    grad_hidden_one = jnp.dot(grad_packed, w_qkv.T, preferred_element_type=f32)
    grad_norm_one, grad_gain_one, grad_shift_one = norm_back(grad_hidden_one, normed_one, inverse_one, gain_one)
    grad_tokens = (grad_mixed + grad_norm_one).reshape(images, slots, width)
    return grad_tokens, (grad_gain_one, grad_shift_one, grad_qkv, grad_out, grad_gain_two, grad_shift_two, grad_up, grad_bias)


def contrast(pooled, own_rows, micro_count):
    count = pooled.shape[0]
    images = own_rows // (2 * micro_count)
    inverse = lax.rsqrt(jnp.sum(pooled * pooled, axis=-1, keepdims=True) + unit_epsilon)
    unit = pooled * inverse
    logits = logit_scale * lax.dot_general(unit, unit, (((1,), (1,)), ((), ())), precision=highest, preferred_element_type=f32)
    row = lax.broadcasted_iota(jnp.int32, (count, count), 0)
    col = lax.broadcasted_iota(jnp.int32, (count, count), 1)
    half = own_rows // 2
    row_mod, col_mod = (row // half) % 2, (col // half) % 2
    row_micro, col_micro = (row // images) % micro_count, (col // images) % micro_count
    allowed = (row_mod != col_mod) & (row_micro == col_micro)
    paired = jnp.where(col == row + half * (1 - 2 * row_mod), 1.0, 0.0)
    logits = jnp.where(allowed, logits, masked_score)
    row_max = jnp.max(logits, axis=1, keepdims=True)
    row_lse = row_max + jnp.log(jnp.sum(jnp.exp(logits - row_max), axis=1, keepdims=True))
    col_max = jnp.max(logits, axis=0, keepdims=True)
    col_lse = col_max + jnp.log(jnp.sum(jnp.exp(logits - col_max), axis=0, keepdims=True))
    scale = 1.0 / count
    diagonal = jnp.sum(jnp.where(paired > 0, logits, 0.0), axis=1, keepdims=True)
    loss = scale * jnp.sum(row_lse - diagonal, axis=0, keepdims=True)
    spread = jnp.exp(logits - row_lse) + jnp.exp(logits - col_lse) - 2.0 * paired
    grad_unit = (logit_scale * scale) * jnp.dot(spread, unit, precision=highest, preferred_element_type=f32)
    grad_pooled = inverse * (grad_unit - unit * jnp.sum(unit * grad_unit, axis=-1, keepdims=True))
    return loss, grad_pooled


def params_of(weights, modality):
    return tuple(lax.dynamic_index_in_dim(one, modality, 0, keepdims=False) for one in weights)


GROWS = 32
SLOPES = [2.0 ** (-8.0 * (head + 1) / HEADS) for head in range(HEADS)]
ROWS = 32
WIDE = 512


def gelu_pair(upper):
    size = jnp.abs(upper)
    bell = jnp.exp(-0.5 * upper * upper)
    below = 1.0 + (0.3275911 * math.sqrt(0.5)) * size
    t = pltpu.reciprocal(below, approx=True)
    t = t * (2.0 - below * t)
    tail = t * (0.5 * 0.254829592 + t * (0.5 * -0.284496736 + t * (0.5 * 1.421413741 + t * (0.5 * -1.453152027 + t * (0.5 * 1.061405429)))))
    tail = tail * bell
    normal = jnp.where(upper < 0, tail, 1.0 - tail)
    return upper * normal, normal + upper * (bell * (1.0 / math.sqrt(2.0 * math.pi)))


def row_norm(values):
    centre = values - jnp.mean(values, axis=-1, keepdims=True)
    inverse = lax.rsqrt(jnp.mean(centre * centre, axis=-1, keepdims=True) + norm_epsilon)
    return centre * inverse, inverse


def dot(a, b):
    return jnp.dot(a, b, preferred_element_type=f32)


def dot_nt(a, b):
    return lax.dot_general(a, b, (((1,), (1,)), ((), ())), preferred_element_type=f32)


def dot_tn(a, b):
    return lax.dot_general(a, b, (((0,), (0,)), ((), ())), preferred_element_type=f32)


def roll_if(flag, value):
    return jnp.where(flag == 1, jnp.concatenate([value[4:], value[:4]]), value)


def forward_kernel(n, micro_count, visible, valid_mask, gain_one, shift_one, gain_two, shift_two, b_up, patches, w_qkv, w_out, w_up, w_down,
                   loss_out, grad_out, got, grad_rows, active_grad, masks, tokens_out, one_out, packed_out, probs_out, att_out, mixed_out, two_out, slope_out,
                   cells, tok, info_in, there, wq, wo, wu, wd, one_t, packed, probs, att_t, mixed, two_t, slope, upper, active, hidden, attended, turned,
                   active_sum, share, every, send_sem, recv_sem, sum_send, sum_recv, isem, wsem, osem, tsem, xsem):
    me = lax.axis_index("dp")
    kind = (me // 8) % 2
    images, slots, width = info_in.shape[0], info_in.shape[2], tok.shape[2]
    rows = images * slots
    per_micro = visible.shape[1]
    ff = wu.shape[2]

    read_cells = pltpu.make_async_copy(patches, cells, isem)
    read_cells.start()
    reads = []
    for slot, which in ((0, kind), (1, 1 - kind)):
        reads.append([pltpu.make_async_copy(source.at[which], target.at[slot], wsem.at[slot, number])
                      for number, (source, target) in enumerate(((w_qkv, wq), (w_out, wo), (w_up, wu), (w_down, wd)))])
    for copy in reads[0] + reads[1]:
        copy.start()
    barrier = pltpu.get_barrier_semaphore()

    def greet(step, carry):
        pl.semaphore_signal(barrier, inc=1, device_id=(lax.rem(me + step, n),), device_id_type=MESH)
        return carry

    lax.fori_loop(1, n, greet, 0)

    for image in range(images):
        seen = visible[image // per_micro, image % per_micro : image % per_micro + 1, :].astype(f32)
        grid_row = jnp.floor((seen + 0.5) * (1.0 / GRID))
        valid = valid_mask[image // per_micro, image % per_micro : image % per_micro + 1, :].astype(f32)
        info_in[image] = jnp.concatenate([grid_row, seen - GRID * grid_row, valid, seen, jnp.zeros((4, slots), f32)])
    read_cells.wait()

    def pick(modality, place):
        def one(image, carry):
            seen = info_in[image, 3:4, :]
            picked = jnp.where(lax.broadcasted_iota(jnp.int32, (cells.shape[2], slots), 0).astype(f32) == seen, 1.0, 0.0).astype(bf16)
            tok[place + image] = dot_tn(picked, cells[image, modality])
            return carry

        lax.fori_loop(0, images, one, 0)

    pick(1 - kind, 2 * images)
    pl.semaphore_wait(barrier, n - 1)
    send_tokens = [
        pltpu.make_async_remote_copy(src_ref=info_in, dst_ref=there, send_sem=xsem.at[0, 0], recv_sem=xsem.at[0, 1], device_id=(me ^ 8,), device_id_type=MESH),
        pltpu.make_async_remote_copy(src_ref=tok.at[pl.ds(2 * images, images)], dst_ref=tok.at[pl.ds(images, images)],
                                     send_sem=xsem.at[1, 0], recv_sem=xsem.at[1, 1], device_id=(me ^ 8,), device_id_type=MESH)]
    for copy in send_tokens:
        copy.start()
    pick(kind, 0)

    def store_tokens(place):
        at = pl.ds(place * images, images)
        return pltpu.make_async_copy(tok.at[at], tokens_out.at[at], tsem.at[place])

    store_tokens(0).start()
    store_tokens(2).start()

    stores = {}

    def ready(number):
        if number in stores:
            stores.pop(number).wait()

    def store(number, place):
        source, target = ((one_t, one_out), (packed, packed_out), (probs, probs_out), (att_t, att_out), (mixed, mixed_out), (two_t, two_out), (slope, slope_out))[number]
        copy = pltpu.make_async_copy(source, target.at[pl.ds(place * images, images)], osem.at[number])
        copy.start()
        stores[number] = copy

    low_half = lax.broadcasted_iota(jnp.int32, (slots, 128), 1) < HEAD_DIM
    row_of = lax.broadcasted_iota(jnp.int32, (8, slots), 0)

    def marks_of(info):
        return jnp.concatenate([jnp.where(row_of == image, info[image, 2:3, :], 0.0) for image in range(images)], axis=1).astype(bf16)

    def group(place, slot, which, info, whole, pauses):
        gain1, shift1 = gain_one[pl.ds(which, 1), :], shift_one[pl.ds(which, 1), :]
        gain2, shift2 = gain_two[pl.ds(which, 1), :], shift_two[pl.ds(which, 1), :]

        def norm(source, first, target, gain, shift):
            def one(image, carry):
                for r in range(0, slots, ROWS):
                    normed, _ = row_norm(source[first + image, r : r + ROWS, :])
                    hidden[image, r : r + ROWS, :] = (normed * gain + shift).astype(bf16)
                target[image] = hidden[image].T.reshape(target.shape[1:])
                return carry

            lax.fori_loop(0, images, one, 0)

        ready(0)
        norm(tok, place * images, one_t, gain1, shift1)
        store(0, place)
        ready(1)
        if pauses is None:
            reads[slot][0].wait()

        def project(i, carry):
            at = pl.ds(pl.multiple_of(i * 768, 768), 768)
            packed[:, :, at] = dot(hidden[...].reshape(rows, width), wq[slot, :, at]).astype(bf16).reshape(images, slots, 768)
            return carry

        lax.fori_loop(0, 3 * width // 768, project, 0)
        store(1, place)
        if pauses:
            pauses[0]()
        ready(2)
        ready(3)

        def attend(image, carry):
            line = info[image]
            column = line.T
            gap_r = column[:, 0:1] - line[0:1, :]
            gap_c = column[:, 1:2] - line[1:2, :]
            away = -jnp.sqrt(gap_r * gap_r + gap_c * gap_c)
            away = jnp.where(column[:, 2:3] > 0, away, -1e33)
            for pair in range(HEADS // 2):
                at = slice(pair * 128, pair * 128 + 128)
                queries = packed[image, :, pair * 128 : pair * 128 + 128]
                keys = packed[image, :, width + pair * 128 : width + pair * 128 + 128]
                values = packed[image, :, 2 * width + pair * 128 : 2 * width + pair * 128 + 128]
                blank = jnp.zeros_like(keys)
                two_keys = jnp.concatenate([jnp.where(low_half, keys, blank), jnp.where(low_half, blank, keys)])
                two_values = jnp.concatenate([jnp.where(low_half, values, blank), jnp.where(low_half, blank, values)])
                scores = dot_nt(two_keys, queries)
                shares = []
                for side in (0, 1):
                    one = scores[side * slots : side * slots + slots] * head_scale + SLOPES[2 * pair + side] * away
                    power = jnp.exp(one - jnp.max(one, axis=0, keepdims=True))
                    shares.append((power * (1.0 / jnp.sum(power, axis=0, keepdims=True))).astype(bf16))
                both_shares = jnp.concatenate(shares)
                probs[image, pair] = both_shares
                flipped = dot_tn(two_values, both_shares).astype(bf16)
                turned[at, :] = flipped
                attended[image, :, at] = flipped.T
            att_t[image] = turned[...].reshape(att_t.shape[1:])
            return carry

        lax.fori_loop(0, images, attend, 0)
        store(2, place)
        store(3, place)
        if pauses:
            pauses[1]()
        ready(4)
        if pauses is None:
            reads[slot][1].wait()

        def output(i, carry):
            at = pl.ds(pl.multiple_of(i * 256, 256), 256)
            mixed[:, :, at] = tok[pl.ds(place * images, images), :, at] + dot(attended[...].reshape(rows, width), wo[slot, :, at]).reshape(images, slots, 256)
            return carry

        lax.fori_loop(0, width // 256, output, 0)
        store(4, place)
        ready(5)
        norm(mixed, 0, two_t, gain2, shift2)
        store(5, place)
        if pauses:
            pauses[2]()
        ready(6)
        if pauses is None:
            reads[slot][2].wait()
        marks = marks_of(info)

        def columns(i):
            return pl.ds(pl.multiple_of(i * WIDE, WIDE), WIDE)

        def rise(i, slot_up):
            upper[slot_up] = dot(hidden[...].reshape(rows, width), wu[slot, :, columns(i)])

        def bend(i, now):
            bias = b_up[pl.ds(which, 1), columns(i)]
            for r in range(0, rows, GROWS):
                value, back = gelu_pair(upper[now, r : r + GROWS, :] + bias)
                if whole:
                    active[r : r + GROWS, :] = value.astype(bf16)
                slope[r // slots, r % slots : r % slots + GROWS, columns(i)] = back.astype(bf16)
            if whole:
                active_sum[slot, :, columns(i)] = dot(marks, active[...])

        rise(0, 0)

        def feed(i, carry):
            rise(2 * i + 1, 1)
            bend(2 * i, 0)
            rise(2 * i + 2, 0)
            bend(2 * i + 1, 1)
            return carry

        steps = ff // WIDE
        lax.fori_loop(0, steps // 2 - 1, feed, 0)
        rise(steps - 1, 1)
        bend(steps - 2, 0)
        bend(steps - 1, 1)
        store(6, place)
        if not whole:
            return None
        reads[slot][3].wait()
        total = active_sum[slot]
        high = total.astype(bf16)
        rest = total - high.astype(f32)
        middle = rest.astype(bf16)
        lowest = (rest - middle.astype(f32)).astype(bf16)
        stacked = jnp.concatenate([high, middle, lowest, jnp.zeros_like(high)])
        parts = dot(stacked, wd[slot])
        downs = parts[0:8] + parts[8:16] + parts[16:24]
        sums, counts = [], []
        for image in range(images):
            weight = info[image].T[:, 2:3]
            sums.append(jnp.sum(mixed[image] * weight, axis=0, keepdims=True))
            counts.append(jnp.sum(weight, axis=0, keepdims=True))
        count = jnp.concatenate(counts + [jnp.ones((8 - images, 1), f32)])
        pooled = (jnp.concatenate(sums + [jnp.zeros((8 - images, width), f32)]) + downs) / count
        share[which] = roll_if(which, total / count)
        return roll_if(which, pooled)

    def copies(sources, flip, first):
        made = []
        for number, source in enumerate(sources):
            made.append(pltpu.make_async_remote_copy(
                src_ref=every.at[source], dst_ref=every.at[source], send_sem=send_sem.at[first + number], recv_sem=recv_sem.at[first + number],
                device_id=(me ^ flip,), device_id_type=MESH))
        for copy in made:
            copy.start()
        return made

    def finish(made):
        for copy in made:
            copy.wait()

    pooled = group(0, 0, kind, info_in, True, None)
    every[me] = pooled + group(2, 1, 1 - kind, info_in, True, None)

    waves = [copies([me], flip, number) [0] for number, flip in enumerate((8, 16, 24))]
    held = [me, me ^ 8, me ^ 16, me ^ 24]
    state = {"wave": waves, "held": held}

    def next_wave(flip, first):
        def run():
            finish(state["wave"])
            state["wave"] = copies(state["held"], flip, first)
            state["held"] = state["held"] + [one ^ flip for one in state["held"]]
        return run

    def sums_out(step, carry):
        peer = lax.rem(me + step, n)
        at = pl.ds(pl.multiple_of(((peer % (n // 2)) // 2) * 384, 384), 384)
        pltpu.make_async_remote_copy(
            src_ref=share.at[peer // (n // 2), :, at], dst_ref=got.at[me], send_sem=sum_send.at[step], recv_sem=sum_recv.at[step],
            device_id=(peer,), device_id_type=MESH).start()
        return carry

    def last_wave():
        next_wave(1, 15)()
        lax.fori_loop(1, n, sums_out, 0)

    send_tokens[0].wait()
    send_tokens[1].wait()
    store_tokens(1).start()
    group(1, 0, kind, there, False, [next_wave(4, 3), next_wave(2, 7), last_wave])
    finish(state["wave"])
    loss, grad = contrast(every[...].reshape(n * 8, width), 8, micro_count)
    loss_out[...] = loss
    grad_out[...] = grad
    got[me] = share[me // (n // 2), :, pl.ds(pl.multiple_of(((me % (n // 2)) // 2) * 384, 384), 384)]

    def per_slot(device, which, info):
        count = jnp.concatenate([jnp.sum(info[image, 2:3, :], axis=1, keepdims=True) for image in range(images)])
        return roll_if(which, grad_out[pl.ds(pl.multiple_of(device * 8, 8), 8), :])[0:images] / count

    spread = jnp.concatenate([per_slot(me, kind, info_in), per_slot(me ^ 8, kind, there), per_slot(me, 1 - kind, info_in), jnp.zeros((24 - 3 * images, width), f32)])
    grad_rows[...] = spread
    low = spread[0:16].astype(bf16)
    for j in range(0, ff, width):
        active_grad[:, j : j + width] = dot_nt(low, wd[0, j : j + width, :])
    lines = [info[image, 2:3, :] for info in (info_in, there, info_in) for image in range(images)]
    masks[...] = jnp.concatenate(lines + [jnp.zeros((slots - 3 * images, slots), f32)]).T

    def sums_in(step, carry):
        peer = lax.rem(me + n - step, n)
        pltpu.make_async_remote_copy(
            src_ref=share.at[0, :, pl.ds(0, 384)], dst_ref=got.at[peer], send_sem=sum_send.at[step], recv_sem=sum_recv.at[step],
            device_id=(peer,), device_id_type=MESH).wait()
        return carry

    lax.fori_loop(1, n, sums_in, 0)
    for number in range(7):
        ready(number)
    for place in range(3):
        store_tokens(place).wait()


def forward(n, visible, valid_mask, patches, weights):
    gain_one, shift_one, w_qkv, w_out, gain_two, shift_two, w_up, b_up, w_down = weights
    micro_count, per_micro, slots = visible.shape
    images = micro_count * per_micro
    width, ff = w_up.shape[1:]
    anywhere, vmem = pl.BlockSpec(memory_space=pl.ANY), pl.BlockSpec(memory_space=pltpu.VMEM)
    turned = (16, width // 16, slots)
    kept = [(turned, bf16), ((slots, 3 * width), bf16), ((HEADS // 2, 2 * slots, slots), bf16), (turned, bf16), ((slots, width), f32),
            (turned, bf16), ((slots, ff), bf16)]
    return pl.pallas_call(
        functools.partial(forward_kernel, n, micro_count),
        out_shape=[jax.ShapeDtypeStruct(shape, f32) for shape in
                   ((1, 1), (8 * n, width), (n, 8, 384), (24, width), (16, ff), (slots, slots), (3 * images, slots, width))]
        + [jax.ShapeDtypeStruct((3 * images,) + dims, dtype) for dims, dtype in kept],
        in_specs=[vmem] * 7 + [anywhere] * 5,
        out_specs=[vmem] * 6 + [anywhere] * 8,
        scratch_shapes=[
            pltpu.VMEM(patches.shape, bf16),
            pltpu.VMEM((3 * images, slots, width), f32),
            pltpu.VMEM((images, 8, slots), f32),
            pltpu.VMEM((images, 8, slots), f32),
            pltpu.VMEM(w_qkv.shape, bf16), pltpu.VMEM(w_out.shape, bf16), pltpu.VMEM(w_up.shape, bf16), pltpu.VMEM(w_down.shape, bf16)]
        + [pltpu.VMEM((images,) + dims, dtype) for dims, dtype in kept]
        + [
            pltpu.VMEM((2, images * slots, WIDE), f32),
            pltpu.VMEM((images * slots, WIDE), bf16),
            pltpu.VMEM((images, slots, width), bf16),
            pltpu.VMEM((images, slots, width), bf16),
            pltpu.VMEM((width, slots), bf16),
            pltpu.VMEM((2, 8, ff), f32),
            pltpu.VMEM((2, 8, ff), f32),
            pltpu.VMEM((n, 8, width), f32),
            pltpu.SemaphoreType.DMA((31,)),
            pltpu.SemaphoreType.DMA((31,)),
            pltpu.SemaphoreType.DMA((n,)),
            pltpu.SemaphoreType.DMA((n,)),
            pltpu.SemaphoreType.DMA,
            pltpu.SemaphoreType.DMA((2, 4)),
            pltpu.SemaphoreType.DMA((7,)),
            pltpu.SemaphoreType.DMA((3,)),
            pltpu.SemaphoreType.DMA((2, 2)),
        ],
        compiler_params=pltpu.CompilerParams(collective_id=0, has_side_effects=True, vmem_limit_bytes=63 << 20),
    )(visible, valid_mask, gain_one, shift_one, gain_two, shift_two, b_up, patches, w_qkv, w_out, w_up, w_down)


CHUNK = 384


def meet(peers):
    barrier = pltpu.get_barrier_semaphore()
    for peer in peers:
        pl.semaphore_signal(barrier, inc=1, device_id=(peer,), device_id_type=MESH)
    pl.semaphore_wait(barrier, len(peers))


def finish_kernel(visible, first, second, extra, loss, up, out, qkv, down,
                  cells, gain_one, shift_one, gain_two, shift_two, bias, loss_out, up_out, out_out, qkv_out, down_out):
    step = pl.program_id(0)
    images = visible.shape[1]
    for source, target in ((up, up_out), (out, out_out), (qkv, qkv_out), (down, down_out)):
        target[...] = source[...]

    @pl.when(step == 0)
    def _():
        rows = extra.shape[0]
        lines = jnp.concatenate([extra[...], jnp.zeros((128 - rows, 128), f32)]).T
        for number, target in enumerate((gain_one, shift_one, gain_two, shift_two)):
            target[...] = lines[number : number + 1, 0:rows]
        bias[...] = jnp.concatenate([lines[4 + k : 5 + k, 0:rows] for k in range(4)], axis=1)
        loss_out[...] = loss[...]

    patch_count, slots = cells.shape[1], visible.shape[2]
    seen = visible[step // images, pl.ds(step % images, 1), :]
    picked = jnp.where(lax.broadcasted_iota(jnp.int32, (patch_count, slots), 0) == seen, 1.0, 0.0).astype(bf16)
    for modality, grads in enumerate((first, second)):
        value = grads[0]
        high = value.astype(bf16)
        rest = (value - high.astype(f32)).astype(bf16)
        cells[0, :, modality, :] = dot(picked, high) + dot(picked, rest)


def finish(visible, grads, patch_count, extra, loss, passed):
    total, slots, width = grads.shape
    images = total // 2
    rows = extra.shape[0]
    whole = pl.BlockSpec(memory_space=pltpu.VMEM)
    pieces = [pl.BlockSpec((rows, width), lambda i: (0, i)), pl.BlockSpec((rows, width), lambda i: (0, 0)),
              pl.BlockSpec((rows, width), lambda i: (0, jnp.minimum(i, 2))), pl.BlockSpec((1, rows, width), lambda i: (i // 2, i % 2, 0))]
    return pl.pallas_call(
        finish_kernel,
        grid=(images,),
        in_specs=[whole, pl.BlockSpec((1, slots, width), lambda i: (i, 0, 0)), pl.BlockSpec((1, slots, width), lambda i: (images + i, 0, 0)), whole, whole]
        + pieces,
        out_specs=[pl.BlockSpec((1, patch_count, 2, width), lambda i: (i, 0, 0, 0))] + [whole] * 6 + pieces,
        out_shape=[jax.ShapeDtypeStruct((images, patch_count, 2, width), f32)] + [jax.ShapeDtypeStruct((1, rows), f32)] * 4
        + [jax.ShapeDtypeStruct((1, 4 * rows), f32), jax.ShapeDtypeStruct((1, 1), f32)] + [jax.ShapeDtypeStruct(one.shape, f32) for one in passed],
        compiler_params=pltpu.CompilerParams(vmem_limit_bytes=62 << 20),
    )(visible, grads, grads, extra, loss, *passed)


def backward_kernel(own, grad_rows, first_active, masks, gain_one, gain_two, got, grad_all, tokens, one_t, packed, probs, att_t, mixed, two_t, slope,
                    w_qkv, w_out, w_up, w_down,
                    up_out, out_out, qkv_out, extra_out, tokens_out, down_out,
                    mine, ring, core_got, first_got, second_got, owner_got,
                    extra, extra_mine, extra_core, extra_first, extra_second, extra_owner,
                    wide, mixed_grad, mixed_low, turned, weights, active_grad, sums, packs, shares, rows_in, rows_out, hidden_grad,
                    sems, extra_sems, wsem, dsem, tsem, psem, rsem, osem):
    me = lax.axis_index("dp")
    core, xx, yy, zz = me % 2, (me // 2) % 2, (me // 4) % 2, me // 8
    kind, low_z = zz % 2, zz // 2
    slots, width = mixed.shape[1:]
    ff = slope.shape[2]
    both = 2 * own
    pairs = 2 * ff // width
    up_pairs = ff // width

    def load_slope(place, count, j):
        at = pl.ds(pl.multiple_of(j * width, 128), width)
        return pltpu.make_async_copy(slope.at[pl.ds(place, count), :, at], wide.at[pl.ds(0, count), :, at], dsem.at[j])

    def load_down(which, j):
        at = pl.ds(pl.multiple_of(j * width, 128), width)
        return pltpu.make_async_copy(w_down.at[which, at, :], weights.at[1, :, at], wsem.at[j])

    def load_up(which):
        return pltpu.make_async_copy(w_up.at[which], weights.at[0], wsem.at[4])

    def load_rest(which):
        return (pltpu.make_async_copy(w_qkv.at[which], weights.at[1, :, pl.ds(0, 3 * width)], wsem.at[5]),
                pltpu.make_async_copy(w_out.at[which], weights.at[1, :, pl.ds(3 * width, width)], wsem.at[6]))

    def load_turned(source, slot, image, part):
        return pltpu.make_async_copy(
            source.at[image, :, part], turned.at[slot, part, :, :, pl.ds(pl.multiple_of(image * slots, 128), slots)], tsem.at[slot, part, image])

    def all_turned(source, slot, act):
        def one(image, carry):
            for part in (0, 1):
                act(load_turned(source, slot, image, part))
            return carry

        lax.fori_loop(0, both, one, 0)

    def begin(copy):
        copy.start()

    def finish(copy):
        copy.wait()

    load_slope(0, both, 0).start()
    all_turned(two_t, 0, begin)
    for j in range(1, up_pairs):
        load_slope(0, both, j).start()
    load_up(kind).start()
    all_turned(att_t, 1, begin)
    for copy in load_rest(kind):
        copy.start()

    meet([me ^ 1, me ^ 2, me ^ 4, me ^ 8, me ^ 16, me ^ 24])

    def sem(stage, chunk, way):
        return sems.at[stage, chunk, way]

    def chunk_sem(chunk, stage, way):
        return sems.at[stage, chunk, way]

    def extra_sem(stage, way):
        return extra_sems.at[stage, way]

    def remote(src, dst, send, recv, flip):
        return pltpu.make_async_remote_copy(src_ref=src, dst_ref=dst, send_sem=send, recv_sem=recv, device_id=(me ^ flip,), device_id_type=MESH)

    def to_core(chunk):
        return remote(ring.at[(chunk // 2) % 2, chunk % 2], core_got.at[chunk], sem(1, chunk, 0), sem(1, chunk, 1), 1)

    def first(chunk, along_x):
        src = mine.at[chunk, :, :, 1 - xx] if along_x else mine.at[chunk, :, 1 - yy]
        return remote(src, first_got.at[chunk], sem(2, chunk, 0), sem(2, chunk, 1), 2 if along_x else 4)

    def second(chunk, along_x):
        src = mine.at[chunk, :, 1 - yy, xx] if along_x else mine.at[chunk, :, yy, 1 - xx]
        return remote(src, second_got.at[chunk], sem(3, chunk, 0), sem(3, chunk, 1), 4 if along_x else 2)

    def third(source, owner, send, recv, half):
        target = 2 * kind + half
        return target, pltpu.make_async_remote_copy(
            src_ref=source.at[half, yy, xx], dst_ref=owner.at[low_z], send_sem=send, recv_sem=recv,
            device_id=(target * 8 + me % 8,), device_id_type=MESH)

    def start_third(source, owner, semaphore):
        for half in (0, 1):
            target, copy = third(source, owner, semaphore(4, half), semaphore(5, low_z), half)

            @pl.when(target != zz)
            def _():
                copy.start()

            @pl.when(target == zz)
            def _():
                owner[low_z] = source[half, yy, xx]

    def wait_third(source, owner, semaphore):
        for half in (0, 1):
            target, copy = third(source, owner, semaphore(4, half), semaphore(5, low_z), half)

            @pl.when(target != zz)
            def _():
                copy.wait_send()

        for origin in (0, 1):
            @pl.when(2 * origin + low_z != zz)
            def _():
                remote(source.at[0, yy, xx], owner.at[origin], semaphore(4, 0), semaphore(5, origin), 8).wait_recv()

    def run_first(pair):
        for odd in (0, 1):
            chunk = 2 * pair + odd
            to_core(chunk).wait_recv()
            mine[chunk] = mine[chunk] + core_got[chunk]
            first(chunk, odd == 0).start()

    def run_second(pair):
        for odd in (0, 1):
            chunk = 2 * pair + odd
            first(chunk, odd == 0).wait()
            if odd == 0:
                mine[chunk, :, :, xx] = mine[chunk, :, :, xx] + first_got[chunk]
            else:
                mine[chunk, :, yy] = mine[chunk, :, yy] + first_got[chunk]
            second(chunk, odd == 0).start()

    def run_third(pair):
        for odd in (0, 1):
            chunk = 2 * pair + odd
            second(chunk, odd == 0).wait()
            mine[chunk, :, yy, xx] = mine[chunk, :, yy, xx] + second_got[chunk]
            start_third(mine.at[chunk], owner_got.at[chunk], functools.partial(chunk_sem, chunk))

    def write(chunk, target, base):
        at = pl.ds(pl.multiple_of((chunk - 2 * base) * CHUNK, 128), CHUNK)
        return pltpu.make_async_copy(owner_got.at[chunk, 0], target.at[:, at], sem(0, chunk, 0))

    outputs = ((up_out, 0, up_pairs), (out_out, up_pairs, up_pairs + 1), (qkv_out, up_pairs + 1, pairs))

    def run_last(target, base, pair):
        for odd in (0, 1):
            chunk = 2 * pair + odd
            wait_third(mine.at[chunk], owner_got.at[chunk], functools.partial(chunk_sem, chunk))
            owner_got[chunk, 0] = owner_got[chunk, 0] + owner_got[chunk, 1]
            write(chunk, target, base).start()

    def serve(run, low, high):
        def one(pair, carry):
            run(pair)
            return carry

        lax.fori_loop(low, high, one, 0)

    def terms(pair, slot, block, reused=True):
        if reused:
            for odd in (0, 1):
                to_core(2 * (pair - 2) + odd).wait_send()
        for part, row_half in ((0, core), (1, 1 - core)):
            left = turned[slot, row_half].reshape(8 * 48, both * slots)
            if block is None:
                right = mixed_low[...]
            else:
                right = wide[:, :, pl.ds(pl.multiple_of(block * width, 128), width)]
            got = dot(left, right.reshape(both * slots, width))
            for odd in (0, 1):
                piece = got[:, odd * CHUNK : odd * CHUNK + CHUNK].reshape(2, 2, 2, 48, CHUNK)
                if part == 0:
                    mine[2 * pair + odd] = piece
                else:
                    ring[pair % 2, odd] = piece
        for odd in (0, 1):
            to_core(2 * pair + odd).start()

    lanes = lax.broadcasted_iota(jnp.int32, (slots, 128), 1)

    def mask_of(place):
        return jnp.sum(jnp.where(lanes == place, masks[...], 0.0), axis=1, keepdims=True)

    def make_active_grad(first_row, which):
        low = grad_rows[first_row : first_row + 16].astype(bf16)
        for j in range(up_pairs):
            load_down(which, j).wait()
            active_grad[:, j * width : (j + 1) * width] = dot_nt(low, weights[1, :, j * width : (j + 1) * width])
        for copy in load_rest(which):
            copy.start()

    def upper_grad(j, place, count):
        at = pl.ds(pl.multiple_of(j * width, 128), width)
        load_slope(place, count, j).wait()

        def one(image, carry):
            row = active_grad[pl.ds(image, 1), at]
            weight = mask_of(place + image)
            for r in range(0, slots, ROWS):
                value = wide[image, r : r + ROWS, at].astype(f32) * (row * weight[r : r + ROWS])
                wide[image, r : r + ROWS, at] = value.astype(bf16)
            return carry

        lax.fori_loop(0, count, one, 0)

    active_grad[...] = first_active[...]
    all_turned(two_t, 0, finish)
    ones = jnp.full((128, both * slots), 1.0, bf16)

    def up_pair(j, carry):
        upper_grad(j, 0, both)

        @pl.when(j >= 2)
        def _():
            for odd in (0, 1):
                to_core(2 * (j - 2) + odd).wait_send()

        right = wide[:, :, pl.ds(pl.multiple_of(j * width, 128), width)].reshape(both * slots, width)
        @pl.when((j >= 1) & (j <= 2))
        def _():
            run_first(j - 1)

        terms(j, 0, j, False)

        bias = dot(ones, right).T.reshape(4, 4, 48, 128)
        lane = lax.broadcasted_iota(jnp.int32, (4, 48, 128), 2)
        spread = jnp.zeros((4, 48, 128), f32)
        for k in range(4):
            spread = spread + jnp.where(lane == 4 + k, bias[:, k], 0.0)
        extra[j // 2, j % 2] = spread.reshape(2, 2, 48, 128)
        return carry

    lax.fori_loop(0, up_pairs, up_pair, 0)
    sums[...] = jnp.zeros_like(sums)

    def hidden_two_back(count):
        def one(k, carry):
            flat = wide[0:count].reshape(count * slots, ff)
            at = pl.ds(pl.multiple_of(k * 256, 256), 256)
            mixed_grad[0:count, :, at] = dot_nt(flat, weights[0, at, :]).reshape(count, slots, 256)
            return carry

        lax.fori_loop(0, width // 256, one, 0)

    def norm_back(rows, grad, gain):
        normed, inverse = row_norm(rows)
        scaled = grad * gain
        back = inverse * (scaled - jnp.mean(scaled, axis=-1, keepdims=True) - normed * jnp.mean(scaled * normed, axis=-1, keepdims=True))
        return normed, back

    def run_hooks(hooks, at):
        for when, act in (hooks or {}).items():
            @pl.when(at == when)
            def _():
                act()

    def fold(values):
        return jnp.sum(values.reshape(ROWS // 8, 8, width), axis=0)

    def norm_two_back(place, count, keep, hooks=None):
        gain = gain_two[pl.ds(kind if keep else 1 - kind, 1), :]

        def load(image):
            return pltpu.make_async_copy(mixed.at[place + image], rows_in.at[image % 2], rsem.at[image % 2])

        load(0).start()

        def one(image, carry):
            @pl.when(image + 1 < count)
            def _():
                load(image + 1).start()

            load(image).wait()
            weight = mask_of(place + image)
            grad_row = grad_rows[pl.ds(place + image, 1), :]
            held, first_sum, second_sum = [], 0.0, 0.0
            for r in range(0, slots, ROWS):
                grad = mixed_grad[image, r : r + ROWS, :]
                normed, back = norm_back(rows_in[image % 2, r : r + ROWS, :], grad, gain)
                value = weight[r : r + ROWS] * grad_row + back
                mixed_low[image, r : r + ROWS, :] = value.astype(bf16)
                held.append(value)
                if keep:
                    first_sum = first_sum + fold(grad * normed)
                    second_sum = second_sum + fold(grad)
            mixed_grad[image] = jnp.concatenate(held)
            if keep:
                sums[2] = sums[2] + first_sum
                sums[3] = sums[3] + second_sum
            run_hooks(hooks, image)
            return carry

        lax.fori_loop(0, count, one, 0)

    def attended_back(count):
        for k in range(0, width, 256):
            flat = mixed_low[0:count].reshape(count * slots, width)
            got = dot_nt(flat, weights[1, k : k + 256, 3 * width : 4 * width])
            wide[0:count, :, 3 * width + k : 3 * width + k + 256] = got.astype(bf16).reshape(count, slots, 256)

    low_half = lax.broadcasted_iota(jnp.int32, (slots, 128), 1) < HEAD_DIM

    def attention_back(place, count, hooks=None):
        def load(image):
            return (pltpu.make_async_copy(packed.at[place + image], packs.at[image % 2], psem.at[0, image % 2]),
                    pltpu.make_async_copy(probs.at[place + image], shares.at[image % 2], psem.at[1, image % 2]))

        for copy in load(0):
            copy.start()

        def one(image, carry):
            @pl.when(image + 1 < count)
            def _():
                for copy in load(image + 1):
                    copy.start()

            for copy in load(image):
                copy.wait()
            now = image % 2
            for pair in range(HEADS // 2):
                at = slice(pair * 128, pair * 128 + 128)
                queries = packs[now, :, pair * 128 : pair * 128 + 128]
                keys = packs[now, :, width + pair * 128 : width + pair * 128 + 128]
                values = packs[now, :, 2 * width + pair * 128 : 2 * width + pair * 128 + 128]
                grad = wide[image, :, 3 * width + pair * 128 : 3 * width + pair * 128 + 128]
                share = shares[now, pair]
                blank = jnp.zeros_like(keys)
                two_keys = jnp.concatenate([jnp.where(low_half, keys, blank), jnp.where(low_half, blank, keys)])
                two_values = jnp.concatenate([jnp.where(low_half, values, blank), jnp.where(low_half, blank, values)])
                grad_share = dot_nt(two_values, grad)
                backs = []
                for side in (0, 1):
                    part = slice(side * slots, side * slots + slots)
                    weight = share[part].astype(f32)
                    product = weight * grad_share[part]
                    backs.append((product - weight * jnp.sum(product, axis=0, keepdims=True)).astype(bf16))
                back = jnp.concatenate(backs)
                grad_values = dot(share, grad)
                grad_keys = dot(back, queries) * head_scale
                grad_queries = dot_tn(back, two_keys) * head_scale
                wide[image, :, pair * 128 : pair * 128 + 128] = grad_queries.astype(bf16)
                wide[image, :, width + pair * 128 : width + pair * 128 + 128] = jnp.where(low_half, grad_keys[:slots], grad_keys[slots:]).astype(bf16)
                wide[image, :, 2 * width + pair * 128 : 2 * width + pair * 128 + 128] = jnp.where(low_half, grad_values[:slots], grad_values[slots:]).astype(bf16)
            run_hooks(hooks, image)
            return carry

        lax.fori_loop(0, count, one, 0)

    def norm_one_back(place, count, keep, out_place, out_count, hooks=None):
        gain = gain_one[pl.ds(kind if keep else 1 - kind, 1), :]

        def load(step):
            return pltpu.make_async_copy(tokens.at[pl.ds(place + 2 * step, 2)], rows_in, rsem.at[0])

        def store(step):
            return pltpu.make_async_copy(rows_out, tokens_out.at[pl.ds(out_place + 2 * step, 2)], osem.at[0])

        load(0).start()

        def one(step, carry):
            flat = wide[pl.ds(2 * step, 2), :, 0 : 3 * width].reshape(2 * slots, 3 * width)
            hidden_grad[...] = dot_nt(flat, weights[1, :, 0 : 3 * width])
            load(step).wait()

            @pl.when((step >= 1) & (step - 1 < out_count // 2))
            def _():
                store(step - 1).wait()

            for side in (0, 1):
                first_sum, second_sum = 0.0, 0.0
                for r in range(0, slots, ROWS):
                    grad = hidden_grad[side * slots + r : side * slots + r + ROWS, :]
                    normed, back = norm_back(rows_in[side, r : r + ROWS, :], grad, gain)
                    rows_out[side, r : r + ROWS, :] = mixed_grad[2 * step + side, r : r + ROWS, :] + back
                    if keep:
                        first_sum = first_sum + fold(grad * normed)
                        second_sum = second_sum + fold(grad)
                if keep:
                    sums[0] = sums[0] + first_sum
                    sums[1] = sums[1] + second_sum

            @pl.when(step + 1 < count // 2)
            def _():
                load(step + 1).start()

            @pl.when(step < out_count // 2)
            def _():
                store(step).start()

            run_hooks(hooks, step)
            return carry

        lax.fori_loop(0, count // 2, one, 0)
        if count == out_count:
            store(count // 2 - 1).wait()

    def serving(*jobs):
        def act():
            for run, pair in jobs:
                run(pair)
        return act

    def step(k):
        run_second(k)
        if k + 2 < pairs:
            run_first(k + 2)
        if k >= 1:
            run_third(k - 1)

    step(0)
    load_up(kind).wait()
    hidden_two_back(both)
    load_up(1 - kind).start()
    all_turned(one_t, 0, begin)
    norm_two_back(0, both, True, {3: lambda: step(1)})
    all_turned(att_t, 1, finish)
    terms(up_pairs, 1, None)
    for copy in load_rest(kind):
        copy.wait()
    attended_back(both)
    attention_back(0, both, {3: lambda: step(2)})
    all_turned(one_t, 0, finish)
    terms(up_pairs + 1, 0, 0)
    step(3)
    terms(up_pairs + 2, 0, 1)
    terms(pairs - 1, 0, 2)
    norm_one_back(0, both, True, kind * own, own, {2: lambda: step(4)})

    vectors = jnp.concatenate([jnp.sum(sums[k], axis=0, keepdims=True) for k in range(4)] + [jnp.zeros((124, width), f32)])
    extra[...] = extra[...] + vectors.T.reshape(extra.shape)
    extra_mine[...] = extra[:, :, :, core]
    extra_to_core = remote(extra.at[:, :, :, 1 - core], extra_core, extra_sems.at[1, 0], extra_sems.at[1, 1], 1)
    extra_first_copy = remote(extra_mine.at[:, :, 1 - xx], extra_first, extra_sems.at[2, 0], extra_sems.at[2, 1], 2)
    extra_second_copy = remote(extra_mine.at[:, 1 - yy, xx], extra_second, extra_sems.at[3, 0], extra_sems.at[3, 1], 4)
    extra_to_core.start()

    for j in range(up_pairs):
        load_slope(both, own, j).start()
        load_down(1 - kind, j).start()
    make_active_grad(both, 1 - kind)

    def other_pair(j, carry):
        upper_grad(j, both, own)
        return carry

    lax.fori_loop(0, up_pairs, other_pair, 0)
    step(5)
    extra_to_core.wait()
    extra_mine[...] = extra_mine[...] + extra_core[...]
    extra_first_copy.start()
    load_up(1 - kind).wait()
    hidden_two_back(own)
    norm_two_back(both, own, False)
    for copy in load_rest(1 - kind):
        copy.wait()
    attended_back(own)
    attention_back(both, own)
    step(6)
    extra_first_copy.wait()
    extra_mine[:, :, xx] = extra_mine[:, :, xx] + extra_first[...]
    extra_second_copy.start()
    norm_one_back(both, own, False, (1 - kind) * own, own)

    reads = [pltpu.make_async_copy(grad_all.at[pl.ds(part * slots, slots), :], rows_in.at[part], rsem.at[part]) for part in (0, 1)]
    reads += [pltpu.make_async_copy(got.at[pl.ds(part * slots, slots), :], rows_out.at[part, :, pl.ds(0, CHUNK)], osem.at[part]) for part in (0, 1)]
    for copy in reads:
        copy.start()
    step(7)
    run_third(7)
    for copy in reads:
        copy.wait()
    sums_all = rows_out[:, :, 0:CHUNK].reshape(2 * slots, CHUNK)
    down = lax.dot_general(sums_all, rows_in[...].reshape(2 * slots, width), (((0,), (0,)), ((), ())), precision=highest, preferred_element_type=f32)
    half = CHUNK // 2
    mixed_grad[0:2, 0 : half // 2, :] = jnp.where(core == 0, down[:half], down[half:]).reshape(2, half // 2, width)
    write_down = pltpu.make_async_copy(mixed_grad.at[pl.ds(0, 2), pl.ds(0, half // 2), :], down_out, wsem.at[3])
    write_down.start()
    for chunk in range(2 * pairs - 4, 2 * pairs):
        to_core(chunk).wait_send()
    extra_second_copy.wait()
    extra_mine[:, yy, xx] = extra_mine[:, yy, xx] + extra_second[...]
    start_third(extra_mine, extra_owner, extra_sem)
    for target, low, high in outputs:
        serve(functools.partial(run_last, target, low), low, high)
    wait_third(extra_mine, extra_owner, extra_sem)
    extra_out[...] = extra_owner[0] + extra_owner[1]
    for target, low, high in outputs:
        for chunk in range(2 * low, 2 * high):
            write(chunk, target, low).wait()
    write_down.wait()


def backward(own, grad_rows, first_active, masks, got, grad_all, tokens, saved, weights):
    gain_one, shift_one, w_qkv, w_out, gain_two, shift_two, w_up, b_up, w_down = weights
    slots, width = tokens.shape[1:]
    ff = w_up.shape[2]
    both = 2 * own
    chunks = 2 * ff // CHUNK
    one_t, packed, probs, att_t, mixed, two_t, slope = saved
    split = lambda one: one.reshape(one.shape[0], 8, 2, one.shape[2], one.shape[3])
    anywhere, vmem = pl.BlockSpec(memory_space=pl.ANY), pl.BlockSpec(memory_space=pltpu.VMEM)
    return pl.pallas_call(
        functools.partial(backward_kernel, own),
        out_shape=(
            jax.ShapeDtypeStruct((48, ff), f32), jax.ShapeDtypeStruct((48, width), f32), jax.ShapeDtypeStruct((48, 3 * width), f32),
            jax.ShapeDtypeStruct((48, 128), f32), jax.ShapeDtypeStruct((both, slots, width), f32),
            jax.ShapeDtypeStruct((2, CHUNK // 4, width), f32),
        ),
        in_specs=[vmem] * 5 + [anywhere] * 14,
        out_specs=(anywhere, anywhere, anywhere, vmem, anywhere, anywhere),
        scratch_shapes=[
            pltpu.VMEM((chunks, 2, 2, 2, 48, CHUNK), f32),
            pltpu.VMEM((2, 2, 2, 2, 2, 48, CHUNK), f32),
            pltpu.VMEM((chunks, 2, 2, 2, 48, CHUNK), f32),
            pltpu.VMEM((chunks, 2, 2, 48, CHUNK), f32),
            pltpu.VMEM((chunks, 2, 48, CHUNK), f32),
            pltpu.VMEM((chunks, 2, 48, CHUNK), f32),
            pltpu.VMEM((2, 2, 2, 2, 48, 128), f32),
            pltpu.VMEM((2, 2, 2, 48, 128), f32),
            pltpu.VMEM((2, 2, 2, 48, 128), f32),
            pltpu.VMEM((2, 2, 48, 128), f32),
            pltpu.VMEM((2, 48, 128), f32),
            pltpu.VMEM((2, 48, 128), f32),
            pltpu.VMEM((both, slots, ff), bf16),
            pltpu.VMEM((both, slots, width), f32),
            pltpu.VMEM((both, slots, width), bf16),
            pltpu.VMEM((2, 2, 8, 48, both * slots), bf16),
            pltpu.VMEM((2, width, ff), bf16),
            pltpu.VMEM((16, ff), f32),
            pltpu.VMEM((4, 8, width), f32),
            pltpu.VMEM((2, slots, 3 * width), bf16),
            pltpu.VMEM((2, HEADS // 2, 2 * slots, slots), bf16),
            pltpu.VMEM((2, slots, width), f32),
            pltpu.VMEM((2, slots, width), f32),
            pltpu.VMEM((2 * slots, width), f32),
            pltpu.SemaphoreType.DMA((6, chunks, 2)),
            pltpu.SemaphoreType.DMA((6, 2)),
            pltpu.SemaphoreType.DMA((7,)),
            pltpu.SemaphoreType.DMA((4,)),
            pltpu.SemaphoreType.DMA((2, 2, both)),
            pltpu.SemaphoreType.DMA((2, 2)),
            pltpu.SemaphoreType.DMA((2,)),
            pltpu.SemaphoreType.DMA((2,)),
        ],
        compiler_params=pltpu.CompilerParams(collective_id=1, has_side_effects=True, vmem_limit_bytes=63 << 20),
    )(grad_rows, first_active, masks, gain_one, gain_two, got.reshape(-1, CHUNK), grad_all, tokens, split(one_t), packed, probs, split(att_t), mixed, split(two_t), slope,
      w_qkv, w_out, w_up, w_down)


def tokens_of(patches, visible, modality):
    micro_count, images, _, patch_count, width = patches.shape
    cells = lax.dynamic_index_in_dim(patches, modality, 2, keepdims=False).reshape(micro_count * images, patch_count, width)
    picked = (visible[:, :, None] == jnp.arange(patch_count)[None, None, :]).astype(bf16)
    return jnp.einsum("isp,ipd->isd", picked, cells, preferred_element_type=f32)


def cells_of(grad_tokens, visible, patch_count):
    picked = (visible[:, None, :] == jnp.arange(patch_count)[None, :, None]).astype(f32)
    return jnp.einsum("ips,isd->ipd", picked, grad_tokens, precision=highest)


def on_tuned(patches, visible, valid_mask, weights):
    n = lax.axis_size("dp")
    micro_count, images, _, patch_count, width = patches.shape
    own = micro_count * images
    loss, grad_all, got, grad_rows, active_grad, masks, tokens, *saved = forward(
        n, visible, valid_mask, patches.reshape(own, 2, patch_count, width), weights)
    up, out, qkv, extra, grad_tokens, down = backward(own, grad_rows, active_grad, masks, got, grad_all, tokens, saved, weights)
    cells, gain_one, shift_one, gain_two, shift_two, bias, loss, up, out, qkv, down = finish(
        visible, grad_tokens, patch_count, extra, loss, (up, out, qkv, down))
    patches_grad = cells.reshape(micro_count, images, patch_count, 2, width).transpose(0, 1, 3, 2, 4)
    vector = lambda one: one.reshape(-1)
    return (loss.reshape(()), patches_grad, vector(gain_one), vector(shift_one), qkv, out, vector(gain_two), vector(shift_two), up,
            vector(bias), down.reshape(-1, width))


def on_plain(patches, visible, valid_mask, weights):
    n = lax.axis_size("dp")
    me = lax.axis_index("dp")
    micro_count, images, _, patch_count, width = patches.shape
    own = micro_count * images
    slots = visible.shape[-1]
    ff = weights[6].shape[2]
    seen = visible.reshape(own, slots)
    mask = valid_mask.reshape(own, slots)
    outcomes = []
    for modality in (0, 1):
        params = params_of(weights, modality)
        outcomes.append((params,) + encode_forward(tokens_of(patches, seen, modality), seen, mask, params))
    pooled = jnp.concatenate([pool(active, mixed, mask, params[8]) for params, active, mixed, _ in outcomes])
    counted = jnp.sum(mask.astype(f32), axis=1)[:, None]
    shares = jnp.stack([active / counted for _, active, _, _ in outcomes])
    down_rows = 2 * ff // n
    shares = shares.reshape(2, own, n // 2, down_rows).transpose(0, 2, 1, 3).reshape(n, own * down_rows)
    loss, grad_all = contrast(lax.all_gather(pooled, "dp", axis=0, tiled=True), 2 * own, micro_count)
    got = lax.all_to_all(shares, "dp", 0, 0, tiled=True)
    grad_all = grad_all.reshape(n, 2, own, width)
    grad_down = jnp.einsum(
        "iw,id->wd", got.reshape(n * own, down_rows),
        lax.dynamic_index_in_dim(grad_all, me // (n // 2), 1, keepdims=False).reshape(n * own, width), precision=highest)
    mine = lax.dynamic_index_in_dim(grad_all, me, 0, keepdims=False)
    backs = [encode_backward(mine[m], outcomes[m][3], mask, outcomes[m][0]) for m in (0, 1)]
    patches_grad = jnp.stack([cells_of(back[0], seen, patch_count) for back in backs], 1).reshape(patches.shape)
    joined = jax.tree.map(lambda a, b: jnp.concatenate([a, b]), backs[0][1], backs[1][1])
    shards = tuple(lax.psum_scatter(one, "dp", scatter_dimension=0, tiled=True) for one in joined)
    return (loss[0, 0], patches_grad) + shards + (grad_down,)


def solution(mesh):
    in_specs = (P(None, "dp"), P(None, "dp"), P(None, "dp")) + (P(),) * 9
    out_specs = (P(), P(None, "dp")) + (P("dp"),) * 9

    def on_device(patches, visible, valid_mask, *weights):
        run = on_tuned if lax.axis_size("dp") == 32 else on_plain
        return run(patches, visible, valid_mask, weights)

    return jax.shard_map(on_device, mesh=mesh, in_specs=in_specs, out_specs=out_specs, check_vma=False)
```
